128 devices in a mesh: pipe: 2 (over y_hi), dp: 16 (over x, y_lo, core), tensor: 4 (over z).
Axes of the slice: x: 4, y: 4 (y_hi: 2, y_lo: 2; y = y_hi * 2 + y_lo), z: 4, core: 2. Of those that a mesh axis runs over, the one named last changes fastest.
Arguments:
- tokens: float32 [3, 1280, 1024], P(None, 'dp'), may hold values from -6 to 6
- cotangent: float32 [3, 1280, 1024], P(None, 'dp'), may hold values from -6 to 6
- doc_lengths: int32 [3, 16, 3], P(None, 'dp'), may hold values from 1 to 60, 80 in all within a row
- live_mask: int32 [3, 1280], P(None, 'dp'), may hold values from 0 to 1, as said below
- norm_gains: float32 [2, 2, 1024], P('pipe'), may hold values from 0.5 to 1.5
- norm_biases: float32 [2, 2, 1024], P('pipe'), may hold values from -2 to 2
- query_key_value: bfloat16 [2, 1024, 3, 1024], P('pipe', None, None, 'tensor'), may hold values from -0.1875 to 0.1875
- query_value_bias: float32 [2, 2, 1024], P('pipe', None, 'tensor'), may hold values from -2 to 2
- output_weight: bfloat16 [2, 1024, 1024], P('pipe', 'tensor'), may hold values from -0.75 to 0.75
- output_biases: float32 [2, 2, 1024], P('pipe'), may hold values from -2 to 2
- expand_weight: bfloat16 [2, 1024, 4096], P('pipe', None, 'tensor'), may hold values from -0.1875 to 0.1875
- expand_bias: float32 [2, 4096], P('pipe', 'tensor'), may hold values from -2 to 2
- reduce_weight: bfloat16 [2, 4096, 1024], P('pipe', 'tensor'), may hold values from -0.125 to 0.125
Outputs:
- activations: float32 [2, 3, 1280, 1024], P('pipe', None, 'dp')
- input_grads: float32 [2, 3, 1280, 1024], P('pipe', None, 'dp')
- norm_gains_grad: float32 [2, 2, 1024], P('pipe')
- norm_biases_grad: float32 [2, 2, 1024], P('pipe')
- query_key_value_grad: float32 [2, 1024, 3, 1024], P('pipe', None, None, 'tensor')
- query_value_bias_grad: float32 [2, 2, 1024], P('pipe', None, 'tensor')
- output_weight_grad: float32 [2, 1024, 1024], P('pipe', 'tensor')
- output_biases_grad: float32 [2, 2, 1024], P('pipe')
- expand_weight_grad: float32 [2, 1024, 4096], P('pipe', None, 'tensor')
- expand_bias_grad: float32 [2, 4096], P('pipe', 'tensor')
- reduce_weight_grad: float32 [2, 4096, 1024], P('pipe', 'tensor')
The draws below stay inside these ranges and needn't reach their ends.
Inputs may be any that keep to these rules, and one draw needn't show every extreme that they name: `live_mask`: in each slot of 80 tokens the live tokens form a prefix of at least 26 tokens; in every micro-batch some slot is fully live.
All inputs are finite; a program needn't handle non-finite values.
Results may differ from the reference program's by a relative error of at most 0.035.
Values may be sent and summed in bfloat16 or wider, within the bound.
A program may use at most 192 MiB of HBM per device.

```python
import math
import jax
import jax.numpy as jnp
import numpy as np
from jax import lax

D = 1024
FF = 4096
HD = 64
HEADS = 16
LAYERS = 2
MB = 3
DOCS = 3
ROWS = 80
TOKENS = 1280
N_DP = 16
N_TENSOR = 4


def draw_live_mask(key, part):
    key = jax.random.fold_in(key, 7)
    count_key, full_key = jax.random.split(key)
    slot_count = TOKENS // ROWS
    counts = jax.random.randint(count_key, (MB, slot_count), ROWS // 3, ROWS + 1)
    full_slot = jax.random.randint(full_key, (MB, 1), 0, slot_count)
    counts = jnp.where(jnp.arange(slot_count)[None, :] == full_slot, ROWS, counts)
    places = jnp.arange(TOKENS) % ROWS
    owners = jnp.arange(TOKENS) // ROWS
    return (places[None, :] < counts[:, owners]).astype(jnp.int32)


def block_scale(rng, shape, shards, low, high):
    loudness = 1.0
    for axis_at, blocks in shards:
        heights = jax.random.uniform(jax.random.fold_in(jax.random.fold_in(rng, 6), axis_at), (blocks,), jnp.float32, low / len(shards), high / len(shards))
        loudness = loudness * jnp.repeat(jnp.exp(heights), shape[axis_at] // blocks).reshape((-1,) + (1,) * (len(shape) - 1 - axis_at))
    return loudness


def length_profile(count, total, bound, skew):
    portions = [(1 << 20) // math.isqrt(standing ** skew) + 1 for standing in range(2, count + 1)]
    surplus, given = total - bound - (count - 1), [1] * (count - 1)
    while surplus > 0:
        free = [i for i in range(count - 1) if given[i] < bound]
        pool, left = sum([portions[i] for i in free]), surplus
        for i in free:
            more = min(bound - given[i], max(1, left * portions[i] // pool), surplus)
            given[i] = given[i] + more
            surplus = surplus - more
    return np.array([bound] + given)


def uneven(rng, amount, total, reach, skew):
    if amount == 2:
        one = jax.random.randint(rng, (), max(1, total - reach), min(reach, total - 1) + 1)
        return jnp.stack([one, total - one])
    sizes = jnp.asarray(length_profile(amount, total, reach, skew), jnp.int32)
    twos = (amount - 1) // 2
    giver, taker = sizes[1:1 + 2 * twos:2], sizes[2:2 + 2 * twos:2]
    room = jnp.minimum(giver - 1, reach - taker)
    shifted = jax.random.randint(jax.random.fold_in(rng, 1), (twos,), 0, 1 << 20) % (room + 1)
    sizes = sizes.at[1:1 + 2 * twos:2].set(giver - shifted).at[2:2 + 2 * twos:2].set(taker + shifted)
    return sizes[jax.random.permutation(jax.random.fold_in(rng, 2), amount)]


def gaussian(rng, dims, scale, limit, shards=(), held_as=jnp.bfloat16):
    values = scale * jax.random.normal(rng, dims, jnp.float32)
    if shards:
        values = values * block_scale(rng, dims, shards, -0.22, 0.18)
    return jnp.clip(values, -limit, limit).astype(held_as)


def setup_inputs(seed: int = 0) -> dict:
    key_of = jax.random.split(jax.random.key(seed), 14)
    return {
        "tokens": gaussian(key_of[0], (MB, TOKENS, D), 1.0, 6.0, ((1, 16),), jnp.float32),
        "cotangent": gaussian(key_of[1], (MB, TOKENS, D), 1.0, 6.0, ((1, 16),), jnp.float32),
        "doc_lengths": jax.vmap(lambda own: uneven(own, DOCS, ROWS, 3 * ROWS // 4, 2))(jax.random.split(key_of[2], MB * N_DP)).reshape((MB, N_DP, DOCS)).astype(jnp.int32),
        "live_mask": draw_live_mask(jax.random.fold_in(key_of[13], 71), 0),
        "norm_gains": jnp.clip(1.0 + 0.1 * jax.random.normal(key_of[4], (LAYERS, 2, D), jnp.float32), 0.5, 1.5),
        "norm_biases": gaussian(key_of[5], (LAYERS, 2, D), 0.3, 2.0, ((0, 2),), jnp.float32),
        "query_key_value": gaussian(key_of[6], (LAYERS, D, 3, D), D ** -0.5, 0.1875, ((0, 2), (3, 4))),
        "query_value_bias": gaussian(key_of[7], (LAYERS, 2, D), 0.3, 2.0, ((0, 2), (2, 4)), jnp.float32),
        "output_weight": gaussian(key_of[8], (LAYERS, D, D), (D // 16) ** -0.5, 0.75, ((0, 2), (1, 4))),
        "output_biases": gaussian(key_of[9], (LAYERS, 2, D), 0.3, 2.0, ((0, 2),), jnp.float32),
        "expand_weight": gaussian(key_of[10], (LAYERS, D, FF), D ** -0.5, 0.1875, ((0, 2), (2, 4))),
        "expand_bias": gaussian(key_of[11], (LAYERS, FF), 0.3, 2.0, ((0, 2), (1, 4)), jnp.float32),
        "reduce_weight": gaussian(key_of[12], (LAYERS, FF, D), (FF // 2) ** -0.5, 0.125, ((0, 2), (1, 4))),
    }


@jax.custom_vjp
def low(v):
    return lax.optimization_barrier(v.astype(jnp.bfloat16)).astype(jnp.float32)

@jax.custom_vjp
def low_back(v):
    return v

def low_keep(v):
    return (low(v), None)

def low_pass(kept, grad):
    return (grad,)

def back_keep(v):
    return (v, None)

def back_low(kept, grad):
    return (low(grad),)
low.defvjp(low_keep, low_pass)
low_back.defvjp(back_keep, back_low)
HIGHEST_PRECISION = lax.Precision.HIGHEST

def layer_norm(inputs, gain, shift):
    center = inputs - lax.optimization_barrier(jnp.mean(inputs, -1, keepdims=True))
    spread = lax.optimization_barrier(jnp.mean(center * center, -1, keepdims=True))
    return center * lax.rsqrt(spread + 1e-05) * gain + shift

def slot_masks(doc_lengths, live_mask):
    slot_count = MB * N_DP
    lengths = doc_lengths.reshape(slot_count, DOCS).astype(jnp.int32)
    live = live_mask.reshape(slot_count, ROWS)
    ends = jnp.cumsum(lengths, -1).astype(jnp.int32)
    places = jnp.arange(ROWS, dtype=jnp.int32)
    segment = lax.optimization_barrier(jnp.sum((places[None, :, None] >= ends[:, None, :]).astype(jnp.int32), -1))
    same = segment[:, :, None] == segment[:, None, :]
    causal = places[:, None] >= places[None, :]
    visible = (live[:, None, :] == 1) | (places[:, None] == places[None, :])[None]
    return same & causal[None] & visible

def group_sum(left, right, width):
    parts = left.reshape(left.shape[0], left.shape[1], N_TENSOR, width // N_TENSOR)
    blocks = right.reshape(N_TENSOR, width // N_TENSOR, right.shape[1])
    partial_terms = jnp.einsum('srgk,gkd->gsrd', parts, blocks, precision=HIGHEST_PRECISION)
    return lax.optimization_barrier(jnp.sum(low(partial_terms), 0))

def layer(inputs, allowed, params):
    gains, shifts, qkv_weight, qv_bias, out_weight, out_bias, up_weight, up_bias, down_weight = params
    slots, row_count = (inputs.shape[0], inputs.shape[1])
    scale = 1.0 / math.sqrt(HD)
    normed_one = low(layer_norm(inputs, gains[0], shifts[0]))
    projected = jnp.einsum('srd,dcn->srcn', normed_one, qkv_weight, precision=HIGHEST_PRECISION)
    queries = low(low_back(projected[:, :, 0] + qv_bias[0])).reshape(slots, row_count, HEADS, HD)
    key_rows = low(low_back(projected[:, :, 1])).reshape(slots, row_count, HEADS, HD)
    value_rows = low(low_back(projected[:, :, 2] + qv_bias[1])).reshape(slots, row_count, HEADS, HD)
    raw_scores = jnp.einsum('sqhe,skhe->shqk', queries, key_rows, precision=HIGHEST_PRECISION) * scale
    scores = low_back(jnp.where(allowed[:, None], raw_scores, -1000000000.0))
    top = lax.optimization_barrier(jnp.max(scores, -1, keepdims=True))
    expo = jnp.exp(scores - top)
    probability = expo / lax.optimization_barrier(jnp.sum(expo, -1, keepdims=True))
    attended = jnp.einsum('shqk,skhe->sqhe', low(probability), value_rows, precision=HIGHEST_PRECISION)
    attended = low(low_back(attended.reshape(slots, row_count, D)))
    middle = inputs + low_back(group_sum(attended, out_weight, D)) + out_bias[0]
    normed_two = low(layer_norm(middle, gains[1], shifts[1]))
    hidden = low_back(jnp.einsum('srd,df->srf', normed_two, up_weight, precision=HIGHEST_PRECISION) + up_bias)
    activated = low(jax.nn.gelu(hidden, approximate=True))
    return middle + low_back(group_sum(activated, down_weight, FF)) + out_bias[1]

def reference(tokens, cotangent, doc_lengths, live_mask, norm_gains, norm_biases, query_key_value, query_value_bias, output_weight, output_biases, expand_weight, expand_bias, reduce_weight):
    slot_count = MB * N_DP
    allowed = slot_masks(doc_lengths, live_mask)
    params = tuple((array.astype(jnp.float32) for array in (norm_gains, norm_biases, query_key_value, query_value_bias, output_weight, output_biases, expand_weight, expand_bias, reduce_weight)))
    start = tokens.astype(jnp.float32).reshape(slot_count, ROWS, D)
    probe = jnp.zeros_like(start)

    def forward(start, probe, params):
        first_out = layer(start, allowed, tuple((array[0] for array in params)))
        second_out = layer(first_out + probe, allowed, tuple((array[1] for array in params)))
        return (first_out, second_out)
    (first_out, second_out), pullback = jax.vjp(forward, start, probe, params)
    output_cotangent = (cotangent * live_mask[..., None].astype(cotangent.dtype)).reshape(slot_count, ROWS, D)
    start_grad, probe_grad, param_grads = pullback((jnp.zeros_like(first_out), output_cotangent))
    gains_grad, shifts_grad, qkv_grad, qv_grad, out_grad, out_bias_grad, up_grad, up_bias_grad, down_grad = param_grads
    shape = (LAYERS, MB, N_DP * ROWS, D)
    activations = jnp.stack([first_out, second_out]).reshape(shape)
    input_grads = jnp.stack([start_grad, probe_grad]).reshape(shape)
    return (activations, input_grads, gains_grad, shifts_grad, qkv_grad, qv_grad, out_grad, out_bias_grad, up_grad, up_bias_grad, down_grad)
```

```python
import functools
import math

import jax
import jax.numpy as jnp
from jax import lax
from jax.experimental import pallas as pl
from jax.experimental.pallas import tpu as pltpu
from jax.sharding import PartitionSpec as P

MESH = pl.DeviceIdType.MESH
F32 = jnp.float32
BF16 = jnp.bfloat16
D = 1024
ROWS = 80
SLOTS = 3
USED = ROWS * SLOTS
PAD = 256
TEN = 4
CH = PAD // TEN
HEADS = 4
HD = 64
W = 256
BUCKETS = ((1024, 1024, 256, 256), (1024, 1024, 256, 256), (256, 1024, 128, 0), (1024, 768, 256, 256))
A1, Y1, A2, Y2, OUT, DOUT, DA2, DY1, DA1, DX, SMALL = range(11)


def dot_nn(a, b):
    return lax.dot_general(a, b, (((1,), (0,)), ((), ())), preferred_element_type=F32)


def dot_nt(a, b):
    return lax.dot_general(a, b, (((1,), (1,)), ((), ())), preferred_element_type=F32)


def dot_tn(a, b):
    return lax.dot_general(a, b, (((0,), (0,)), ((), ())), preferred_element_type=F32)


def tile(j, size=W):
    return pl.ds(pl.multiple_of(j * size, size), size)


def normed(u):
    center = u - jnp.mean(u, -1, keepdims=True)
    inverse = lax.rsqrt(jnp.mean(center * center, -1, keepdims=True) + 1e-05)
    return center * inverse, inverse


def norm_back(grad, u, gain):
    unit, inverse = normed(u)
    scaled = grad * gain
    along = jnp.mean(scaled * unit, -1, keepdims=True)
    grad_u = inverse * (scaled - jnp.mean(scaled, -1, keepdims=True) - unit * along)
    return grad_u, jnp.sum(grad * unit, 0, keepdims=True), jnp.sum(grad, 0, keepdims=True)


def kernel(
    reduce_dp,
    tok_hbm, cot_hbm, docs, live, gains, shifts, wqkv_hbm, qvb, wo_hbm, obias, wup_hbm, upb, wdn_hbm,
    act_out, dx_out, gdn_out, gup_out, go_out, gqkv_out, small_out,
    tok, cot, wqkv, wo, wup, wdn, mask, xc, a1, qkv, prob, att, y1s, y1r, x2c, a2, slope, g,
    y2s, y2r, actg, doc, dy2, dg, dh, da2s, da2r, dx2c, dy1, dqkv, da1s, da1r, dxg,
    pipe_f, pipe_b, pipe_fs, pipe_bs, sm, smz, smc, smy, smx, acc0, acc1, acc2,
    wg0, wg1, wg2, wg3, rc0, rc1, rc2, rc3, p10, p11, p12, p13, q10, q11, q13,
    p20, p21, p22, p23, q20, q21, q23,
    load_sem, out_sem, tp_s, tp_r, pp_s, pp_r, dp_s, dp_r, dp_l, sd_s, sd_r,
):
    wgs, rcs = (wg0, wg1, wg2, wg3), (rc0, rc1, rc2, rc3)
    p1s, q1s = (p10, p11, p12, p13), (q10, q11, None, q13)
    p2s, q2s = (p20, p21, p22, p23), (q20, q21, None, q23)
    gouts = (gdn_out, gup_out, go_out, gqkv_out)
    pipe = lax.axis_index("pipe")
    dp = lax.axis_index("dp")
    z = lax.axis_index("tensor")
    first = pipe == 0
    second = pipe == 1
    gx, gy, gc = dp // 4, (dp // 2) % 2, dp % 2
    core_peer = gx * 4 + gy * 2 + (1 - gc)
    y_peer = gx * 4 + (1 - gy) * 2 + gc
    x_peers = [((gx + t) % 4) * 4 + gy * 2 + gc for t in (1, 2, 3)]
    mine = tile(z, CH)

    def load(k, src, dst):
        return pltpu.make_async_copy(src, dst, load_sem.at[k])

    loads = {
        "tok": load(0, tok_hbm, tok.at[pl.ds(0, USED)]),
        "cot": load(1, cot_hbm, cot.at[pl.ds(0, USED)]),
        "qkv": load(2, wqkv_hbm, wqkv),
        "o": load(3, wo_hbm, wo),
        "up": load(4, wup_hbm, wup),
        "dn": load(5, wdn_hbm, wdn),
    }
    for name in ("tok", "cot", "qkv", "o", "up", "dn"):
        loads[name].start()

    barrier = pltpu.get_barrier_semaphore()
    partners = [{"tensor": (z + t) % 4} for t in (1, 2, 3)] + [{"pipe": 1 - pipe}]
    if reduce_dp:
        partners += [{"dp": core_peer}, {"dp": y_peer}] + [{"dp": p} for p in x_peers]
    for partner in partners:
        pl.semaphore_signal(barrier, inc=1, device_id=partner, device_id_type=MESH)

    def places(shape, axis):
        at = lax.broadcasted_iota(jnp.int32, shape, axis)
        slot = (at >= ROWS).astype(jnp.int32) + (at >= 2 * ROWS).astype(jnp.int32)
        slot = slot + (at >= 3 * ROWS).astype(jnp.int32)
        spot = at - ROWS * slot
        segment = 4 * slot
        alive = jnp.zeros(shape, F32)
        for s in range(SLOTS):
            end = jnp.int32(0)
            for k in range(3):
                end = end + docs[s, k]
                segment = segment + jnp.where((slot == s) & (spot >= end), 1, 0)
            alive = jnp.where((slot == s) & (spot.astype(F32) < counts[s : s + 1, :]), 1.0, alive)
        return at, segment, alive

    counts = jnp.sum(live[...].astype(F32), 1, keepdims=True)
    row_at, row_segment, row_live = places((PAD, 1), 0)
    col_at, col_segment, col_live = places((1, PAD), 1)
    seen = (row_segment == col_segment) & (col_at <= row_at)
    seen = seen & ((col_live + jnp.where(row_at == col_at, 1.0, 0.0)) > 0.5)
    mask[...] = jnp.where(seen, 1.0, 0.0)
    sm[...] = jnp.zeros_like(sm)
    head_of = lax.broadcasted_iota(jnp.int32, (1, W), 1) // HD

    pl.semaphore_wait(barrier, len(partners))

    def tp_copy(k, t, src, dst):
        return pltpu.make_async_remote_copy(
            src_ref=src,
            dst_ref=dst,
            send_sem=tp_s.at[k, t - 1],
            recv_sem=tp_r.at[k, t - 1],
            device_id={"tensor": (z + t) % 4},
            device_id_type=MESH,
        )

    def scatter(k, src, dst):
        return [tp_copy(k, t, src.at[tile((z + t) % 4, CH)], dst.at[t - 1]) for t in (2, 1, 3)]

    def gather(k, buf):
        return [tp_copy(k, t, buf.at[mine], buf.at[mine]) for t in (2, 1, 3)]

    def start(copies):
        for copy in copies:
            copy.start()

    def arrive(copies):
        for copy in copies:
            copy.wait_recv()

    def sent(copies):
        for copy in copies:
            copy.wait_send()

    ex = {
        A1: gather(A1, a1),
        Y1: scatter(Y1, y1s, y1r),
        A2: gather(A2, a2),
        Y2: scatter(Y2, y2s, y2r),
        OUT: gather(OUT, actg),
        DOUT: gather(DOUT, dy2),
        DA2: scatter(DA2, da2s, da2r),
        DY1: gather(DY1, dy1),
        DA1: scatter(DA1, da1s, da1r),
        DX: gather(DX, dxg),
        SMALL: [tp_copy(SMALL, t, smz.at[z], smz.at[z]) for t in (2, 1, 3)],
    }
    forth = pltpu.make_async_remote_copy(
        src_ref=pipe_fs, dst_ref=pipe_f, send_sem=pp_s.at[0], recv_sem=pp_r.at[0],
        device_id={"pipe": 1 - pipe}, device_id_type=MESH,
    )
    back = pltpu.make_async_remote_copy(
        src_ref=pipe_bs, dst_ref=pipe_b, send_sem=pp_s.at[1], recv_sem=pp_r.at[1],
        device_id={"pipe": 1 - pipe}, device_id_type=MESH,
    )

    def summed(src, dst):
        total = src[mine].astype(F32)
        for t in range(3):
            total = total + dst[t].astype(F32)
        return total

    def dp_copy(b, k, src, dst, peer):
        return pltpu.make_async_remote_copy(
            src_ref=src, dst_ref=dst, send_sem=dp_s.at[b, k], recv_sem=dp_r.at[b, k],
            device_id={"dp": peer}, device_id_type=MESH,
        )

    def rows(at, size):
        return pl.ds(pl.multiple_of(at, 16), size)

    def add_into(dst, at, size, terms):
        step = min(size, 64)

        @pl.loop(0, size // step)
        def _(i):
            off = pl.multiple_of(i * step, 16)
            total = dst[rows(at + off, step), :].astype(F32)
            for term in terms:
                total = total + term(off, step).astype(F32)
            dst[rows(at + off, step), :] = total.astype(BF16)

    def bucket(b):
        size, _, p, q = BUCKETS[b]
        half = size // 2
        wg, rc, out = wgs[b], rcs[b], gouts[b]
        p1, q1, p2, q2 = p1s[b], q1s[b], p2s[b], q2s[b]
        base = gc * half
        p8, p4, q8, q2n = p // 8, p // 4, q // 8, q // 2
        c = {}
        c["core"] = [dp_copy(b, 0, wg.at[rows((1 - gc) * half, half)], rc, core_peer)]
        xs = [(gx + t) % 4 for t in (1, 2, 3)]
        order = (1, 0, 2)
        c["p1"] = [
            dp_copy(b, 1 + i, rc.at[rows(xs[i] * p4, p4)], p1.at[i], x_peers[i]) for i in order
        ]
        p_fin = gx * p4 + gy * p8
        c["p2"] = [dp_copy(b, 5, rc.at[rows(gx * p4 + (1 - gy) * p8, p8)], p2, y_peer)]
        c["p3"] = [dp_copy(b, 9, rc.at[rows(p_fin, p8)], out.at[rows(base + p_fin, p8)], y_peer)]
        p_part = out.at[rows(base + gx * p4, p4)]
        c["p4"] = [dp_copy(b, 13 + i, p_part, p_part, x_peers[i]) for i in order]
        half_out = out.at[rows(base, half)]
        c["all"] = [dp_copy(b, 17, half_out, half_out, core_peer)]
        keep = [
            pltpu.make_async_copy(
                rc.at[rows(p_fin, p8)], out.at[rows(base + p_fin, p8)], dp_l.at[b, 0]
            )
        ]
        if q:
            q_fin = p + gy * q2n + gx * q8
            c["q1"] = [dp_copy(b, 4, rc.at[rows(p + (1 - gy) * q2n, q2n)], q1, y_peer)]
            c["q2"] = [
                dp_copy(b, 6 + i, rc.at[rows(p + gy * q2n + xs[i] * q8, q8)], q2.at[i], x_peers[i])
                for i in order
            ]
            c["q3"] = [
                dp_copy(b, 10 + i, rc.at[rows(q_fin, q8)], out.at[rows(base + q_fin, q8)], x_peers[i])
                for i in order
            ]
            q_part = out.at[rows(base + p + gy * q2n, q2n)]
            c["q4"] = [dp_copy(b, 16, q_part, q_part, y_peer)]
            keep.append(
                pltpu.make_async_copy(
                    rc.at[rows(q_fin, q8)], out.at[rows(base + q_fin, q8)], dp_l.at[b, 1]
                )
            )

        def step0():
            start(c["core"])

        def step1():
            arrive(c["core"])
            add_into(rc, 0, half, [lambda o, n: wg[rows(base + o, n), :]])
            start(c["p1"])
            if q:
                start(c["q1"])

        def step2():
            if q:
                arrive(c["q1"])
                add_into(rc, p + gy * q2n, q2n, [lambda o, n: q1[rows(o, n), :]])
                start(c["q2"])
            arrive(c["p1"])
            add_into(rc, gx * p4, p4, [
                (lambda o, n, i=i: p1[i, rows(o, n), :]) for i in range(3)
            ])
            start(c["p2"])

        def step3():
            arrive(c["p2"])
            add_into(rc, p_fin, p8, [lambda o, n: p2[rows(o, n), :]])
            start(c["p3"])
            keep[0].start()
            if q:
                arrive(c["q2"])
                add_into(rc, q_fin, q8, [
                    (lambda o, n, i=i: q2[i, rows(o, n), :]) for i in range(3)
                ])
                start(c["q3"])
                keep[1].start()

        def step4():
            keep[0].wait()
            arrive(c["p3"])
            start(c["p4"])
            if q:
                keep[1].wait()
                arrive(c["q3"])
                start(c["q4"])

        def step5():
            arrive(c["p4"])
            if q:
                arrive(c["q4"])
            start(c["all"])

        def step6():
            arrive(c["all"])
            for group in c.values():
                sent(group)

        return [step0, step1, step2, step3, step4, step5, step6]

    def sd_copy(k, src, dst, peer):
        return pltpu.make_async_remote_copy(
            src_ref=src, dst_ref=dst, send_sem=sd_s.at[k], recv_sem=sd_r.at[k],
            device_id={"dp": peer}, device_id_type=MESH,
        )

    @pl.when(first)
    def _():
        loads["tok"].wait()
        tok[pl.ds(USED, PAD - USED), :] = jnp.zeros((PAD - USED, D), F32)

        @pl.loop(0, TEN)
        def _(i):
            unit, _ = normed(tok[tile(i, CH), :])
            a1[tile(i, CH), :] = (unit * gains[0:1, :] + shifts[0:1, :]).astype(BF16)

        xc[...] = tok[mine, :]
        loads["cot"].wait()
        loads["dn"].wait()

    def output_grads():
        @pl.loop(0, D // W)
        def _(j):
            dg[:, tile(j)] = dot_nt(dy2[...], wdn[tile(j), :])

    @pl.when(second)
    def _():
        loads["cot"].wait()
        cot[pl.ds(USED, PAD - USED), :] = jnp.zeros((PAD - USED, D), F32)
        masked = cot[...] * row_live
        cot[...] = masked
        dy2[...] = masked.astype(BF16)
        sm[5:6, :] = jnp.sum(masked, 0, keepdims=True)
        doc[...] = cot[mine, :]
        loads["dn"].wait()
        output_grads()
        loads["tok"].wait()
        forth.wait_recv()
        inputs = pipe_f[...].astype(F32)
        xc[...] = inputs
        unit, _ = normed(inputs)
        a1[mine, :] = (unit * gains[0:1, :] + shifts[0:1, :]).astype(BF16)
        start(ex[A1])
        arrive(ex[A1])

    loads["qkv"].wait()
    for j in range(3):
        part = dot_nn(a1[...], wqkv[:, j * W : (j + 1) * W])
        if j != 1:
            part = part + qvb[j // 2 : j // 2 + 1, :]
        qkv[:, j * W : (j + 1) * W] = part.astype(BF16)

    def head_rows(values, h):
        return (values.astype(F32) * jnp.where(head_of == h, 1.0, 0.0)).astype(BF16)

    acc0[...] = jnp.zeros_like(acc0)

    @pl.loop(0, HEADS)
    def _(h):
        scores = dot_nt(head_rows(qkv[:, 0:W], h), qkv[:, W : 2 * W]) * (1.0 / math.sqrt(HD))
        scores = jnp.where(mask[...] > 0.5, scores, -1000000000.0)
        expo = jnp.exp(scores - jnp.max(scores, -1, keepdims=True))
        p = expo / jnp.sum(expo, -1, keepdims=True)
        prob[h] = p
        acc0[...] += dot_nn(p.astype(BF16), head_rows(qkv[:, 2 * W : 3 * W], h))

    att[...] = acc0[...].astype(BF16)
    loads["o"].wait()

    @pl.loop(0, D // W)
    def _(j):
        y1s[:, tile(j)] = dot_nn(att[...], wo[:, tile(j)]).astype(BF16)

    start(ex[Y1])
    arrive(ex[Y1])
    middle = xc[...] + summed(y1s, y1r) + obias[0:1, :]
    x2c[...] = middle
    unit, _ = normed(middle)
    a2[mine, :] = (unit * gains[1:2, :] + shifts[1:2, :]).astype(BF16)
    start(ex[A2])
    loads["up"].wait()
    arrive(ex[A2])

    @pl.loop(0, D // W)
    def _(j):
        hidden = dot_nn(a2[...], wup[:, tile(j)]) + upb[:, tile(j)]
        square = hidden * hidden
        root = math.sqrt(2.0 / math.pi)
        bent = jnp.tanh(root * hidden * (1.0 + 0.044715 * square))
        lifted = 0.5 * (1.0 + bent)
        g[:, tile(j)] = (hidden * lifted).astype(BF16)
        inner = root * (1.0 + 3.0 * 0.044715 * square)
        slope[:, tile(j)] = lifted + 0.5 * hidden * (1.0 - bent * bent) * inner

    def down():
        @pl.loop(0, D // W)
        def _(j):
            y2s[:, tile(j)] = dot_nn(g[...], wdn[:, tile(j)]).astype(BF16)

        start(ex[Y2])

    def layer_output():
        arrive(ex[Y2])
        result = (x2c[...] + summed(y2s, y2r) + obias[1:2, :]).astype(BF16)
        pipe_fs[...] = result
        actg[mine, :] = result

    act_copy = pltpu.make_async_copy(actg.at[pl.ds(0, USED)], act_out, out_sem.at[0])

    @pl.when(first)
    def _():
        down()
        layer_output()
        forth.start()
        start(ex[OUT])
        back.wait_recv()
        dy2[mine, :] = pipe_b[...]
        doc[...] = pipe_b[...].astype(F32)
        start(ex[DOUT])
        arrive(ex[DOUT])
        output_grads()

    @pl.loop(0, D // W)
    def _(j):
        grad = (dg[:, tile(j)] * slope[:, tile(j)]).astype(BF16)
        dh[:, tile(j)] = grad
        sm[7:8, tile(j)] = jnp.sum(grad.astype(F32), 0, keepdims=True)

    @pl.loop(0, D // W)
    def _(j):
        da2s[:, tile(j)] = dot_nt(dh[...], wup[tile(j), :]).astype(BF16)

    start(ex[DA2])

    @pl.when(first)
    def _():
        sm[5:6, :] = jnp.sum(dy2[...].astype(F32), 0, keepdims=True)

    @pl.loop(0, D // W)
    def _(j):
        wgs[0][tile(j), :] = dot_tn(g[:, tile(j)], dy2[...]).astype(BF16)

    @pl.loop(0, D // W)
    def _(j):
        wgs[1][tile(j), :] = dot_tn(a2[:, tile(j)], dh[...]).astype(BF16)

    arrive(ex[DA2])
    grad_u, gain_grad, shift_grad = norm_back(summed(da2s, da2r), x2c[...], gains[1:2, :])
    grad_middle = doc[...] + grad_u
    dx2c[...] = grad_middle
    sm[1:2, :] = gain_grad
    sm[3:4, :] = shift_grad
    sm[4:5, :] = jnp.sum(grad_middle, 0, keepdims=True)
    dy1[mine, :] = grad_middle.astype(BF16)
    start(ex[DY1])
    arrive(ex[DY1])

    att_grad = dot_nt(dy1[...], wo[...]).astype(BF16)
    dqkv[:, 2 * W : 3 * W] = att_grad
    acc0[...] = jnp.zeros_like(acc0)
    acc1[...] = jnp.zeros_like(acc1)
    acc2[...] = jnp.zeros_like(acc2)

    @pl.loop(0, HEADS)
    def _(h):
        p = prob[h]
        own = head_rows(dqkv[:, 2 * W : 3 * W], h)
        grad_p = dot_nt(own, qkv[:, 2 * W : 3 * W])
        acc2[...] += dot_tn(p.astype(BF16), own)
        grad_s = p * (grad_p - jnp.sum(grad_p * p, -1, keepdims=True))
        grad_s = grad_s.astype(BF16)
        acc0[...] += dot_nn(grad_s, head_rows(qkv[:, W : 2 * W], h))
        acc1[...] += dot_tn(grad_s, head_rows(qkv[:, 0:W], h))

    scale = 1.0 / math.sqrt(HD)
    for j, (acc, factor) in enumerate(((acc0, scale), (acc1, scale), (acc2, 1.0))):
        low = (acc[...] * factor).astype(BF16)
        dqkv[:, j * W : (j + 1) * W] = low
        if j != 1:
            at = (j // 2) * W
            sm[6:7, at : at + W] = jnp.sum(low.astype(F32), 0, keepdims=True)

    @pl.loop(0, D // W)
    def _(j):
        da1s[:, tile(j)] = dot_nt(dqkv[...], wqkv[tile(j), :]).astype(BF16)

    start(ex[DA1])
    wgs[2][...] = dot_tn(att[...], dy1[...]).astype(BF16)

    @pl.loop(0, D // W)
    def _(j):
        wgs[3][tile(j), :] = dot_tn(a1[:, tile(j)], dqkv[...]).astype(BF16)

    arrive(ex[DA1])
    grad_u, gain_grad, shift_grad = norm_back(summed(da1s, da1r), xc[...], gains[0:1, :])
    sm[0:1, :] = gain_grad
    sm[2:3, :] = shift_grad
    low = (dx2c[...] + grad_u).astype(BF16)
    pipe_bs[...] = low
    dxg[mine, :] = low

    @pl.when(second)
    def _():
        back.start()

    start(ex[DX])
    smz[z] = sm[...]
    start(ex[SMALL])

    @pl.when(second)
    def _():
        down()
        layer_output()
        start(ex[OUT])

    if reduce_dp:
        steps = [bucket(b) for b in range(4)]
        for s in range(7):
            for b in range(4):
                steps[b][s]()

    arrive(ex[OUT])
    act_copy.start()
    arrive(ex[DX])
    dx_copy = pltpu.make_async_copy(dxg.at[pl.ds(0, USED)], dx_out, out_sem.at[1])
    dx_copy.start()

    arrive(ex[SMALL])
    whole = smz[0] + smz[1] + smz[2] + smz[3]
    own_rows = lax.broadcasted_iota(jnp.int32, (8, D), 0) >= 5
    whole = jnp.where(own_rows, sm[...], whole)
    if reduce_dp:
        smc[gc] = whole
        core_copy = sd_copy(0, smc.at[gc], smc.at[gc], core_peer)
        core_copy.start()
        core_copy.wait()
        smy[gy] = smc[0] + smc[1]
        y_copy = sd_copy(1, smy.at[gy], smy.at[gy], y_peer)
        y_copy.start()
        y_copy.wait()
        smx[gx] = smy[0] + smy[1]
        x_copies = [sd_copy(2 + i, smx.at[gx], smx.at[gx], x_peers[i]) for i in range(3)]
        start(x_copies)
        for copy in x_copies:
            copy.wait()
        whole = smx[0] + smx[1] + smx[2] + smx[3]
    small_out[...] = whole

    act_copy.wait()
    dx_copy.wait()
    for k in (Y1, A2, Y2, OUT, DA2, DY1, DA1, DX, SMALL):
        sent(ex[k])

    @pl.when(first)
    def _():
        forth.wait_send()
        sent(ex[DOUT])

    @pl.when(second)
    def _():
        back.wait_send()
        sent(ex[A1])

    if not reduce_dp:
        copies = [
            pltpu.make_async_copy(wg, out, dp_l.at[b, 0])
            for b, (wg, out) in enumerate(zip(wgs, gouts))
        ]
        start(copies)
        for copy in copies:
            copy.wait()


def call(reduce_dp, *operands):
    hbm = pl.BlockSpec(memory_space=pl.ANY)
    vmem = pl.BlockSpec(memory_space=pltpu.VMEM)
    smem = pl.BlockSpec(memory_space=pltpu.SMEM)

    def low(*shape):
        return pltpu.VMEM(shape, BF16)

    def wide(*shape):
        return pltpu.VMEM(shape, F32)

    scratch = [
        wide(PAD, D), wide(PAD, D), low(D, 768), low(256, D), low(D, D), low(D, D),
        wide(PAD, PAD), wide(CH, D), low(PAD, D), low(PAD, 768), wide(HEADS, PAD, PAD), low(PAD, W),
        low(PAD, D), low(3, CH, D), wide(CH, D), low(PAD, D), wide(PAD, D), low(PAD, D),
        low(PAD, D), low(3, CH, D), low(PAD, D), wide(CH, D), low(PAD, D), wide(PAD, D), low(PAD, D),
        low(PAD, D), low(3, CH, D), wide(CH, D), low(PAD, D), low(PAD, 768), low(PAD, D),
        low(3, CH, D), low(PAD, D),
        low(CH, D), low(CH, D), low(CH, D), low(CH, D),
        wide(8, D), wide(4, 8, D), wide(2, 8, D), wide(2, 8, D), wide(4, 8, D),
        wide(PAD, W), wide(PAD, W), wide(PAD, W),
    ]
    scratch += [low(size, width) for size, width, p, q in BUCKETS]
    scratch += [low(size // 2, width) for size, width, p, q in BUCKETS]
    scratch += [low(3, p // 4, width) for size, width, p, q in BUCKETS]
    scratch += [low(q // 2, width) for size, width, p, q in BUCKETS if q]
    scratch += [low(p // 8, width) for size, width, p, q in BUCKETS]
    scratch += [low(3, q // 8, width) for size, width, p, q in BUCKETS if q]
    dma = pltpu.SemaphoreType.DMA
    scratch += [
        dma((6,)), dma((2,)), dma((11, 3)), dma((11, 3)), dma((2,)), dma((2,)),
        dma((4, 18)), dma((4, 18)), dma((4, 2)), dma((5,)), dma((5,)),
    ]
    return pl.pallas_call(
        functools.partial(kernel, reduce_dp),
        out_shape=[
            jax.ShapeDtypeStruct((USED, D), BF16),
            jax.ShapeDtypeStruct((USED, D), BF16),
            *[jax.ShapeDtypeStruct((size, width), BF16) for size, width, _, _ in BUCKETS],
            jax.ShapeDtypeStruct((8, D), F32),
        ],
        in_specs=[hbm, hbm, smem, vmem, vmem, vmem, hbm, vmem, hbm, vmem, hbm, vmem, hbm],
        out_specs=[hbm] * 6 + [vmem],
        scratch_shapes=scratch,
        compiler_params=pltpu.CompilerParams(
            collective_id=0, has_side_effects=True, vmem_limit_bytes=60 * 1024 * 1024
        ),
        name="layers",
    )(*operands)


def local(
    tokens,
    cotangent,
    doc_lengths,
    live_mask,
    norm_gains,
    norm_biases,
    query_key_value,
    query_value_bias,
    output_weight,
    output_biases,
    expand_weight,
    expand_bias,
    reduce_weight,
):
    reduce_dp = lax.axis_size("dp") == 16
    act, dx, gdn, gup, go, gqkv, small = call(
        reduce_dp,
        tokens.reshape(USED, D),
        cotangent.reshape(USED, D),
        doc_lengths.reshape(SLOTS, 3),
        live_mask,
        norm_gains[0],
        norm_biases[0],
        query_key_value[0].reshape(D, 768),
        query_value_bias[0],
        output_weight[0],
        output_biases[0],
        expand_weight[0],
        expand_bias,
        reduce_weight[0],
    )
    return (
        act.astype(F32).reshape(1, SLOTS, ROWS, D),
        dx.astype(F32).reshape(1, SLOTS, ROWS, D),
        small[None, 0:2],
        small[None, 2:4],
        gqkv.astype(F32).reshape(1, D, 3, 256),
        small[6, 0:512].reshape(1, 2, 256),
        go.astype(F32)[None],
        small[None, 4:6],
        gup.astype(F32)[None],
        small[7:8],
        gdn.astype(F32)[None],
    )


def solution(mesh):
    in_specs = (
        P(None, "dp", None),
        P(None, "dp", None),
        P(None, "dp", None),
        P(None, "dp"),
        P("pipe", None, None),
        P("pipe", None, None),
        P("pipe", None, None, "tensor"),
        P("pipe", None, "tensor"),
        P("pipe", "tensor", None),
        P("pipe", None, None),
        P("pipe", None, "tensor"),
        P("pipe", "tensor"),
        P("pipe", "tensor", None),
    )
    out_specs = (
        P("pipe", None, "dp", None),
        P("pipe", None, "dp", None),
        P("pipe", None, None),
        P("pipe", None, None),
        P("pipe", None, None, "tensor"),
        P("pipe", None, "tensor"),
        P("pipe", "tensor", None),
        P("pipe", None, None),
        P("pipe", None, "tensor"),
        P("pipe", "tensor"),
        P("pipe", "tensor", None),
    )
    return jax.shard_map(local, mesh=mesh, in_specs=in_specs, out_specs=out_specs, check_vma=False)
```

```python
import functools
import math

import jax
import jax.numpy as jnp
from jax import lax
from jax.experimental import pallas as pl
from jax.experimental.pallas import tpu as pltpu
from jax.sharding import PartitionSpec as P

MESH = pl.DeviceIdType.MESH
F32 = jnp.float32
BF16 = jnp.bfloat16
D = 1024
ROWS = 80
SLOTS = 3
USED = ROWS * SLOTS
PAD = 256
TEN = 4
CH = PAD // TEN
HEADS = 4
HD = 64
W = 256
BLOCKS = (slice(0, 512), slice(512, 1024))
BUCKETS = ((1024, 1024, 256, 256), (1024, 1024, 256, 256), (256, 1024, 128, 0), (3072, 256, 768, 768))
A1, Y1, A2, Y2, OUT, DOUT, DA2, DY1, DA1, DX, SMALL = range(11)


def dot_nn(a, b):
    return lax.dot_general(a, b, (((1,), (0,)), ((), ())), preferred_element_type=F32)


def dot_nt(a, b):
    return lax.dot_general(a, b, (((1,), (1,)), ((), ())), preferred_element_type=F32)


def dot_tn(a, b):
    return lax.dot_general(a, b, (((0,), (0,)), ((), ())), preferred_element_type=F32)


def tile(j, size=W):
    return pl.ds(pl.multiple_of(j * size, size), size)


def normed(u):
    center = u - jnp.mean(u, -1, keepdims=True)
    inverse = lax.rsqrt(jnp.mean(center * center, -1, keepdims=True) + 1e-05)
    return center * inverse, inverse


def norm_back(grad, u, gain):
    unit, inverse = normed(u)
    scaled = grad * gain
    along = jnp.mean(scaled * unit, -1, keepdims=True)
    grad_u = inverse * (scaled - jnp.mean(scaled, -1, keepdims=True) - unit * along)
    return grad_u, jnp.sum(grad * unit, 0, keepdims=True), jnp.sum(grad, 0, keepdims=True)


def kernel(
    reduce_dp,
    tok_hbm, cot_hbm, docs, live, gains, shifts, wqkv_hbm, qvb, wo_hbm, obias, wup_hbm, upb, wdn_hbm,
    act_out, dx_out, gdn_out, gup_out, go_out, gqkv_out, small_out,
    tok, cot, wqkv, wo, wup, wdn, mask, xc, a1, qkv, prob, att, y1s, y1r, x2c, a2, slope, g,
    y2s, y2r, actg, doc, dy2, dg, dh, da2s, da2r, dx2c, dy1, dqkv, da1s, da1r, dxg,
    pipe_f, pipe_b, pipe_fs, pipe_bs, sm, smz, smc, smy, smx,
    wg0, wg1, wg2, wg3, rc0, rc1, rc2, rc3, p10, p11, p12, p13, q10, q11, q13,
    p20, p21, p22, p23, q20, q21, q23,
    load_sem, out_sem, tp_s, tp_r, pp_s, pp_r, dp_s, dp_r, dp_l, sd_s, sd_r,
):
    wgs, rcs = (wg0, wg1, wg2, wg3), (rc0, rc1, rc2, rc3)
    p1s, q1s = (p10, p11, p12, p13), (q10, q11, None, q13)
    p2s, q2s = (p20, p21, p22, p23), (q20, q21, None, q23)
    gouts = (gdn_out, gup_out, go_out, gqkv_out)
    pipe = lax.axis_index("pipe")
    dp = lax.axis_index("dp")
    z = lax.axis_index("tensor")
    first = pipe == 0
    second = pipe == 1
    gx, gy, gc = dp // 4, (dp // 2) % 2, dp % 2
    core_peer = gx * 4 + gy * 2 + (1 - gc)
    y_peer = gx * 4 + (1 - gy) * 2 + gc
    x_peers = [((gx + t) % 4) * 4 + gy * 2 + gc for t in (1, 2, 3)]
    mine = tile(z, CH)

    def load(k, src, dst):
        return pltpu.make_async_copy(src, dst, load_sem.at[k])

    loads = {
        "tok": load(0, tok_hbm, tok.at[pl.ds(0, USED)]),
        "cot": load(1, cot_hbm, cot.at[pl.ds(0, USED)]),
        "qkv": load(2, wqkv_hbm, wqkv),
        "o": load(3, wo_hbm, wo),
        "up": load(4, wup_hbm, wup),
        "dn": load(5, wdn_hbm, wdn),
    }

    @pl.when(first)
    def _():
        for name in ("tok", "qkv", "o", "up", "dn"):
            loads[name].start()

    @pl.when(second)
    def _():
        for name in ("cot", "dn", "qkv", "o", "up"):
            loads[name].start()

    barrier = pltpu.get_barrier_semaphore()
    partners = [{"tensor": (z + t) % 4} for t in (1, 2, 3)] + [{"pipe": 1 - pipe}]
    if reduce_dp:
        partners += [{"dp": core_peer}, {"dp": y_peer}] + [{"dp": p} for p in x_peers]
    for partner in partners:
        pl.semaphore_signal(barrier, inc=1, device_id=partner, device_id_type=MESH)

    def places(shape, axis):
        at = lax.broadcasted_iota(jnp.int32, shape, axis)
        slot = (at >= ROWS).astype(jnp.int32) + (at >= 2 * ROWS).astype(jnp.int32)
        slot = slot + (at >= 3 * ROWS).astype(jnp.int32)
        spot = at - ROWS * slot
        segment = 4 * slot
        alive = jnp.zeros(shape, F32)
        for s in range(SLOTS):
            end = jnp.int32(0)
            for k in range(3):
                end = end + docs[s, k]
                segment = segment + jnp.where((slot == s) & (spot >= end), 1, 0)
            alive = jnp.where((slot == s) & (spot.astype(F32) < counts[s : s + 1, :]), 1.0, alive)
        return at, segment, alive

    counts = jnp.sum(live[...].astype(F32), 1, keepdims=True)
    row_at, row_segment, row_live = places((PAD, 1), 0)
    col_at, col_segment, col_live = places((1, PAD), 1)
    seen = (row_segment == col_segment) & (col_at <= row_at)
    seen = seen & ((col_live + jnp.where(row_at == col_at, 1.0, 0.0)) > 0.5)
    mask[...] = jnp.where(seen, 1.0, 0.0)
    sm[...] = jnp.zeros_like(sm)
    head_of = lax.broadcasted_iota(jnp.int32, (1, W), 1) // HD

    pl.semaphore_wait(barrier, len(partners))

    def tp_copy(k, t, src, dst):
        return pltpu.make_async_remote_copy(
            src_ref=src,
            dst_ref=dst,
            send_sem=tp_s.at[k, t - 1],
            recv_sem=tp_r.at[k, t - 1],
            device_id={"tensor": (z + t) % 4},
            device_id_type=MESH,
        )

    def scatter(k, src, dst):
        return [tp_copy(k, t, src.at[tile((z + t) % 4, CH)], dst.at[t - 1]) for t in (2, 1, 3)]

    def gather(k, buf):
        return [tp_copy(k, t, buf.at[mine], buf.at[mine]) for t in (2, 1, 3)]

    def start(copies):
        for copy in copies:
            copy.start()

    def arrive(copies):
        for copy in copies:
            copy.wait_recv()

    def sent(copies):
        for copy in copies:
            copy.wait_send()

    ex = {
        A1: gather(A1, a1),
        Y1: scatter(Y1, y1s, y1r),
        A2: gather(A2, a2),
        Y2: scatter(Y2, y2s, y2r),
        OUT: gather(OUT, actg),
        DOUT: gather(DOUT, dy2),
        DA2: scatter(DA2, da2s, da2r),
        DY1: gather(DY1, dy1),
        DA1: scatter(DA1, da1s, da1r),
        DX: gather(DX, dxg),
        SMALL: [tp_copy(SMALL, t, smz.at[z], smz.at[z]) for t in (2, 1, 3)],
    }
    forth = pltpu.make_async_remote_copy(
        src_ref=pipe_fs, dst_ref=pipe_f, send_sem=pp_s.at[0], recv_sem=pp_r.at[0],
        device_id={"pipe": 1 - pipe}, device_id_type=MESH,
    )
    back = pltpu.make_async_remote_copy(
        src_ref=pipe_bs, dst_ref=pipe_b, send_sem=pp_s.at[1], recv_sem=pp_r.at[1],
        device_id={"pipe": 1 - pipe}, device_id_type=MESH,
    )

    def summed(src, dst):
        total = src[mine].astype(F32)
        for t in range(3):
            total = total + dst[t].astype(F32)
        return total

    def dp_copy(b, k, src, dst, peer):
        return pltpu.make_async_remote_copy(
            src_ref=src, dst_ref=dst, send_sem=dp_s.at[b, k], recv_sem=dp_r.at[b, k],
            device_id={"dp": peer}, device_id_type=MESH,
        )

    def rows(at, size):
        return pl.ds(pl.multiple_of(at, 16), size)

    def add_into(dst, at, size, terms):
        step = next(n for n in (64, 48, 32, 16) if size % n == 0)

        @pl.loop(0, size // step)
        def _(i):
            off = pl.multiple_of(i * step, 16)
            total = dst[rows(at + off, step), :].astype(F32)
            for term in terms:
                total = total + term(off, step).astype(F32)
            dst[rows(at + off, step), :] = total.astype(BF16)

    def bucket(b):
        size, _, p, q = BUCKETS[b]
        half = size // 2
        wg, rc, out = wgs[b], rcs[b], gouts[b]
        p1, q1, p2, q2 = p1s[b], q1s[b], p2s[b], q2s[b]
        base = gc * half
        p8, p4, q8, q2n = p // 8, p // 4, q // 8, q // 2
        c = {}
        c["core"] = [dp_copy(b, 0, wg.at[rows((1 - gc) * half, half)], rc, core_peer)]
        xs = [(gx + t) % 4 for t in (1, 2, 3)]
        order = (1, 0, 2)
        c["p1"] = [
            dp_copy(b, 1 + i, rc.at[rows(xs[i] * p4, p4)], p1.at[i], x_peers[i]) for i in order
        ]
        p_fin = gx * p4 + gy * p8
        c["p2"] = [dp_copy(b, 5, rc.at[rows(gx * p4 + (1 - gy) * p8, p8)], p2, y_peer)]
        c["p3"] = [dp_copy(b, 9, rc.at[rows(p_fin, p8)], out.at[rows(base + p_fin, p8)], y_peer)]
        p_part = out.at[rows(base + gx * p4, p4)]
        c["p4"] = [dp_copy(b, 13 + i, p_part, p_part, x_peers[i]) for i in order]
        half_out = out.at[rows(base, half)]
        c["all"] = [dp_copy(b, 17, half_out, half_out, core_peer)]
        keep = [
            pltpu.make_async_copy(
                rc.at[rows(p_fin, p8)], out.at[rows(base + p_fin, p8)], dp_l.at[b, 0]
            )
        ]
        if q:
            q_fin = p + gy * q2n + gx * q8
            c["q1"] = [dp_copy(b, 4, rc.at[rows(p + (1 - gy) * q2n, q2n)], q1, y_peer)]
            c["q2"] = [
                dp_copy(b, 6 + i, rc.at[rows(p + gy * q2n + xs[i] * q8, q8)], q2.at[i], x_peers[i])
                for i in order
            ]
            c["q3"] = [
                dp_copy(b, 10 + i, rc.at[rows(q_fin, q8)], out.at[rows(base + q_fin, q8)], x_peers[i])
                for i in order
            ]
            q_part = out.at[rows(base + p + gy * q2n, q2n)]
            c["q4"] = [dp_copy(b, 16, q_part, q_part, y_peer)]
            keep.append(
                pltpu.make_async_copy(
                    rc.at[rows(q_fin, q8)], out.at[rows(base + q_fin, q8)], dp_l.at[b, 1]
                )
            )

        def step0():
            start(c["core"])

        def step1():
            arrive(c["core"])
            add_into(rc, 0, half, [lambda o, n: wg[rows(base + o, n), :]])
            start(c["p1"])
            if q:
                start(c["q1"])

        def step2():
            if q:
                arrive(c["q1"])
                add_into(rc, p + gy * q2n, q2n, [lambda o, n: q1[rows(o, n), :]])
                start(c["q2"])
            arrive(c["p1"])
            add_into(rc, gx * p4, p4, [
                (lambda o, n, i=i: p1[i, rows(o, n), :]) for i in range(3)
            ])
            start(c["p2"])

        def step3():
            arrive(c["p2"])
            add_into(rc, p_fin, p8, [lambda o, n: p2[rows(o, n), :]])
            start(c["p3"])
            keep[0].start()
            if q:
                arrive(c["q2"])
                add_into(rc, q_fin, q8, [
                    (lambda o, n, i=i: q2[i, rows(o, n), :]) for i in range(3)
                ])
                start(c["q3"])
                keep[1].start()

        def step4():
            keep[0].wait()
            arrive(c["p3"])
            start(c["p4"])
            if q:
                keep[1].wait()
                arrive(c["q3"])
                start(c["q4"])

        def step5():
            arrive(c["p4"])
            if q:
                arrive(c["q4"])
            start(c["all"])

        def step6():
            arrive(c["all"])
            for group in c.values():
                sent(group)

        return [step0, step1, step2, step3, step4, step5, step6]

    def sd_copy(k, src, dst, peer):
        return pltpu.make_async_remote_copy(
            src_ref=src, dst_ref=dst, send_sem=sd_s.at[k], recv_sem=sd_r.at[k],
            device_id={"dp": peer}, device_id_type=MESH,
        )

    steps = [bucket(b) for b in range(4)] if reduce_dp else None

    def early(b, s):
        if reduce_dp:
            pl.when(first)(steps[b][s])

    @pl.when(first)
    def _():
        loads["tok"].wait()
        tok[pl.ds(USED, PAD - USED), :] = jnp.zeros((PAD - USED, D), F32)

        @pl.loop(0, TEN)
        def _(i):
            unit, _ = normed(tok[tile(i, CH), :])
            a1[tile(i, CH), :] = (unit * gains[0:1, :] + shifts[0:1, :]).astype(BF16)

        xc[...] = tok[mine, :]

    def output_grads():
        for j in BLOCKS:
            dg[:, j] = dot_nt(dy2[...], wdn[j, :])

    @pl.when(second)
    def _():
        loads["cot"].wait()
        cot[pl.ds(USED, PAD - USED), :] = jnp.zeros((PAD - USED, D), F32)
        masked = cot[...] * row_live
        cot[...] = masked
        dy2[...] = masked.astype(BF16)
        sm[5:6, :] = jnp.sum(masked, 0, keepdims=True)
        doc[...] = cot[mine, :]
        loads["dn"].wait()
        output_grads()
        forth.wait_recv()
        inputs = pipe_f[...].astype(F32)
        xc[...] = inputs
        unit, _ = normed(inputs)
        a1[mine, :] = (unit * gains[0:1, :] + shifts[0:1, :]).astype(BF16)
        start(ex[A1])
        arrive(ex[A1])

    loads["qkv"].wait()
    for j in range(3):
        part = dot_nn(a1[...], wqkv[j])
        if j != 1:
            part = part + qvb[j // 2 : j // 2 + 1, :]
        qkv[:, j * W : (j + 1) * W] = part.astype(BF16)

    def head_rows(values, h):
        return (values.astype(F32) * jnp.where(head_of == h, 1.0, 0.0)).astype(BF16)

    attended = jnp.zeros((PAD, W), F32)
    for h in range(HEADS):
        scores = dot_nt(head_rows(qkv[:, 0:W], h), qkv[:, W : 2 * W]) * (1.0 / math.sqrt(HD))
        scores = jnp.where(mask[...] > 0.5, scores, -1000000000.0)
        expo = jnp.exp(scores - jnp.max(scores, -1, keepdims=True))
        p = expo / jnp.sum(expo, -1, keepdims=True)
        prob[h] = p
        attended = attended + dot_nn(p.astype(BF16), head_rows(qkv[:, 2 * W : 3 * W], h))

    att[...] = attended.astype(BF16)
    loads["o"].wait()
    for j in BLOCKS:
        y1s[:, j] = dot_nn(att[...], wo[:, j]).astype(BF16)

    start(ex[Y1])
    arrive(ex[Y1])
    middle = xc[...] + summed(y1s, y1r) + obias[0:1, :]
    x2c[...] = middle
    unit, _ = normed(middle)
    a2[mine, :] = (unit * gains[1:2, :] + shifts[1:2, :]).astype(BF16)
    start(ex[A2])
    loads["up"].wait()
    arrive(ex[A2])

    for j in BLOCKS:
        hidden = dot_nn(a2[...], wup[:, j]) + upb[:, j]
        square = hidden * hidden
        root = math.sqrt(2.0 / math.pi)
        bent = jnp.tanh(root * hidden * (1.0 + 0.044715 * square))
        lifted = 0.5 * (1.0 + bent)
        g[:, j] = (hidden * lifted).astype(BF16)
        inner = root * (1.0 + 3.0 * 0.044715 * square)
        slope[:, j] = lifted + 0.5 * hidden * (1.0 - bent * bent) * inner

    def down():
        for j in BLOCKS:
            y2s[:, j] = dot_nn(g[...], wdn[:, j]).astype(BF16)

        start(ex[Y2])

    def layer_output():
        arrive(ex[Y2])
        result = (x2c[...] + summed(y2s, y2r) + obias[1:2, :]).astype(BF16)
        pipe_fs[...] = result
        actg[mine, :] = result

    act_copy = pltpu.make_async_copy(actg.at[pl.ds(0, USED)], act_out, out_sem.at[0])

    @pl.when(first)
    def _():
        loads["dn"].wait()
        down()
        layer_output()
        forth.start()
        start(ex[OUT])
        back.wait_recv()
        dy2[mine, :] = pipe_b[...]
        doc[...] = pipe_b[...].astype(F32)
        start(ex[DOUT])
        arrive(ex[DOUT])
        output_grads()

    for j in BLOCKS:
        grad = (dg[:, j] * slope[:, j]).astype(BF16)
        dh[:, j] = grad
        sm[7:8, j] = jnp.sum(grad.astype(F32), 0, keepdims=True)

    for j in BLOCKS:
        da2s[:, j] = dot_nt(dh[...], wup[j, :]).astype(BF16)

    start(ex[DA2])

    @pl.when(first)
    def _():
        sm[5:6, :] = jnp.sum(dy2[...].astype(F32), 0, keepdims=True)

    for j in BLOCKS:
        wg0[j, :] = dot_tn(g[:, j], dy2[...]).astype(BF16)

    early(0, 0)
    for j in BLOCKS:
        wg1[j, :] = dot_tn(a2[:, j], dh[...]).astype(BF16)

    early(1, 0)
    arrive(ex[DA2])
    grad_u, gain_grad, shift_grad = norm_back(summed(da2s, da2r), x2c[...], gains[1:2, :])
    grad_middle = doc[...] + grad_u
    dy1[mine, :] = grad_middle.astype(BF16)
    start(ex[DY1])
    dx2c[...] = grad_middle
    sm[1:2, :] = gain_grad
    sm[3:4, :] = shift_grad
    sm[4:5, :] = jnp.sum(grad_middle, 0, keepdims=True)
    early(0, 1)
    arrive(ex[DY1])

    att_grad = dot_nt(dy1[...], wo[...]).astype(BF16)
    dqkv[:, 2 * W : 3 * W] = att_grad
    grad_q = grad_k = grad_v = jnp.zeros((PAD, W), F32)
    for h in range(HEADS):
        p = prob[h]
        own = head_rows(dqkv[:, 2 * W : 3 * W], h)
        grad_p = dot_nt(own, qkv[:, 2 * W : 3 * W])
        grad_v = grad_v + dot_tn(p.astype(BF16), own)
        grad_s = p * (grad_p - jnp.sum(grad_p * p, -1, keepdims=True))
        grad_s = grad_s.astype(BF16)
        grad_q = grad_q + dot_nn(grad_s, head_rows(qkv[:, W : 2 * W], h))
        grad_k = grad_k + dot_tn(grad_s, head_rows(qkv[:, 0:W], h))

    scale = 1.0 / math.sqrt(HD)
    for j, (grad, factor) in enumerate(((grad_q, scale), (grad_k, scale), (grad_v, 1.0))):
        low = (grad * factor).astype(BF16)
        dqkv[:, j * W : (j + 1) * W] = low
        if j != 1:
            at = (j // 2) * W
            sm[6:7, at : at + W] = jnp.sum(low.astype(F32), 0, keepdims=True)

    for j in BLOCKS:
        part = dot_nt(dqkv[:, 0:W], wqkv[0, j, :]) + dot_nt(dqkv[:, W : 2 * W], wqkv[1, j, :])
        da1s[:, j] = (part + dot_nt(dqkv[:, 2 * W : 3 * W], wqkv[2, j, :])).astype(BF16)

    start(ex[DA1])
    wg2[...] = dot_tn(att[...], dy1[...]).astype(BF16)
    early(2, 0)
    for j in range(D // W):
        part = dot_tn(a1[:, j * W : (j + 1) * W], dqkv[...]).astype(BF16)
        for i in range(3):
            at = i * D + j * W
            wg3[at : at + W, :] = part[:, i * W : (i + 1) * W]

    early(3, 0)
    early(1, 1)
    arrive(ex[DA1])
    grad_u, gain_grad, shift_grad = norm_back(summed(da1s, da1r), xc[...], gains[0:1, :])
    sm[0:1, :] = gain_grad
    sm[2:3, :] = shift_grad
    low = (dx2c[...] + grad_u).astype(BF16)
    pipe_bs[...] = low
    dxg[mine, :] = low

    @pl.when(second)
    def _():
        back.start()

    start(ex[DX])
    smz[z] = sm[...]
    start(ex[SMALL])

    @pl.when(second)
    def _():
        down()
        layer_output()
        start(ex[OUT])

    if reduce_dp:
        early(0, 2)
        early(2, 1)
        early(3, 1)
        early(1, 2)

        @pl.when(first)
        def _():
            for b, s in ((0, 3), (2, 2), (3, 2), (1, 3), (0, 4), (2, 3), (3, 3), (1, 4)):
                steps[b][s]()

        @pl.when(second)
        def _():
            for s in range(5):
                for b in range(4):
                    if s < 4 or b < 2:
                        steps[b][s]()

        for b, s in ((0, 5), (2, 4), (3, 4), (1, 5), (2, 5), (3, 5)):
            steps[b][s]()
        for b in range(4):
            steps[b][6]()

    arrive(ex[OUT])
    act_copy.start()
    arrive(ex[DX])
    dx_copy = pltpu.make_async_copy(dxg.at[pl.ds(0, USED)], dx_out, out_sem.at[1])
    dx_copy.start()

    arrive(ex[SMALL])
    whole = smz[0] + smz[1] + smz[2] + smz[3]
    own_rows = lax.broadcasted_iota(jnp.int32, (8, D), 0) >= 5
    whole = jnp.where(own_rows, sm[...], whole)
    if reduce_dp:
        smc[gc] = whole
        core_copy = sd_copy(0, smc.at[gc], smc.at[gc], core_peer)
        core_copy.start()
        core_copy.wait()
        smy[gy] = smc[0] + smc[1]
        y_copy = sd_copy(1, smy.at[gy], smy.at[gy], y_peer)
        y_copy.start()
        y_copy.wait()
        smx[gx] = smy[0] + smy[1]
        x_copies = [sd_copy(2 + i, smx.at[gx], smx.at[gx], x_peers[i]) for i in range(3)]
        start(x_copies)
        for copy in x_copies:
            copy.wait()
        whole = smx[0] + smx[1] + smx[2] + smx[3]
    small_out[...] = whole

    act_copy.wait()
    dx_copy.wait()
    for k in (Y1, A2, Y2, OUT, DA2, DY1, DA1, DX, SMALL):
        sent(ex[k])

    @pl.when(first)
    def _():
        forth.wait_send()
        sent(ex[DOUT])

    @pl.when(second)
    def _():
        back.wait_send()
        sent(ex[A1])

    if not reduce_dp:
        copies = [
            pltpu.make_async_copy(wg, out, dp_l.at[b, 0])
            for b, (wg, out) in enumerate(zip(wgs, gouts))
        ]
        start(copies)
        for copy in copies:
            copy.wait()


def call(reduce_dp, *operands):
    hbm = pl.BlockSpec(memory_space=pl.ANY)
    vmem = pl.BlockSpec(memory_space=pltpu.VMEM)
    smem = pl.BlockSpec(memory_space=pltpu.SMEM)

    def low(*shape):
        return pltpu.VMEM(shape, BF16)

    def wide(*shape):
        return pltpu.VMEM(shape, F32)

    scratch = [
        wide(PAD, D), wide(PAD, D), low(3, D, W), low(256, D), low(D, D), low(D, D),
        wide(PAD, PAD), wide(CH, D), low(PAD, D), low(PAD, 768), wide(HEADS, PAD, PAD), low(PAD, W),
        low(PAD, D), low(3, CH, D), wide(CH, D), low(PAD, D), wide(PAD, D), low(PAD, D),
        low(PAD, D), low(3, CH, D), low(PAD, D), wide(CH, D), low(PAD, D), wide(PAD, D), low(PAD, D),
        low(PAD, D), low(3, CH, D), wide(CH, D), low(PAD, D), low(PAD, 768), low(PAD, D),
        low(3, CH, D), low(PAD, D),
        low(CH, D), low(CH, D), low(CH, D), low(CH, D),
        wide(8, D), wide(4, 8, D), wide(2, 8, D), wide(2, 8, D), wide(4, 8, D),
    ]
    scratch += [low(size, width) for size, width, p, q in BUCKETS]
    scratch += [low(size // 2, width) for size, width, p, q in BUCKETS]
    scratch += [low(3, p // 4, width) for size, width, p, q in BUCKETS]
    scratch += [low(q // 2, width) for size, width, p, q in BUCKETS if q]
    scratch += [low(p // 8, width) for size, width, p, q in BUCKETS]
    scratch += [low(3, q // 8, width) for size, width, p, q in BUCKETS if q]
    dma = pltpu.SemaphoreType.DMA
    scratch += [
        dma((6,)), dma((2,)), dma((11, 3)), dma((11, 3)), dma((2,)), dma((2,)),
        dma((4, 18)), dma((4, 18)), dma((4, 2)), dma((5,)), dma((5,)),
    ]
    return pl.pallas_call(
        functools.partial(kernel, reduce_dp),
        out_shape=[
            jax.ShapeDtypeStruct((USED, D), BF16),
            jax.ShapeDtypeStruct((USED, D), BF16),
            *[jax.ShapeDtypeStruct((size, width), BF16) for size, width, _, _ in BUCKETS],
            jax.ShapeDtypeStruct((8, D), F32),
        ],
        in_specs=[hbm, hbm, smem, vmem, vmem, vmem, hbm, vmem, hbm, vmem, hbm, vmem, hbm],
        out_specs=[hbm] * 6 + [vmem],
        scratch_shapes=scratch,
        compiler_params=pltpu.CompilerParams(
            collective_id=0, has_side_effects=True, vmem_limit_bytes=40 * 1024 * 1024
        ),
        name="layers",
    )(*operands)


def widen_kernel(*refs):
    small, lows = refs[6], refs[:6]
    outs, (gains, shifts, qv, biases, upb) = refs[7:13], refs[13:]
    for low, out in zip(lows, outs):
        out[...] = low[...].astype(F32)
    gains[...] = small[0:2, :]
    shifts[...] = small[2:4, :]
    biases[...] = small[4:6, :]
    qv[0:1, :] = small[6:7, 0:W]
    qv[1:2, :] = small[6:7, W : 2 * W]
    upb[...] = small[7:8, :]


def widen(lows, small):
    count = 8

    def spec(shape):
        blocks = 5 if shape[0] == USED else count
        return pl.BlockSpec(
            (shape[0] // blocks, shape[1]), lambda i: (jnp.minimum(i, blocks - 1), 0)
        )

    def fixed(shape):
        return pl.BlockSpec(shape, lambda i: (0, 0))

    flat = [(2, D), (2, D), (2, W), (2, D), (1, D)]
    return pl.pallas_call(
        widen_kernel,
        grid=(count,),
        out_shape=[jax.ShapeDtypeStruct(a.shape, F32) for a in lows]
        + [jax.ShapeDtypeStruct(shape, F32) for shape in flat],
        in_specs=[spec(a.shape) for a in lows] + [fixed((8, D))],
        out_specs=[spec(a.shape) for a in lows] + [fixed(shape) for shape in flat],
        compiler_params=pltpu.CompilerParams(vmem_limit_bytes=40 * 1024 * 1024),
        name="widen",
    )(*lows, small)


def local(
    tokens,
    cotangent,
    doc_lengths,
    live_mask,
    norm_gains,
    norm_biases,
    query_key_value,
    query_value_bias,
    output_weight,
    output_biases,
    expand_weight,
    expand_bias,
    reduce_weight,
):
    reduce_dp = lax.axis_size("dp") == 16
    act, dx, gdn, gup, go, gqkv, small = call(
        reduce_dp,
        tokens.reshape(USED, D),
        cotangent.reshape(USED, D),
        doc_lengths.reshape(SLOTS, 3),
        live_mask,
        norm_gains[0],
        norm_biases[0],
        query_key_value[0].transpose(1, 0, 2),
        query_value_bias[0],
        output_weight[0],
        output_biases[0],
        expand_weight[0],
        expand_bias,
        reduce_weight[0],
    )
    act, dx, gdn, gup, go, gqkv, gains, shifts, qv, biases, upb = widen(
        (act, dx, gdn, gup, go, gqkv), small
    )
    return (
        act.reshape(1, SLOTS, ROWS, D),
        dx.reshape(1, SLOTS, ROWS, D),
        gains[None],
        shifts[None],
        gqkv.reshape(3, D, W).transpose(1, 0, 2)[None],
        qv[None],
        go[None],
        biases[None],
        gup[None],
        upb,
        gdn[None],
    )


def solution(mesh):
    in_specs = (
        P(None, "dp", None),
        P(None, "dp", None),
        P(None, "dp", None),
        P(None, "dp"),
        P("pipe", None, None),
        P("pipe", None, None),
        P("pipe", None, None, "tensor"),
        P("pipe", None, "tensor"),
        P("pipe", "tensor", None),
        P("pipe", None, None),
        P("pipe", None, "tensor"),
        P("pipe", "tensor"),
        P("pipe", "tensor", None),
    )
    out_specs = (
        P("pipe", None, "dp", None),
        P("pipe", None, "dp", None),
        P("pipe", None, None),
        P("pipe", None, None),
        P("pipe", None, None, "tensor"),
        P("pipe", None, "tensor"),
        P("pipe", "tensor", None),
        P("pipe", None, None),
        P("pipe", None, "tensor"),
        P("pipe", "tensor"),
        P("pipe", "tensor", None),
    )
    return jax.shard_map(local, mesh=mesh, in_specs=in_specs, out_specs=out_specs, check_vma=False)
```

```python
import functools
import math

import jax
import jax.numpy as jnp
from jax import lax
from jax.experimental import pallas as pl
from jax.experimental.pallas import tpu as pltpu
from jax.sharding import PartitionSpec as P

MESH = pl.DeviceIdType.MESH
F32 = jnp.float32
BF16 = jnp.bfloat16
D = 1024
ROWS = 80
SLOTS = 3
USED = ROWS * SLOTS
PAD = 256
TEN = 4
CH = PAD // TEN
HEADS = 4
HD = 64
W = 256
BLOCKS = (slice(0, 512), slice(512, 1024))
BUCKETS = (
    (1024, 1024, (256, 128, 128)),
    (1024, 1024, (128, 256, 128)),
    (256, 1024, (0, 0, 128)),
    (3072, 256, (512, 512, 512)),
)
A1, Y1, A2, Y2, OUT, DOUT, DA2, DY1, DA1, DX, SMALL = range(11)


def dot_nn(a, b):
    return lax.dot_general(a, b, (((1,), (0,)), ((), ())), preferred_element_type=F32)


def dot_nt(a, b):
    return lax.dot_general(a, b, (((1,), (1,)), ((), ())), preferred_element_type=F32)


def dot_tn(a, b):
    return lax.dot_general(a, b, (((0,), (0,)), ((), ())), preferred_element_type=F32)


def tile(j, size=W):
    return pl.ds(pl.multiple_of(j * size, size), size)


def normed(u):
    center = u - jnp.mean(u, -1, keepdims=True)
    inverse = lax.rsqrt(jnp.mean(center * center, -1, keepdims=True) + 1e-05)
    return center * inverse, inverse


def norm_back(grad, u, gain):
    unit, inverse = normed(u)
    scaled = grad * gain
    along = jnp.mean(scaled * unit, -1, keepdims=True)
    grad_u = inverse * (scaled - jnp.mean(scaled, -1, keepdims=True) - unit * along)
    return grad_u, jnp.sum(grad * unit, 0, keepdims=True), jnp.sum(grad, 0, keepdims=True)


def kernel(
    reduce_dp,
    tok_hbm, cot_hbm, docs, live_hbm, gains_hbm, shifts_hbm, wqkv_hbm, qvb_hbm, wo_hbm, obias_hbm,
    wup_hbm, upb_hbm, wdn_hbm,
    act_out, dx_out, gdn_out, gup_out, go_out, gqkv_out, small_out,
    tok, cot, wqkv, wo, wup, wdn, mask, xc, a1, qkv, prob, att, y1s, y1r, x2c, a2, slope, g,
    y2s, y2r, actg, doc, dy2, dg, dh, da2s, da2r, dx2c, dy1, dqkv, da1s, da1r, dxg,
    pipe_f, pipe_b, pipe_fs, pipe_bs, sm, smz, smc, smy, smx,
    wg0, wg1, wg2, wg3, rc0, rc1, rc2, rc3, in0, in1, in2, in3,
    live, gains, shifts, qvb, obias, upb,
    load_sem, out_sem, tp_s, tp_r, pp_s, pp_r, dp_s, dp_r, dp_l, sd_s, sd_r,
):
    wgs, rcs = (wg0, wg1, wg2, wg3), (rc0, rc1, rc2, rc3)
    ins = (in0, in1, in2, in3)
    gouts = (gdn_out, gup_out, go_out, gqkv_out)
    pipe = lax.axis_index("pipe")
    dp = lax.axis_index("dp")
    z = lax.axis_index("tensor")
    first = pipe == 0
    second = pipe == 1
    gx, gy, gc = dp // 4, (dp // 2) % 2, dp % 2
    core_peer = gx * 4 + gy * 2 + (1 - gc)
    y_peer = gx * 4 + (1 - gy) * 2 + gc
    x_peers = [((gx + t) % 4) * 4 + gy * 2 + gc for t in (1, 2, 3)]
    mine = tile(z, CH)
    cube_bits = (((gx + 1) // 2) % 2, gx // 2, gy)
    cube_peers = (
        (gx + 1 - 2 * (gx % 2)) * 4 + gy * 2 + gc,
        (3 - gx) * 4 + gy * 2 + gc,
        y_peer,
    )

    def load(k, src, dst):
        return pltpu.make_async_copy(src, dst, load_sem.at[k])

    loads = {
        "tok": load(0, tok_hbm, tok.at[pl.ds(0, USED)]),
        "cot": load(1, cot_hbm, cot.at[pl.ds(0, USED)]),
        "qkv": load(2, wqkv_hbm, wqkv),
        "o": load(3, wo_hbm, wo),
        "up": load(4, wup_hbm, wup),
        "dn": load(5, wdn_hbm, wdn),
    }

    small_loads = [
        load(6 + k, src, dst)
        for k, (src, dst) in enumerate((
            (live_hbm, live), (gains_hbm, gains), (shifts_hbm, shifts),
            (qvb_hbm, qvb), (obias_hbm, obias), (upb_hbm, upb),
        ))
    ]
    for copy in small_loads:
        copy.start()

    @pl.when(first)
    def _():
        for name in ("tok", "qkv", "o", "up", "dn"):
            loads[name].start()

    @pl.when(second)
    def _():
        for name in ("cot", "dn", "qkv", "o", "up"):
            loads[name].start()

    barrier = pltpu.get_barrier_semaphore()
    partners = [{"tensor": (z + t) % 4} for t in (1, 2, 3)] + [{"pipe": 1 - pipe}]
    if reduce_dp:
        partners += [{"dp": core_peer}, {"dp": y_peer}] + [{"dp": p} for p in x_peers]
    for partner in partners:
        pl.semaphore_signal(barrier, inc=1, device_id=partner, device_id_type=MESH)

    def places(shape, axis):
        at = lax.broadcasted_iota(jnp.int32, shape, axis)
        slot = (at >= ROWS).astype(jnp.int32) + (at >= 2 * ROWS).astype(jnp.int32)
        slot = slot + (at >= 3 * ROWS).astype(jnp.int32)
        spot = at - ROWS * slot
        segment = 4 * slot
        alive = jnp.zeros(shape, F32)
        for s in range(SLOTS):
            end = jnp.int32(0)
            for k in range(3):
                end = end + docs[s, 0, k]
                segment = segment + jnp.where((slot == s) & (spot >= end), 1, 0)
            alive = jnp.where((slot == s) & (spot.astype(F32) < counts[s : s + 1, :]), 1.0, alive)
        return at, segment, alive

    for copy in small_loads:
        copy.wait()
    counts = jnp.sum(live[...].astype(F32), 1, keepdims=True)
    row_at, row_segment, row_live = places((PAD, 1), 0)
    col_at, col_segment, col_live = places((1, PAD), 1)
    seen = (row_segment == col_segment) & (col_at <= row_at)
    seen = seen & ((col_live + jnp.where(row_at == col_at, 1.0, 0.0)) > 0.5)
    mask[...] = jnp.where(seen, 1.0, 0.0)
    sm[...] = jnp.zeros_like(sm)
    head_of = lax.broadcasted_iota(jnp.int32, (1, W), 1) // HD

    pl.semaphore_wait(barrier, len(partners))

    def tp_copy(k, t, src, dst):
        return pltpu.make_async_remote_copy(
            src_ref=src,
            dst_ref=dst,
            send_sem=tp_s.at[k, t - 1],
            recv_sem=tp_r.at[k, t - 1],
            device_id={"tensor": (z + t) % 4},
            device_id_type=MESH,
        )

    def scatter(k, src, dst):
        return [tp_copy(k, t, src.at[tile((z + t) % 4, CH)], dst.at[t - 1]) for t in (2, 1, 3)]

    def gather(k, buf):
        return [tp_copy(k, t, buf.at[mine], buf.at[mine]) for t in (2, 1, 3)]

    def start(copies):
        for copy in copies:
            copy.start()

    def arrive(copies):
        for copy in copies:
            copy.wait_recv()

    def sent(copies):
        for copy in copies:
            copy.wait_send()

    ex = {
        A1: gather(A1, a1),
        Y1: scatter(Y1, y1s, y1r),
        A2: gather(A2, a2),
        Y2: scatter(Y2, y2s, y2r),
        OUT: gather(OUT, actg),
        DOUT: gather(DOUT, dy2),
        DA2: scatter(DA2, da2s, da2r),
        DY1: gather(DY1, dy1),
        DA1: scatter(DA1, da1s, da1r),
        DX: gather(DX, dxg),
        SMALL: [tp_copy(SMALL, t, smz.at[z], smz.at[z]) for t in (2, 1, 3)],
    }
    forth = pltpu.make_async_remote_copy(
        src_ref=pipe_fs, dst_ref=pipe_f, send_sem=pp_s.at[0], recv_sem=pp_r.at[0],
        device_id={"pipe": 1 - pipe}, device_id_type=MESH,
    )
    back = pltpu.make_async_remote_copy(
        src_ref=pipe_bs, dst_ref=pipe_b, send_sem=pp_s.at[1], recv_sem=pp_r.at[1],
        device_id={"pipe": 1 - pipe}, device_id_type=MESH,
    )

    def summed(src, dst):
        total = src[mine].astype(F32)
        for t in range(3):
            total = total + dst[t].astype(F32)
        return total

    def dp_copy(b, k, src, dst, peer):
        return pltpu.make_async_remote_copy(
            src_ref=src, dst_ref=dst, send_sem=dp_s.at[b, k], recv_sem=dp_r.at[b, k],
            device_id={"dp": peer}, device_id_type=MESH,
        )

    def rows(at, size):
        return pl.ds(pl.multiple_of(at, 16), size)

    def add_into(dst, at, size, term):
        step = next(n for n in (64, 48, 32, 16) if size % n == 0)

        @pl.loop(0, size // step)
        def _(i):
            off = pl.multiple_of(i * step, 16)
            total = dst[rows(at + off, step), :].astype(F32) + term(off, step).astype(F32)
            dst[rows(at + off, step), :] = total.astype(BF16)

    def bucket(b):
        size, _, parts = BUCKETS[b]
        half = size // 2
        wg, rc, inc, out = wgs[b], rcs[b], ins[b], gouts[b]
        base = gc * half
        whole = rows((1 - gc) * half, half)
        core = dp_copy(b, 0, wg.at[whole], rc, core_peer)
        pieces = []
        for part, count in enumerate(parts):
            if not count:
                continue
            at = sum(parts[:part])
            begin, spare, size = at, at * 7 // 8, count
            down, up = [], []
            for step in range(3):
                link = (part + step) % 3
                bit, peer = cube_bits[link], cube_peers[link]
                size = size // 2
                own = begin + bit * size
                copy = dp_copy(
                    b, 1 + part * 6 + step, rc.at[rows(begin + (1 - bit) * size, size)],
                    inc.at[rows(spare, size)], peer,
                )
                down.append((copy, own, size, spare))
                here = out.at[rows(base + own, size)]
                source = rc.at[rows(own, size)] if step == 2 else here
                up.append(dp_copy(b, 4 + part * 6 + step, source, here, peer))
                begin, spare = own, spare + size
            keep = pltpu.make_async_copy(
                rc.at[rows(begin, size)], out.at[rows(base + begin, size)], dp_l.at[b, part]
            )
            there = out.at[rows(base + at, count)]
            last = dp_copy(b, 19 + part, there, there, core_peer)
            pieces.append((at, count, down, up, keep, last))

        def step0():
            core.start()

        def step1():
            core.wait_recv()
            for at, count, down, up, keep, last in pieces:
                add_into(rc, at, count, lambda o, n, at=at: wg[rows(base + at + o, n), :])
                down[0][0].start()

        def reduce(step):
            def run():
                for at, count, down, up, keep, last in pieces:
                    copy, own, size, spare = down[step]
                    copy.wait_recv()
                    add_into(rc, own, size, lambda o, n, spare=spare: inc[rows(spare + o, n), :])
                    if step < 2:
                        down[step + 1][0].start()
                    else:
                        up[2].start()
                        keep.start()

            return run

        def spread(step):
            def run():
                for at, count, down, up, keep, last in pieces:
                    up[step].wait_recv()
                    if step == 2:
                        keep.wait()
                    if step:
                        up[step - 1].start()
                    else:
                        last.start()

            return run

        def finish():
            core.wait_send()
            for at, count, down, up, keep, last in pieces:
                last.wait_recv()
                for copy in [d[0] for d in down] + up + [last]:
                    copy.wait_send()

        return [step0, step1, reduce(0), reduce(1), reduce(2), spread(2), spread(1), spread(0), finish]

    def sd_copy(k, src, dst, peer):
        return pltpu.make_async_remote_copy(
            src_ref=src, dst_ref=dst, send_sem=sd_s.at[k], recv_sem=sd_r.at[k],
            device_id={"dp": peer}, device_id_type=MESH,
        )

    steps = [bucket(b) for b in range(4)] if reduce_dp else None

    def now(b, s):
        if reduce_dp:
            steps[b][s]()

    def early(b, s):
        if reduce_dp:
            pl.when(first)(steps[b][s])

    @pl.when(first)
    def _():
        loads["tok"].wait()
        tok[pl.ds(USED, PAD - USED), :] = jnp.zeros((PAD - USED, D), F32)

        @pl.loop(0, TEN)
        def _(i):
            unit, _ = normed(tok[tile(i, CH), :])
            a1[tile(i, CH), :] = (unit * gains[0:1, :] + shifts[0:1, :]).astype(BF16)

        xc[...] = tok[mine, :]

    def output_grads():
        for j in BLOCKS:
            dg[:, j] = dot_nt(dy2[...], wdn[j, :])

    @pl.when(second)
    def _():
        loads["cot"].wait()
        cot[pl.ds(USED, PAD - USED), :] = jnp.zeros((PAD - USED, D), F32)
        masked = cot[...] * row_live
        cot[...] = masked
        dy2[...] = masked.astype(BF16)
        sm[5:6, :] = jnp.sum(masked, 0, keepdims=True)
        doc[...] = cot[mine, :]
        loads["dn"].wait()
        output_grads()
        forth.wait_recv()
        inputs = pipe_f[...].astype(F32)
        xc[...] = inputs
        unit, _ = normed(inputs)
        a1[mine, :] = (unit * gains[0:1, :] + shifts[0:1, :]).astype(BF16)
        start(ex[A1])
        arrive(ex[A1])

    loads["qkv"].wait()
    for j in range(3):
        part = dot_nn(a1[...], wqkv[j])
        if j != 1:
            part = part + qvb[j // 2 : j // 2 + 1, :]
        qkv[:, j * W : (j + 1) * W] = part.astype(BF16)

    def head_rows(values, h):
        return (values.astype(F32) * jnp.where(head_of == h, 1.0, 0.0)).astype(BF16)

    attended = jnp.zeros((PAD, W), F32)
    for h in range(HEADS):
        scores = dot_nt(head_rows(qkv[:, 0:W], h), qkv[:, W : 2 * W]) * (1.0 / math.sqrt(HD))
        scores = jnp.where(mask[...] > 0.5, scores, -1000000000.0)
        expo = jnp.exp(scores - jnp.max(scores, -1, keepdims=True))
        p = expo / jnp.sum(expo, -1, keepdims=True)
        prob[h] = p
        attended = attended + dot_nn(p.astype(BF16), head_rows(qkv[:, 2 * W : 3 * W], h))

    att[...] = attended.astype(BF16)
    loads["o"].wait()
    for j in BLOCKS:
        y1s[:, j] = dot_nn(att[...], wo[:, j]).astype(BF16)

    start(ex[Y1])
    arrive(ex[Y1])
    middle = xc[...] + summed(y1s, y1r) + obias[0:1, :]
    x2c[...] = middle
    unit, _ = normed(middle)
    a2[mine, :] = (unit * gains[1:2, :] + shifts[1:2, :]).astype(BF16)
    start(ex[A2])
    loads["up"].wait()
    arrive(ex[A2])

    for j in BLOCKS:
        hidden = dot_nn(a2[...], wup[:, j]) + upb[:, j]
        square = hidden * hidden
        root = math.sqrt(2.0 / math.pi)
        bent = jnp.tanh(root * hidden * (1.0 + 0.044715 * square))
        lifted = 0.5 * (1.0 + bent)
        g[:, j] = (hidden * lifted).astype(BF16)
        inner = root * (1.0 + 3.0 * 0.044715 * square)
        slope[:, j] = lifted + 0.5 * hidden * (1.0 - bent * bent) * inner

    def down():
        for j in BLOCKS:
            y2s[:, j] = dot_nn(g[...], wdn[:, j]).astype(BF16)

        start(ex[Y2])

    def layer_output():
        arrive(ex[Y2])
        result = (x2c[...] + summed(y2s, y2r) + obias[1:2, :]).astype(BF16)
        pipe_fs[...] = result
        actg[mine, :] = result

    act_copy = pltpu.make_async_copy(actg.at[pl.ds(0, USED)], act_out, out_sem.at[0])

    @pl.when(first)
    def _():
        loads["dn"].wait()
        down()
        layer_output()
        forth.start()
        start(ex[OUT])
        back.wait_recv()
        dy2[mine, :] = pipe_b[...]
        doc[...] = pipe_b[...].astype(F32)
        start(ex[DOUT])
        arrive(ex[DOUT])
        output_grads()

    for j in BLOCKS:
        grad = (dg[:, j] * slope[:, j]).astype(BF16)
        dh[:, j] = grad
        sm[7:8, j] = jnp.sum(grad.astype(F32), 0, keepdims=True)

    for j in BLOCKS:
        da2s[:, j] = dot_nt(dh[...], wup[j, :]).astype(BF16)

    start(ex[DA2])

    @pl.when(first)
    def _():
        sm[5:6, :] = jnp.sum(dy2[...].astype(F32), 0, keepdims=True)

    for j in BLOCKS:
        wg0[j, :] = dot_tn(g[:, j], dy2[...]).astype(BF16)

    now(0, 0)
    for j in BLOCKS:
        wg1[j, :] = dot_tn(a2[:, j], dh[...]).astype(BF16)

    now(1, 0)
    arrive(ex[DA2])
    grad_u, gain_grad, shift_grad = norm_back(summed(da2s, da2r), x2c[...], gains[1:2, :])
    grad_middle = doc[...] + grad_u
    dy1[mine, :] = grad_middle.astype(BF16)
    start(ex[DY1])
    dx2c[...] = grad_middle
    sm[1:2, :] = gain_grad
    sm[3:4, :] = shift_grad
    sm[4:5, :] = jnp.sum(grad_middle, 0, keepdims=True)
    early(0, 1)
    early(1, 1)
    arrive(ex[DY1])

    att_grad = dot_nt(dy1[...], wo[...]).astype(BF16)
    dqkv[:, 2 * W : 3 * W] = att_grad
    grad_q = grad_k = grad_v = jnp.zeros((PAD, W), F32)
    for h in range(HEADS):
        p = prob[h]
        own = head_rows(dqkv[:, 2 * W : 3 * W], h)
        grad_p = dot_nt(own, qkv[:, 2 * W : 3 * W])
        grad_v = grad_v + dot_tn(p.astype(BF16), own)
        grad_s = p * (grad_p - jnp.sum(grad_p * p, -1, keepdims=True))
        grad_s = grad_s.astype(BF16)
        grad_q = grad_q + dot_nn(grad_s, head_rows(qkv[:, W : 2 * W], h))
        grad_k = grad_k + dot_tn(grad_s, head_rows(qkv[:, 0:W], h))

    scale = 1.0 / math.sqrt(HD)
    for j, (grad, factor) in enumerate(((grad_q, scale), (grad_k, scale), (grad_v, 1.0))):
        low = (grad * factor).astype(BF16)
        dqkv[:, j * W : (j + 1) * W] = low
        if j != 1:
            at = (j // 2) * W
            sm[6:7, at : at + W] = jnp.sum(low.astype(F32), 0, keepdims=True)

    for j in BLOCKS:
        part = dot_nt(dqkv[:, 0:W], wqkv[0, j, :]) + dot_nt(dqkv[:, W : 2 * W], wqkv[1, j, :])
        da1s[:, j] = (part + dot_nt(dqkv[:, 2 * W : 3 * W], wqkv[2, j, :])).astype(BF16)

    start(ex[DA1])
    wg2[...] = dot_tn(att[...], dy1[...]).astype(BF16)
    now(2, 0)
    for j in range(D // W):
        part = dot_tn(a1[:, j * W : (j + 1) * W], dqkv[...]).astype(BF16)
        for i in range(3):
            at = i * D + j * W
            wg3[at : at + W, :] = part[:, i * W : (i + 1) * W]

    now(3, 0)
    early(0, 2)
    early(1, 2)
    arrive(ex[DA1])
    grad_u, gain_grad, shift_grad = norm_back(summed(da1s, da1r), xc[...], gains[0:1, :])
    sm[0:1, :] = gain_grad
    sm[2:3, :] = shift_grad
    low = (dx2c[...] + grad_u).astype(BF16)
    pipe_bs[...] = low
    dxg[mine, :] = low

    @pl.when(second)
    def _():
        back.start()

    start(ex[DX])
    smz[z] = sm[...]
    start(ex[SMALL])

    @pl.when(second)
    def _():
        down()
        layer_output()
        start(ex[OUT])

    if reduce_dp:
        core_copy = sd_copy(0, smc.at[gc], smc.at[gc], core_peer)
        y_copy = sd_copy(1, smy.at[gy], smy.at[gy], y_peer)
        x_copies = [sd_copy(2 + i, smx.at[gx], smx.at[gx], x_peers[i]) for i in range(3)]

    def small0():
        arrive(ex[SMALL])
        whole = smz[0] + smz[1] + smz[2] + smz[3]
        own_rows = lax.broadcasted_iota(jnp.int32, (8, D), 0) >= 5
        whole = jnp.where(own_rows, sm[...], whole)
        if reduce_dp:
            smc[gc] = whole
            core_copy.start()
        else:
            small_out[...] = whole

    def small1():
        core_copy.wait()
        smy[gy] = smc[0] + smc[1]
        y_copy.start()

    def small2():
        y_copy.wait()
        smx[gx] = smy[0] + smy[1]
        start(x_copies)

    def small3():
        for copy in x_copies:
            copy.wait()
        small_out[...] = smx[0] + smx[1] + smx[2] + smx[3]

    dx_copy = pltpu.make_async_copy(dxg.at[pl.ds(0, USED)], dx_out, out_sem.at[1])

    def layer_results():
        arrive(ex[OUT])
        act_copy.start()
        arrive(ex[DX])
        dx_copy.start()

    if reduce_dp:
        early(2, 1)
        early(3, 1)

        @pl.when(second)
        def _():
            for b, s in ((0, 1), (1, 1), (0, 2), (1, 2), (2, 1), (3, 1)):
                steps[b][s]()

        def wave(*items):
            for b, s in items:
                steps[b][s]()

        small0()
        wave((0, 3), (1, 3), (3, 2), (2, 2))
        small1()
        wave((0, 4), (1, 4), (3, 3), (2, 3))
        small2()
        wave((0, 5), (1, 5), (3, 4), (2, 4))
        small3()
        layer_results()
        wave((3, 5), (2, 5), (0, 6), (1, 6), (3, 6), (2, 6))
        wave((0, 7), (1, 7), (3, 7), (2, 7), (0, 8), (1, 8), (3, 8), (2, 8))
    else:
        small0()
        layer_results()

    act_copy.wait()
    dx_copy.wait()
    for k in (Y1, A2, Y2, OUT, DA2, DY1, DA1, DX, SMALL):
        sent(ex[k])

    @pl.when(first)
    def _():
        forth.wait_send()
        sent(ex[DOUT])

    @pl.when(second)
    def _():
        back.wait_send()
        sent(ex[A1])

    if not reduce_dp:
        copies = [
            pltpu.make_async_copy(wg, out, dp_l.at[b, 0])
            for b, (wg, out) in enumerate(zip(wgs, gouts))
        ]
        start(copies)
        for copy in copies:
            copy.wait()


def call(reduce_dp, *operands):
    hbm = pl.BlockSpec(memory_space=pltpu.HBM)
    anywhere = pl.BlockSpec(memory_space=pl.ANY)
    vmem = pl.BlockSpec(memory_space=pltpu.VMEM)
    smem = pl.BlockSpec(memory_space=pltpu.SMEM)

    def low(*shape):
        return pltpu.VMEM(shape, BF16)

    def wide(*shape):
        return pltpu.VMEM(shape, F32)

    scratch = [
        wide(PAD, D), wide(PAD, D), low(3, D, W), low(256, D), low(D, D), low(D, D),
        wide(PAD, PAD), wide(CH, D), low(PAD, D), low(PAD, 768), wide(HEADS, PAD, PAD), low(PAD, W),
        low(PAD, D), low(3, CH, D), wide(CH, D), low(PAD, D), wide(PAD, D), low(PAD, D),
        low(PAD, D), low(3, CH, D), low(PAD, D), wide(CH, D), low(PAD, D), wide(PAD, D), low(PAD, D),
        low(PAD, D), low(3, CH, D), wide(CH, D), low(PAD, D), low(PAD, 768), low(PAD, D),
        low(3, CH, D), low(PAD, D),
        low(CH, D), low(CH, D), low(CH, D), low(CH, D),
        wide(8, D), wide(4, 8, D), wide(2, 8, D), wide(2, 8, D), wide(4, 8, D),
    ]
    scratch += [low(size, width) for size, width, _ in BUCKETS]
    scratch += [low(size // 2, width) for size, width, _ in BUCKETS]
    scratch += [low(size * 7 // 16, width) for size, width, _ in BUCKETS]
    scratch += [
        pltpu.VMEM((SLOTS, ROWS), jnp.int32), wide(2, D), wide(2, D), wide(2, W), wide(2, D), wide(1, D),
    ]
    dma = pltpu.SemaphoreType.DMA
    scratch += [
        dma((12,)), dma((2,)), dma((11, 3)), dma((11, 3)), dma((2,)), dma((2,)),
        dma((4, 22)), dma((4, 22)), dma((4, 3)), dma((5,)), dma((5,)),
    ]
    return pl.pallas_call(
        functools.partial(kernel, reduce_dp),
        out_shape=[
            jax.ShapeDtypeStruct((USED, D), BF16),
            jax.ShapeDtypeStruct((USED, D), BF16),
            *[jax.ShapeDtypeStruct((size, width), BF16) for size, width, _ in BUCKETS],
            jax.ShapeDtypeStruct((8, D), F32),
        ],
        in_specs=[hbm, hbm, smem] + [hbm] * 10,
        out_specs=[anywhere] * 6 + [vmem],
        scratch_shapes=scratch,
        compiler_params=pltpu.CompilerParams(
            collective_id=0, has_side_effects=True, vmem_limit_bytes=60 * 1024 * 1024
        ),
        name="layers",
    )(*operands)


def widen_kernel(*refs):
    small, lows = refs[6], refs[:6]
    outs, (gains, shifts, qv, biases, upb) = refs[7:13], refs[13:]
    for low, out in zip(lows, outs):
        out[...] = low[...].astype(F32)
    gains[...] = small[0:2, :]
    shifts[...] = small[2:4, :]
    biases[...] = small[4:6, :]
    qv[0:1, :] = small[6:7, 0:W]
    qv[1:2, :] = small[6:7, W : 2 * W]
    upb[...] = small[7:8, :]


def widen(lows, small):
    count = 8

    def spec(shape):
        blocks = 5 if shape[0] == USED else count
        return pl.BlockSpec(
            (shape[0] // blocks, shape[1]), lambda i: (jnp.minimum(i, blocks - 1), 0)
        )

    def fixed(shape):
        return pl.BlockSpec(shape, lambda i: (0, 0))

    flat = [(2, D), (2, D), (2, W), (2, D), (1, D)]
    return pl.pallas_call(
        widen_kernel,
        grid=(count,),
        out_shape=[jax.ShapeDtypeStruct(a.shape, F32) for a in lows]
        + [jax.ShapeDtypeStruct(shape, F32) for shape in flat],
        in_specs=[spec(a.shape) for a in lows] + [fixed((8, D))],
        out_specs=[spec(a.shape) for a in lows] + [fixed(shape) for shape in flat],
        compiler_params=pltpu.CompilerParams(vmem_limit_bytes=60 * 1024 * 1024),
        name="widen",
    )(*lows, small)


def local(
    tokens,
    cotangent,
    doc_lengths,
    live_mask,
    norm_gains,
    norm_biases,
    query_key_value,
    query_value_bias,
    output_weight,
    output_biases,
    expand_weight,
    expand_bias,
    reduce_weight,
):
    reduce_dp = lax.axis_size("dp") == 16
    act, dx, gdn, gup, go, gqkv, small = call(
        reduce_dp,
        tokens.reshape(USED, D),
        cotangent.reshape(USED, D),
        doc_lengths,
        live_mask,
        norm_gains[0],
        norm_biases[0],
        query_key_value[0].transpose(1, 0, 2),
        query_value_bias[0],
        output_weight[0],
        output_biases[0],
        expand_weight[0],
        expand_bias,
        reduce_weight[0],
    )
    act, dx, gdn, gup, go, gqkv, gains, shifts, qv, biases, upb = widen(
        (act, dx, gdn, gup, go, gqkv), small
    )
    return (
        act.reshape(1, SLOTS, ROWS, D),
        dx.reshape(1, SLOTS, ROWS, D),
        gains[None],
        shifts[None],
        gqkv.reshape(3, D, W).transpose(1, 0, 2)[None],
        qv[None],
        go[None],
        biases[None],
        gup[None],
        upb,
        gdn[None],
    )


def solution(mesh):
    in_specs = (
        P(None, "dp", None),
        P(None, "dp", None),
        P(None, "dp", None),
        P(None, "dp"),
        P("pipe", None, None),
        P("pipe", None, None),
        P("pipe", None, None, "tensor"),
        P("pipe", None, "tensor"),
        P("pipe", "tensor", None),
        P("pipe", None, None),
        P("pipe", None, "tensor"),
        P("pipe", "tensor"),
        P("pipe", "tensor", None),
    )
    out_specs = (
        P("pipe", None, "dp", None),
        P("pipe", None, "dp", None),
        P("pipe", None, None),
        P("pipe", None, None),
        P("pipe", None, None, "tensor"),
        P("pipe", None, "tensor"),
        P("pipe", "tensor", None),
        P("pipe", None, None),
        P("pipe", None, "tensor"),
        P("pipe", "tensor"),
        P("pipe", "tensor", None),
    )
    return jax.shard_map(local, mesh=mesh, in_specs=in_specs, out_specs=out_specs, check_vma=False)
```

```python
import functools
import math

import jax
import jax.numpy as jnp
from jax import lax
from jax.experimental import pallas as pl
from jax.experimental.pallas import tpu as pltpu
from jax.sharding import PartitionSpec as P

MESH = pl.DeviceIdType.MESH
F32 = jnp.float32
BF16 = jnp.bfloat16
D = 1024
ROWS = 80
SLOTS = 3
USED = ROWS * SLOTS
PAD = 256
TEN = 4
HALF = PAD // 2
CH = HALF // TEN
HALVES = (slice(0, HALF), slice(HALF, PAD))
OWN = (slice(0, CH), slice(CH, 2 * CH))
HEADS = 4
HD = 64
W = 256
BLOCKS = (slice(0, 512), slice(512, 1024))
BUCKETS = (
    (1024, 1024, (256, 128, 128)),
    (1024, 1024, (128, 256, 128)),
    (256, 1024, (0, 0, 128)),
    (3072, 256, (512, 512, 512)),
)
A1, Y1, A2, Y2, OUT, DOUT, DA2, DY1, DA1, DX, SMALL = range(11)


def dot_nn(a, b):
    return lax.dot_general(a, b, (((1,), (0,)), ((), ())), preferred_element_type=F32)


def dot_nt(a, b):
    return lax.dot_general(a, b, (((1,), (1,)), ((), ())), preferred_element_type=F32)


def dot_tn(a, b):
    return lax.dot_general(a, b, (((0,), (0,)), ((), ())), preferred_element_type=F32)


def tile(j, size=W):
    return pl.ds(pl.multiple_of(j * size, size), size)


def normed(u):
    center = u - jnp.mean(u, -1, keepdims=True)
    inverse = lax.rsqrt(jnp.mean(center * center, -1, keepdims=True) + 1e-05)
    return center * inverse, inverse


def norm_back(grad, u, gain):
    unit, inverse = normed(u)
    scaled = grad * gain
    along = jnp.mean(scaled * unit, -1, keepdims=True)
    grad_u = inverse * (scaled - jnp.mean(scaled, -1, keepdims=True) - unit * along)
    return grad_u, jnp.sum(grad * unit, 0, keepdims=True), jnp.sum(grad, 0, keepdims=True)


def kernel(
    reduce_dp,
    tok_hbm, cot_hbm, docs, live_hbm, gains_hbm, shifts_hbm, wqkv_hbm, qvb_hbm, wo_hbm, obias_hbm,
    wup_hbm, upb_hbm, wdn_hbm,
    act_out, dx_out, gdn_out, gup_out, go_out, gqkv_out, small_out,
    tok, cot, wqkv, wo, wup, wdn, mask, xc, a1, qkv, prob, att, y1s, y1r, x2c, a2, slope, g,
    y2s, y2r, actg, doc, dy2, dg, dh, da2s, da2r, dx2c, dy1, dqkv, da1s, da1r, dxg,
    pipe_f, pipe_b, pipe_fs, pipe_bs, kacc, vacc, sm, smz, smc, smy, smx,
    wg0, wg1, wg2, wg3, rc0, rc1, rc2, rc3, in0, in1, in2, in3,
    live, gains, shifts, qvb, obias, upb,
    load_sem, out_sem, tp_s, tp_r, pp_s, pp_r, dp_s, dp_r, dp_l, sd_s, sd_r,
):
    wgs, rcs = (wg0, wg1, wg2, wg3), (rc0, rc1, rc2, rc3)
    ins = (in0, in1, in2, in3)
    gouts = (gdn_out, gup_out, go_out, gqkv_out)
    pipe = lax.axis_index("pipe")
    dp = lax.axis_index("dp")
    z = lax.axis_index("tensor")
    first = pipe == 0
    second = pipe == 1
    gx, gy, gc = dp // 4, (dp // 2) % 2, dp % 2
    core_peer = gx * 4 + gy * 2 + (1 - gc)
    y_peer = gx * 4 + (1 - gy) * 2 + gc
    x_peers = [((gx + t) % 4) * 4 + gy * 2 + gc for t in (1, 2, 3)]
    mine = [pl.ds(pl.multiple_of(h * HALF + z * CH, CH), CH) for h in range(2)]
    cube_bits = (((gx + 1) // 2) % 2, gx // 2, gy)
    cube_peers = (
        (gx + 1 - 2 * (gx % 2)) * 4 + gy * 2 + gc,
        (3 - gx) * 4 + gy * 2 + gc,
        y_peer,
    )

    def load(k, src, dst):
        return pltpu.make_async_copy(src, dst, load_sem.at[k])

    loads = {
        "tok": load(0, tok_hbm, tok.at[pl.ds(0, USED)]),
        "cot": load(1, cot_hbm, cot.at[pl.ds(0, USED)]),
        "qkv": load(2, wqkv_hbm, wqkv),
        "o": load(3, wo_hbm, wo),
        "up": load(4, wup_hbm, wup),
        "dn": load(5, wdn_hbm, wdn),
    }

    small_loads = [
        load(6 + k, src, dst)
        for k, (src, dst) in enumerate((
            (live_hbm, live), (gains_hbm, gains), (shifts_hbm, shifts),
            (qvb_hbm, qvb), (obias_hbm, obias), (upb_hbm, upb),
        ))
    ]
    for copy in small_loads:
        copy.start()

    @pl.when(first)
    def _():
        for name in ("tok", "qkv", "o", "up", "dn"):
            loads[name].start()

    @pl.when(second)
    def _():
        for name in ("cot", "dn", "qkv", "o", "up"):
            loads[name].start()

    barrier = pltpu.get_barrier_semaphore()
    partners = [{"tensor": (z + t) % 4} for t in (1, 2, 3)] + [{"pipe": 1 - pipe}]
    if reduce_dp:
        partners += [{"dp": core_peer}, {"dp": y_peer}] + [{"dp": p} for p in x_peers]
    for partner in partners:
        pl.semaphore_signal(barrier, inc=1, device_id=partner, device_id_type=MESH)

    def places(shape, axis):
        at = lax.broadcasted_iota(jnp.int32, shape, axis)
        slot = (at >= ROWS).astype(jnp.int32) + (at >= 2 * ROWS).astype(jnp.int32)
        slot = slot + (at >= 3 * ROWS).astype(jnp.int32)
        spot = at - ROWS * slot
        segment = 4 * slot
        alive = jnp.zeros(shape, F32)
        for s in range(SLOTS):
            end = jnp.int32(0)
            for k in range(3):
                end = end + docs[s, 0, k]
                segment = segment + jnp.where((slot == s) & (spot >= end), 1, 0)
            alive = jnp.where((slot == s) & (spot.astype(F32) < counts[s : s + 1, :]), 1.0, alive)
        return at, segment, alive

    for copy in small_loads:
        copy.wait()
    counts = jnp.sum(live[...].astype(F32), 1, keepdims=True)
    row_at, row_segment, row_live = places((PAD, 1), 0)
    col_at, col_segment, col_live = places((1, PAD), 1)
    seen = (row_segment == col_segment) & (col_at <= row_at)
    seen = seen & ((col_live + jnp.where(row_at == col_at, 1.0, 0.0)) > 0.5)
    mask[...] = jnp.where(seen, 1.0, 0.0)
    sm[...] = jnp.zeros_like(sm)
    head_of = lax.broadcasted_iota(jnp.int32, (1, W), 1) // HD

    pl.semaphore_wait(barrier, len(partners))

    def tp_copy(k, h, t, src, dst):
        return pltpu.make_async_remote_copy(
            src_ref=src,
            dst_ref=dst,
            send_sem=tp_s.at[2 * k + h, t - 1],
            recv_sem=tp_r.at[2 * k + h, t - 1],
            device_id={"tensor": (z + t) % 4},
            device_id_type=MESH,
        )

    def scatter(k, h, src, dst):
        copies = []
        for t in (2, 1, 3):
            at = pl.multiple_of(h * HALF + ((z + t) % 4) * CH, CH)
            copies.append(tp_copy(k, h, t, src.at[pl.ds(at, CH)], dst.at[h, t - 1]))
        return copies

    def gather(k, h, buf):
        return [tp_copy(k, h, t, buf.at[mine[h]], buf.at[mine[h]]) for t in (2, 1, 3)]

    def start(copies):
        for copy in copies:
            copy.start()

    def arrive(copies):
        for copy in copies:
            copy.wait_recv()

    def sent(copies):
        for copy in copies:
            copy.wait_send()

    ex = {}
    for h in range(2):
        for k, buf in ((A1, a1), (A2, a2), (OUT, actg), (DOUT, dy2), (DY1, dy1), (DX, dxg)):
            ex[k, h] = gather(k, h, buf)
        for k, src, dst in ((Y1, y1s, y1r), (Y2, y2s, y2r), (DA2, da2s, da2r), (DA1, da1s, da1r)):
            ex[k, h] = scatter(k, h, src, dst)
    ex[SMALL, 0] = [tp_copy(SMALL, 0, t, smz.at[z], smz.at[z]) for t in (2, 1, 3)]

    def hand_over(src, dst, k):
        return [
            pltpu.make_async_remote_copy(
                src_ref=src.at[h], dst_ref=dst.at[h], send_sem=pp_s.at[k + h], recv_sem=pp_r.at[k + h],
                device_id={"pipe": 1 - pipe}, device_id_type=MESH,
            )
            for h in range(2)
        ]

    forth = hand_over(pipe_fs, pipe_f, 0)
    back = hand_over(pipe_bs, pipe_b, 2)

    def summed(src, dst, h):
        total = src[mine[h], :].astype(F32)
        for t in range(3):
            total = total + dst[h, t].astype(F32)
        return total

    def dp_copy(b, k, src, dst, peer):
        return pltpu.make_async_remote_copy(
            src_ref=src, dst_ref=dst, send_sem=dp_s.at[b, k], recv_sem=dp_r.at[b, k],
            device_id={"dp": peer}, device_id_type=MESH,
        )

    def rows(at, size):
        return pl.ds(pl.multiple_of(at, 16), size)

    def add_into(dst, at, size, term):
        step = next(n for n in (64, 48, 32, 16) if size % n == 0)

        @pl.loop(0, size // step)
        def _(i):
            off = pl.multiple_of(i * step, 16)
            total = dst[rows(at + off, step), :].astype(F32) + term(off, step).astype(F32)
            dst[rows(at + off, step), :] = total.astype(BF16)

    def bucket(b):
        size, _, parts = BUCKETS[b]
        half = size // 2
        wg, rc, inc, out = wgs[b], rcs[b], ins[b], gouts[b]
        base = gc * half
        whole = rows((1 - gc) * half, half)
        core = dp_copy(b, 0, wg.at[whole], rc, core_peer)
        pieces = []
        for part, count in enumerate(parts):
            if not count:
                continue
            at = sum(parts[:part])
            begin, spare, size = at, at * 7 // 8, count
            down, up = [], []
            for step in range(3):
                link = (part + step) % 3
                bit, peer = cube_bits[link], cube_peers[link]
                size = size // 2
                own = begin + bit * size
                copy = dp_copy(
                    b, 1 + part * 6 + step, rc.at[rows(begin + (1 - bit) * size, size)],
                    inc.at[rows(spare, size)], peer,
                )
                down.append((copy, own, size, spare))
                here = out.at[rows(base + own, size)]
                source = rc.at[rows(own, size)] if step == 2 else here
                up.append(dp_copy(b, 4 + part * 6 + step, source, here, peer))
                begin, spare = own, spare + size
            keep = pltpu.make_async_copy(
                rc.at[rows(begin, size)], out.at[rows(base + begin, size)], dp_l.at[b, part]
            )
            there = out.at[rows(base + at, count)]
            last = dp_copy(b, 19 + part, there, there, core_peer)
            pieces.append((at, count, down, up, keep, last))

        def step0():
            core.start()

        def step1():
            core.wait_recv()
            for at, count, down, up, keep, last in pieces:
                add_into(rc, at, count, lambda o, n, at=at: wg[rows(base + at + o, n), :])
                down[0][0].start()

        def reduce(step):
            def run():
                for at, count, down, up, keep, last in pieces:
                    copy, own, size, spare = down[step]
                    copy.wait_recv()
                    add_into(rc, own, size, lambda o, n, spare=spare: inc[rows(spare + o, n), :])
                    if step < 2:
                        down[step + 1][0].start()
                    else:
                        up[2].start()
                        keep.start()

            return run

        def spread(step):
            def run():
                for at, count, down, up, keep, last in pieces:
                    up[step].wait_recv()
                    if step == 2:
                        keep.wait()
                    if step:
                        up[step - 1].start()
                    else:
                        last.start()

            return run

        def finish():
            core.wait_send()
            for at, count, down, up, keep, last in pieces:
                last.wait_recv()
                for copy in [d[0] for d in down] + up + [last]:
                    copy.wait_send()

        return [step0, step1, reduce(0), reduce(1), reduce(2), spread(2), spread(1), spread(0), finish]

    def sd_copy(k, src, dst, peer):
        return pltpu.make_async_remote_copy(
            src_ref=src, dst_ref=dst, send_sem=sd_s.at[k], recv_sem=sd_r.at[k],
            device_id={"dp": peer}, device_id_type=MESH,
        )

    steps = [bucket(b) for b in range(4)] if reduce_dp else None

    def now(b, s):
        if reduce_dp:
            steps[b][s]()

    def early(b, s):
        if reduce_dp:
            pl.when(first)(steps[b][s])

    def output_grads(h):
        half = HALVES[h]
        for j in BLOCKS:
            dg[half, j] = dot_nt(dy2[half, :], wdn[j, :])

    @pl.when(first)
    def _():
        loads["tok"].wait()
        tok[pl.ds(USED, PAD - USED), :] = jnp.zeros((PAD - USED, D), F32)

    @pl.when(second)
    def _():
        loads["cot"].wait()
        cot[pl.ds(USED, PAD - USED), :] = jnp.zeros((PAD - USED, D), F32)
        masked = cot[...] * row_live
        cot[...] = masked
        dy2[...] = masked.astype(BF16)
        sm[5:6, :] = jnp.sum(masked, 0, keepdims=True)
        loads["dn"].wait()
        for h in range(2):
            doc[OWN[h], :] = cot[mine[h], :]
            output_grads(h)

    def take(h):
        half = HALVES[h]

        @pl.when(first)
        def _():
            unit, _ = normed(tok[half, :])
            a1[half, :] = (unit * gains[0:1, :] + shifts[0:1, :]).astype(BF16)
            xc[OWN[h], :] = tok[mine[h], :]

        @pl.when(second)
        def _():
            forth[h].wait_recv()
            inputs = pipe_f[h].astype(F32)
            xc[OWN[h], :] = inputs
            unit, _ = normed(inputs)
            a1[mine[h], :] = (unit * gains[0:1, :] + shifts[0:1, :]).astype(BF16)
            start(ex[A1, h])
            arrive(ex[A1, h])

    def head_rows(values, n):
        return (values.astype(F32) * jnp.where(head_of == n, 1.0, 0.0)).astype(BF16)

    def attend(h):
        half, keys = HALVES[h], slice(0, (h + 1) * HALF)
        for j in range(3):
            part = dot_nn(a1[half, :], wqkv[j])
            if j != 1:
                part = part + qvb[j // 2 : j // 2 + 1, :]
            qkv[half, j * W : (j + 1) * W] = part.astype(BF16)
        attended = jnp.zeros((HALF, W), F32)
        for n in range(HEADS):
            scores = dot_nt(head_rows(qkv[half, 0:W], n), qkv[keys, W : 2 * W]) * (1.0 / math.sqrt(HD))
            scores = jnp.where(mask[half, keys] > 0.5, scores, -1000000000.0)
            expo = jnp.exp(scores - jnp.max(scores, -1, keepdims=True))
            p = expo / jnp.sum(expo, -1, keepdims=True)
            prob[n, half, keys] = p
            attended = attended + dot_nn(p.astype(BF16), head_rows(qkv[keys, 2 * W : 3 * W], n))
        att[half, :] = attended.astype(BF16)
        if h == 0:
            loads["o"].wait()
        for j in BLOCKS:
            y1s[half, j] = dot_nn(att[half, :], wo[:, j]).astype(BF16)
        start(ex[Y1, h])

    def middle(h):
        arrive(ex[Y1, h])
        value = xc[OWN[h], :] + summed(y1s, y1r, h) + obias[0:1, :]
        x2c[OWN[h], :] = value
        unit, _ = normed(value)
        a2[mine[h], :] = (unit * gains[1:2, :] + shifts[1:2, :]).astype(BF16)
        start(ex[A2, h])

    def feed(h):
        half = HALVES[h]
        arrive(ex[A2, h])
        for j in BLOCKS:
            hidden = dot_nn(a2[half, :], wup[:, j]) + upb[:, j]
            square = hidden * hidden
            root = math.sqrt(2.0 / math.pi)
            bent = jnp.tanh(root * hidden * (1.0 + 0.044715 * square))
            lifted = 0.5 * (1.0 + bent)
            g[half, j] = (hidden * lifted).astype(BF16)
            inner = root * (1.0 + 3.0 * 0.044715 * square)
            slope[half, j] = lifted + 0.5 * hidden * (1.0 - bent * bent) * inner

    def down(h):
        half = HALVES[h]
        for j in BLOCKS:
            y2s[half, j] = dot_nn(g[half, :], wdn[:, j]).astype(BF16)
        start(ex[Y2, h])

    def layer_output(h):
        arrive(ex[Y2, h])
        result = (x2c[OWN[h], :] + summed(y2s, y2r, h) + obias[1:2, :]).astype(BF16)
        pipe_fs[h] = result
        actg[mine[h], :] = result

    take(0)
    loads["qkv"].wait()
    attend(0)
    take(1)
    attend(1)
    middle(0)
    middle(1)
    loads["up"].wait()

    @pl.when(first)
    def _():
        loads["dn"].wait()

    for h in range(2):
        feed(h)
        pl.when(first)(functools.partial(down, h))

    act_copy = pltpu.make_async_copy(actg.at[pl.ds(0, USED)], act_out, out_sem.at[0])

    def feed_back(h):
        half = HALVES[h]
        for j in BLOCKS:
            grad = (dg[half, j] * slope[half, j]).astype(BF16)
            dh[half, j] = grad
            sm[7:8, j] += jnp.sum(grad.astype(F32), 0, keepdims=True)
        for j in BLOCKS:
            da2s[half, j] = dot_nt(dh[half, :], wup[j, :]).astype(BF16)
        start(ex[DA2, h])

    def receive(h):
        back[h].wait_recv()
        dy2[mine[h], :] = pipe_b[h]
        doc[OWN[h], :] = pipe_b[h].astype(F32)
        start(ex[DOUT, h])

    @pl.when(first)
    def _():
        for h in range(2):
            layer_output(h)
            forth[h].start()
            start(ex[OUT, h])
        receive(1)
        arrive(ex[DOUT, 1])
        receive(0)
        output_grads(1)

    feed_back(1)

    @pl.when(first)
    def _():
        arrive(ex[DOUT, 0])
        output_grads(0)

    feed_back(0)

    def down_grad():
        for j in BLOCKS:
            wg0[j, :] = dot_tn(g[:, j], dy2[...]).astype(BF16)
        now(0, 0)

    def up_grad():
        for j in BLOCKS:
            wg1[j, :] = dot_tn(a2[:, j], dh[...]).astype(BF16)
        now(1, 0)

    def attention_grads():
        wg2[...] = dot_tn(att[...], dy1[...]).astype(BF16)
        now(2, 0)
        for j in range(D // W):
            part = dot_tn(a1[:, j * W : (j + 1) * W], dqkv[...]).astype(BF16)
            for i in range(3):
                at = i * D + j * W
                wg3[at : at + W, :] = part[:, i * W : (i + 1) * W]
        now(3, 0)

    def middle_back(h):
        arrive(ex[DA2, h])
        grad_u, gain_grad, shift_grad = norm_back(
            summed(da2s, da2r, h), x2c[OWN[h], :], gains[1:2, :]
        )
        grad_middle = doc[OWN[h], :] + grad_u
        dy1[mine[h], :] = grad_middle.astype(BF16)
        start(ex[DY1, h])
        dx2c[OWN[h], :] = grad_middle
        sm[1:2, :] += gain_grad
        sm[3:4, :] += shift_grad
        sm[4:5, :] += jnp.sum(grad_middle, 0, keepdims=True)

    pl.when(first)(down_grad)
    middle_back(1)
    pl.when(first)(up_grad)
    middle_back(0)
    early(0, 1)
    early(1, 1)

    def attend_back(h):
        half, keys = HALVES[h], slice(0, (h + 1) * HALF)
        count = (h + 1) * HALF
        arrive(ex[DY1, h])
        dqkv[half, 2 * W : 3 * W] = dot_nt(dy1[half, :], wo[...]).astype(BF16)
        grad_q = jnp.zeros((HALF, W), F32)
        grad_k = grad_v = jnp.zeros((count, W), F32)
        for n in range(HEADS):
            p = prob[n, half, keys]
            own = head_rows(dqkv[half, 2 * W : 3 * W], n)
            grad_p = dot_nt(own, qkv[keys, 2 * W : 3 * W])
            grad_v = grad_v + dot_tn(p.astype(BF16), own)
            grad_s = p * (grad_p - jnp.sum(grad_p * p, -1, keepdims=True))
            grad_s = grad_s.astype(BF16)
            grad_q = grad_q + dot_nn(grad_s, head_rows(qkv[keys, W : 2 * W], n))
            grad_k = grad_k + dot_tn(grad_s, head_rows(qkv[half, 0:W], n))
        if h:
            kacc[...] = grad_k[0:HALF]
            vacc[...] = grad_v[0:HALF]
            grad_k, grad_v = grad_k[HALF:], grad_v[HALF:]
        else:
            grad_k, grad_v = grad_k + kacc[...], grad_v + vacc[...]
        scale = 1.0 / math.sqrt(HD)
        for j, (grad, factor) in enumerate(((grad_q, scale), (grad_k, scale), (grad_v, 1.0))):
            low = (grad * factor).astype(BF16)
            dqkv[half, j * W : (j + 1) * W] = low
            if j != 1:
                at = (j // 2) * W
                sm[6:7, at : at + W] += jnp.sum(low.astype(F32), 0, keepdims=True)
        for j in BLOCKS:
            part = dot_nt(dqkv[half, 0:W], wqkv[0, j, :])
            part = part + dot_nt(dqkv[half, W : 2 * W], wqkv[1, j, :])
            part = part + dot_nt(dqkv[half, 2 * W : 3 * W], wqkv[2, j, :])
            da1s[half, j] = part.astype(BF16)
        start(ex[DA1, h])

    def input_grads(h):
        arrive(ex[DA1, h])
        grad_u, gain_grad, shift_grad = norm_back(
            summed(da1s, da1r, h), xc[OWN[h], :], gains[0:1, :]
        )
        low = (dx2c[OWN[h], :] + grad_u).astype(BF16)
        pipe_bs[h] = low
        pl.when(second)(lambda: back[h].start())
        dxg[mine[h], :] = low
        start(ex[DX, h])
        sm[0:1, :] += gain_grad
        sm[2:3, :] += shift_grad

    attend_back(1)
    attend_back(0)
    early(0, 2)
    pl.when(first)(attention_grads)
    early(1, 2)
    input_grads(1)
    input_grads(0)

    @pl.when(first)
    def _():
        sm[5:6, :] = jnp.sum(dy2[...].astype(F32), 0, keepdims=True)

    smz[z] = sm[...]
    start(ex[SMALL, 0])

    @pl.when(second)
    def _():
        for h in range(2):
            down(h)
        down_grad()
        up_grad()
        attention_grads()
        for h in range(2):
            layer_output(h)
            start(ex[OUT, h])

    if reduce_dp:
        core_copy = sd_copy(0, smc.at[gc], smc.at[gc], core_peer)
        y_copy = sd_copy(1, smy.at[gy], smy.at[gy], y_peer)
        x_copies = [sd_copy(2 + i, smx.at[gx], smx.at[gx], x_peers[i]) for i in range(3)]

    def small0():
        arrive(ex[SMALL, 0])
        whole = smz[0] + smz[1] + smz[2] + smz[3]
        own_rows = lax.broadcasted_iota(jnp.int32, (8, D), 0) >= 5
        whole = jnp.where(own_rows, sm[...], whole)
        if reduce_dp:
            smc[gc] = whole
            core_copy.start()
        else:
            small_out[...] = whole

    def small1():
        core_copy.wait()
        smy[gy] = smc[0] + smc[1]
        y_copy.start()

    def small2():
        y_copy.wait()
        smx[gx] = smy[0] + smy[1]
        start(x_copies)

    def small3():
        for copy in x_copies:
            copy.wait()
        small_out[...] = smx[0] + smx[1] + smx[2] + smx[3]

    dx_copy = pltpu.make_async_copy(dxg.at[pl.ds(0, USED)], dx_out, out_sem.at[1])

    def layer_results():
        for h in range(2):
            arrive(ex[OUT, h])
            arrive(ex[DX, h])
        act_copy.start()
        dx_copy.start()

    if reduce_dp:
        early(2, 1)
        early(3, 1)

        @pl.when(second)
        def _():
            for b, s in ((0, 1), (1, 1), (0, 2), (1, 2), (2, 1), (3, 1)):
                steps[b][s]()

        def wave(*items):
            for b, s in items:
                steps[b][s]()

        small0()
        wave((0, 3), (1, 3), (3, 2), (2, 2))
        small1()
        wave((0, 4), (1, 4), (3, 3), (2, 3))
        small2()
        wave((0, 5), (1, 5), (3, 4), (2, 4))
        small3()
        layer_results()
        wave((3, 5), (2, 5), (0, 6), (1, 6), (3, 6), (2, 6))
        wave((0, 7), (1, 7), (3, 7), (2, 7), (0, 8), (1, 8), (3, 8), (2, 8))
    else:
        small0()
        layer_results()

    act_copy.wait()
    dx_copy.wait()
    sent(ex[SMALL, 0])
    for h in range(2):
        for k in (Y1, A2, Y2, OUT, DA2, DY1, DA1, DX):
            sent(ex[k, h])

    @pl.when(first)
    def _():
        for h in range(2):
            forth[h].wait_send()
            sent(ex[DOUT, h])

    @pl.when(second)
    def _():
        for h in range(2):
            back[h].wait_send()
            sent(ex[A1, h])

    if not reduce_dp:
        copies = [
            pltpu.make_async_copy(wg, out, dp_l.at[b, 0])
            for b, (wg, out) in enumerate(zip(wgs, gouts))
        ]
        start(copies)
        for copy in copies:
            copy.wait()


def call(reduce_dp, *operands):
    hbm = pl.BlockSpec(memory_space=pltpu.HBM)
    anywhere = pl.BlockSpec(memory_space=pl.ANY)
    vmem = pl.BlockSpec(memory_space=pltpu.VMEM)
    smem = pl.BlockSpec(memory_space=pltpu.SMEM)

    def low(*shape):
        return pltpu.VMEM(shape, BF16)

    def wide(*shape):
        return pltpu.VMEM(shape, F32)

    scratch = [
        wide(PAD, D), wide(PAD, D), low(3, D, W), low(256, D), low(D, D), low(D, D),
        wide(PAD, PAD), wide(2 * CH, D), low(PAD, D), low(PAD, 768), wide(HEADS, PAD, PAD), low(PAD, W),
        low(PAD, D), low(2, 3, CH, D), wide(2 * CH, D), low(PAD, D), wide(PAD, D), low(PAD, D),
        low(PAD, D), low(2, 3, CH, D), low(PAD, D), wide(2 * CH, D), low(PAD, D), wide(PAD, D), low(PAD, D),
        low(PAD, D), low(2, 3, CH, D), wide(2 * CH, D), low(PAD, D), low(PAD, 768), low(PAD, D),
        low(2, 3, CH, D), low(PAD, D),
        low(2, CH, D), low(2, CH, D), low(2, CH, D), low(2, CH, D), wide(HALF, W), wide(HALF, W),
        wide(8, D), wide(4, 8, D), wide(2, 8, D), wide(2, 8, D), wide(4, 8, D),
    ]
    scratch += [low(size, width) for size, width, _ in BUCKETS]
    scratch += [low(size // 2, width) for size, width, _ in BUCKETS]
    scratch += [low(size * 7 // 16, width) for size, width, _ in BUCKETS]
    scratch += [
        pltpu.VMEM((SLOTS, ROWS), jnp.int32), wide(2, D), wide(2, D), wide(2, W), wide(2, D), wide(1, D),
    ]
    dma = pltpu.SemaphoreType.DMA
    scratch += [
        dma((12,)), dma((2,)), dma((22, 3)), dma((22, 3)), dma((4,)), dma((4,)),
        dma((4, 22)), dma((4, 22)), dma((4, 3)), dma((5,)), dma((5,)),
    ]
    return pl.pallas_call(
        functools.partial(kernel, reduce_dp),
        out_shape=[
            jax.ShapeDtypeStruct((USED, D), BF16),
            jax.ShapeDtypeStruct((USED, D), BF16),
            *[jax.ShapeDtypeStruct((size, width), BF16) for size, width, _ in BUCKETS],
            jax.ShapeDtypeStruct((8, D), F32),
        ],
        in_specs=[hbm, hbm, smem] + [hbm] * 10,
        out_specs=[anywhere] * 6 + [vmem],
        scratch_shapes=scratch,
        compiler_params=pltpu.CompilerParams(
            collective_id=0, has_side_effects=True, vmem_limit_bytes=60 * 1024 * 1024
        ),
        name="layers",
    )(*operands)


def widen_kernel(*refs):
    small, lows = refs[6], refs[:6]
    outs, (gains, shifts, qv, biases, upb) = refs[7:13], refs[13:]
    for low, out in zip(lows, outs):
        out[...] = low[...].astype(F32)
    gains[...] = small[0:2, :]
    shifts[...] = small[2:4, :]
    biases[...] = small[4:6, :]
    qv[0:1, :] = small[6:7, 0:W]
    qv[1:2, :] = small[6:7, W : 2 * W]
    upb[...] = small[7:8, :]


def widen(lows, small):
    count = 8

    def spec(shape):
        blocks = 5 if shape[0] == USED else count
        return pl.BlockSpec(
            (shape[0] // blocks, shape[1]), lambda i: (jnp.minimum(i, blocks - 1), 0)
        )

    def fixed(shape):
        return pl.BlockSpec(shape, lambda i: (0, 0))

    flat = [(2, D), (2, D), (2, W), (2, D), (1, D)]
    return pl.pallas_call(
        widen_kernel,
        grid=(count,),
        out_shape=[jax.ShapeDtypeStruct(a.shape, F32) for a in lows]
        + [jax.ShapeDtypeStruct(shape, F32) for shape in flat],
        in_specs=[spec(a.shape) for a in lows] + [fixed((8, D))],
        out_specs=[spec(a.shape) for a in lows] + [fixed(shape) for shape in flat],
        compiler_params=pltpu.CompilerParams(vmem_limit_bytes=60 * 1024 * 1024),
        name="widen",
    )(*lows, small)


def local(
    tokens,
    cotangent,
    doc_lengths,
    live_mask,
    norm_gains,
    norm_biases,
    query_key_value,
    query_value_bias,
    output_weight,
    output_biases,
    expand_weight,
    expand_bias,
    reduce_weight,
):
    reduce_dp = lax.axis_size("dp") == 16
    act, dx, gdn, gup, go, gqkv, small = call(
        reduce_dp,
        tokens.reshape(USED, D),
        cotangent.reshape(USED, D),
        doc_lengths,
        live_mask,
        norm_gains[0],
        norm_biases[0],
        query_key_value[0].transpose(1, 0, 2),
        query_value_bias[0],
        output_weight[0],
        output_biases[0],
        expand_weight[0],
        expand_bias,
        reduce_weight[0],
    )
    act, dx, gdn, gup, go, gqkv, gains, shifts, qv, biases, upb = widen(
        (act, dx, gdn, gup, go, gqkv), small
    )
    return (
        act.reshape(1, SLOTS, ROWS, D),
        dx.reshape(1, SLOTS, ROWS, D),
        gains[None],
        shifts[None],
        gqkv.reshape(3, D, W).transpose(1, 0, 2)[None],
        qv[None],
        go[None],
        biases[None],
        gup[None],
        upb,
        gdn[None],
    )


def solution(mesh):
    in_specs = (
        P(None, "dp", None),
        P(None, "dp", None),
        P(None, "dp", None),
        P(None, "dp"),
        P("pipe", None, None),
        P("pipe", None, None),
        P("pipe", None, None, "tensor"),
        P("pipe", None, "tensor"),
        P("pipe", "tensor", None),
        P("pipe", None, None),
        P("pipe", None, "tensor"),
        P("pipe", "tensor"),
        P("pipe", "tensor", None),
    )
    out_specs = (
        P("pipe", None, "dp", None),
        P("pipe", None, "dp", None),
        P("pipe", None, None),
        P("pipe", None, None),
        P("pipe", None, None, "tensor"),
        P("pipe", None, "tensor"),
        P("pipe", "tensor", None),
        P("pipe", None, None),
        P("pipe", None, "tensor"),
        P("pipe", "tensor"),
        P("pipe", "tensor", None),
    )
    return jax.shard_map(local, mesh=mesh, in_specs=in_specs, out_specs=out_specs, check_vma=False)
```

```python
import functools
import math

import jax
import jax.numpy as jnp
from jax import lax
from jax.experimental import pallas as pl
from jax.experimental.pallas import tpu as pltpu
from jax.sharding import PartitionSpec as P

MESH = pl.DeviceIdType.MESH
F32 = jnp.float32
BF16 = jnp.bfloat16
D = 1024
ROWS = 80
SLOTS = 3
USED = ROWS * SLOTS
PAD = 256
TEN = 4
HALF = PAD // 2
CH = HALF // TEN
HALVES = (slice(0, HALF), slice(HALF, PAD))
OWN = (slice(0, CH), slice(CH, 2 * CH))
HEADS = 4
HD = 64
W = 256
BLOCKS = (slice(0, 512), slice(512, 1024))
BUCKETS = (
    (1024, 1024, (256, 128, 128)),
    (1024, 1024, (128, 256, 128)),
    (256, 1024, (0, 0, 128)),
    (1536, 256, (256, 256, 256)),
    (1536, 256, (256, 256, 256)),
)
PLACE = (0, 0, 0, 0, 1536)
Y1, A2, Y2, OUT, DA2, DY1, DA1, DX, SMALL = range(9)


def dot_nn(a, b):
    return lax.dot_general(a, b, (((1,), (0,)), ((), ())), preferred_element_type=F32)


def dot_nt(a, b):
    return lax.dot_general(a, b, (((1,), (1,)), ((), ())), preferred_element_type=F32)


def dot_tn(a, b):
    return lax.dot_general(a, b, (((0,), (0,)), ((), ())), preferred_element_type=F32)


def tile(j, size=W):
    return pl.ds(pl.multiple_of(j * size, size), size)


def normed(u):
    center = u - jnp.mean(u, -1, keepdims=True)
    inverse = lax.rsqrt(jnp.mean(center * center, -1, keepdims=True) + 1e-05)
    return center * inverse, inverse


def norm_back(grad, u, gain):
    unit, inverse = normed(u)
    scaled = grad * gain
    along = jnp.mean(scaled * unit, -1, keepdims=True)
    grad_u = inverse * (scaled - jnp.mean(scaled, -1, keepdims=True) - unit * along)
    return grad_u, jnp.sum(grad * unit, 0, keepdims=True), jnp.sum(grad, 0, keepdims=True)


def kernel(
    reduce_dp,
    tok_hbm, cot_hbm, docs, live_hbm, gains_hbm, shifts_hbm, wqkv_hbm, qvb_hbm, wo_hbm, obias_hbm,
    wup_hbm, upb_hbm, wdn_hbm,
    act_out, dx_out, gdn_out, gup_out, go_out, gqkv_out, small_out,
    tok, cot, wqkv, wo, wup, wdn, mask, xc, a1, qkv, prob, att, y1s, y1r, x2c, a2, slope, g,
    y2s, y2r, actg, doc, dy2, dg, dh, da2s, da2r, dx2c, dy1, dqkv, da1s, da1r, dxg,
    pipe_f, pipe_fs, pipe_bs, kacc, vacc, sm, smz, smc, smy, smx,
    wg0, wg1, wg2, wg3, wg4, rc0, rc1, rc2, rc3, rc4, in0, in1, in2, in3, in4,
    live, gains, shifts, qvb, obias, upb,
    load_sem, out_sem, tp_s, tp_r, pp_s, pp_r, dp_s, dp_r, dp_l, sd_s, sd_r,
):
    wgs, rcs = (wg0, wg1, wg2, wg3, wg4), (rc0, rc1, rc2, rc3, rc4)
    ins = (in0, in1, in2, in3, in4)
    gouts = (gdn_out, gup_out, go_out, gqkv_out, gqkv_out)
    pipe = lax.axis_index("pipe")
    dp = lax.axis_index("dp")
    z = lax.axis_index("tensor")
    first = pipe == 0
    second = pipe == 1
    gx, gy, gc = dp // 4, (dp // 2) % 2, dp % 2
    core_peer = gx * 4 + gy * 2 + (1 - gc)
    y_peer = gx * 4 + (1 - gy) * 2 + gc
    x_peers = [((gx + t) % 4) * 4 + gy * 2 + gc for t in (1, 2, 3)]
    mine = [pl.ds(pl.multiple_of(h * HALF + z * CH, CH), CH) for h in range(2)]
    cube_bits = (((gx + 1) // 2) % 2, gx // 2, gy)
    cube_peers = (
        (gx + 1 - 2 * (gx % 2)) * 4 + gy * 2 + gc,
        (3 - gx) * 4 + gy * 2 + gc,
        y_peer,
    )

    def load(k, src, dst):
        return pltpu.make_async_copy(src, dst, load_sem.at[k])

    loads = {
        "tok": load(0, tok_hbm, tok.at[pl.ds(0, USED)]),
        "cot": load(1, cot_hbm, cot.at[pl.ds(0, USED)]),
        "qkv": load(2, wqkv_hbm, wqkv),
        "o": load(3, wo_hbm, wo),
        "up": load(4, wup_hbm, wup),
        "dn": load(5, wdn_hbm, wdn),
    }

    small_loads = [
        load(6 + k, src, dst)
        for k, (src, dst) in enumerate((
            (live_hbm, live), (gains_hbm, gains), (shifts_hbm, shifts),
            (qvb_hbm, qvb), (obias_hbm, obias), (upb_hbm, upb),
        ))
    ]
    for copy in small_loads:
        copy.start()

    @pl.when(first)
    def _():
        for name in ("tok", "qkv", "o", "up", "dn"):
            loads[name].start()

    @pl.when(second)
    def _():
        for name in ("cot", "dn", "qkv", "o", "up"):
            loads[name].start()

    barrier = pltpu.get_barrier_semaphore()
    partners = [{"tensor": (z + t) % 4} for t in (1, 2, 3)]
    partners += [{"pipe": 1 - pipe, "tensor": (z + t) % 4} for t in range(4)]
    if reduce_dp:
        partners += [{"dp": core_peer}, {"dp": y_peer}] + [{"dp": p} for p in x_peers]
    for partner in partners:
        pl.semaphore_signal(barrier, inc=1, device_id=partner, device_id_type=MESH)

    def places(shape, axis):
        at = lax.broadcasted_iota(jnp.int32, shape, axis)
        slot = (at >= ROWS).astype(jnp.int32) + (at >= 2 * ROWS).astype(jnp.int32)
        slot = slot + (at >= 3 * ROWS).astype(jnp.int32)
        spot = at - ROWS * slot
        segment = 4 * slot
        alive = jnp.zeros(shape, F32)
        for s in range(SLOTS):
            end = jnp.int32(0)
            for k in range(3):
                end = end + docs[s, 0, k]
                segment = segment + jnp.where((slot == s) & (spot >= end), 1, 0)
            alive = jnp.where((slot == s) & (spot.astype(F32) < counts[s : s + 1, :]), 1.0, alive)
        return at, segment, alive

    for copy in small_loads:
        copy.wait()
    counts = jnp.sum(live[...].astype(F32), 1, keepdims=True)
    row_at, row_segment, row_live = places((PAD, 1), 0)
    col_at, col_segment, col_live = places((1, PAD), 1)
    seen = (row_segment == col_segment) & (col_at <= row_at)
    seen = seen & ((col_live + jnp.where(row_at == col_at, 1.0, 0.0)) > 0.5)
    mask[...] = jnp.where(seen, 1.0, 0.0)
    sm[...] = jnp.zeros_like(sm)
    head_of = lax.broadcasted_iota(jnp.int32, (1, W), 1) // HD

    def tp_copy(k, h, t, src, dst):
        return pltpu.make_async_remote_copy(
            src_ref=src,
            dst_ref=dst,
            send_sem=tp_s.at[2 * k + h, t - 1],
            recv_sem=tp_r.at[2 * k + h, t - 1],
            device_id={"tensor": (z + t) % 4},
            device_id_type=MESH,
        )

    def scatter(k, h, src, dst):
        copies = []
        for t in (2, 1, 3):
            at = pl.multiple_of(h * HALF + ((z + t) % 4) * CH, CH)
            copies.append(tp_copy(k, h, t, src.at[pl.ds(at, CH)], dst.at[h, t - 1]))
        return copies

    def gather(k, h, buf):
        return [tp_copy(k, h, t, buf.at[mine[h]], buf.at[mine[h]]) for t in (2, 1, 3)]

    def start(copies):
        for copy in copies:
            copy.start()

    def arrive(copies):
        for copy in copies:
            copy.wait_recv()

    def sent(copies):
        for copy in copies:
            copy.wait_send()

    ex = {}
    for h in range(2):
        for k, buf in ((A2, a2), (OUT, actg), (DY1, dy1), (DX, dxg)):
            ex[k, h] = gather(k, h, buf)
        for k, src, dst in ((Y1, y1s, y1r), (Y2, y2s, y2r), (DA2, da2s, da2r), (DA1, da1s, da1r)):
            ex[k, h] = scatter(k, h, src, dst)
    ex[SMALL, 0] = [tp_copy(SMALL, 0, t, smz.at[z], smz.at[z]) for t in (2, 1, 3)]

    def hand_over(src, dst, k, h):
        return [
            pltpu.make_async_remote_copy(
                src_ref=src.at[h], dst_ref=dst.at[mine[h]],
                send_sem=pp_s.at[k + h, t], recv_sem=pp_r.at[k + h, t],
                device_id={"pipe": 1 - pipe, "tensor": (z + t) % 4}, device_id_type=MESH,
            )
            for t in (2, 1, 3, 0)
        ]

    forth = [hand_over(pipe_fs, pipe_f, 0, h) for h in range(2)]
    back = [hand_over(pipe_bs, dy2, 2, h) for h in range(2)]

    def summed(src, dst, h):
        total = src[mine[h], :].astype(F32)
        for t in range(3):
            total = total + dst[h, t].astype(F32)
        return total

    def dp_copy(b, k, src, dst, peer):
        return pltpu.make_async_remote_copy(
            src_ref=src, dst_ref=dst, send_sem=dp_s.at[b, k], recv_sem=dp_r.at[b, k],
            device_id={"dp": peer}, device_id_type=MESH,
        )

    def rows(at, size):
        return pl.ds(pl.multiple_of(at, 16), size)

    def add_into(dst, at, size, term):
        step = next(n for n in (64, 48, 32, 16) if size % n == 0)

        @pl.loop(0, size // step)
        def _(i):
            off = pl.multiple_of(i * step, 16)
            total = dst[rows(at + off, step), :].astype(F32) + term(off, step).astype(F32)
            dst[rows(at + off, step), :] = total.astype(BF16)

    def bucket(b):
        size, _, parts = BUCKETS[b]
        half = size // 2
        wg, rc, inc, out = wgs[b], rcs[b], ins[b], gouts[b]
        base = PLACE[b] + gc * half
        whole = rows((1 - gc) * half, half)
        core = dp_copy(b, 0, wg.at[whole], rc, core_peer)
        pieces = []
        for part, count in enumerate(parts):
            if not count:
                continue
            at = sum(parts[:part])
            begin, spare, size = at, at * 7 // 8, count
            down, up = [], []
            for step in range(3):
                link = (part + step) % 3
                bit, peer = cube_bits[link], cube_peers[link]
                size = size // 2
                own = begin + bit * size
                copy = dp_copy(
                    b, 1 + part * 6 + step, rc.at[rows(begin + (1 - bit) * size, size)],
                    inc.at[rows(spare, size)], peer,
                )
                down.append((copy, own, size, spare))
                here = out.at[rows(base + own, size)]
                source = rc.at[rows(own, size)] if step == 2 else here
                up.append(dp_copy(b, 4 + part * 6 + step, source, here, peer))
                begin, spare = own, spare + size
            keep = pltpu.make_async_copy(
                rc.at[rows(begin, size)], out.at[rows(base + begin, size)], dp_l.at[b, part]
            )
            there = out.at[rows(base + at, count)]
            last = dp_copy(b, 19 + part, there, there, core_peer)
            pieces.append((at, count, down, up, keep, last))

        def step0():
            core.start()

        def step1():
            core.wait_recv()
            for at, count, down, up, keep, last in pieces:
                add_into(rc, at, count, lambda o, n, at=at: wg[rows(gc * half + at + o, n), :])
                down[0][0].start()

        def reduce(step):
            def run():
                for at, count, down, up, keep, last in pieces:
                    copy, own, size, spare = down[step]
                    copy.wait_recv()
                    add_into(rc, own, size, lambda o, n, spare=spare: inc[rows(spare + o, n), :])
                    if step < 2:
                        down[step + 1][0].start()
                    else:
                        up[2].start()
                        keep.start()

            return run

        def spread(step):
            def run():
                for at, count, down, up, keep, last in pieces:
                    up[step].wait_recv()
                    if step == 2:
                        keep.wait()
                    if step:
                        up[step - 1].start()
                    else:
                        last.start()

            return run

        def finish():
            core.wait_send()
            for at, count, down, up, keep, last in pieces:
                last.wait_recv()
                for copy in [d[0] for d in down] + up + [last]:
                    copy.wait_send()

        return [step0, step1, reduce(0), reduce(1), reduce(2), spread(2), spread(1), spread(0), finish]

    def sd_copy(k, src, dst, peer):
        return pltpu.make_async_remote_copy(
            src_ref=src, dst_ref=dst, send_sem=sd_s.at[k], recv_sem=sd_r.at[k],
            device_id={"dp": peer}, device_id_type=MESH,
        )

    steps = [bucket(b) for b in range(5)] if reduce_dp else None

    def now(b, s):
        if reduce_dp:
            steps[b][s]()

    def early(b, s):
        if reduce_dp:
            pl.when(first)(steps[b][s])

    def output_grads(h):
        half = HALVES[h]
        for j in BLOCKS:
            dg[half, j] = dot_nt(dy2[half, :], wdn[j, :])

    @pl.when(first)
    def _():
        loads["tok"].wait()
        tok[pl.ds(USED, PAD - USED), :] = jnp.zeros((PAD - USED, D), F32)

    @pl.when(second)
    def _():
        loads["cot"].wait()
        cot[pl.ds(USED, PAD - USED), :] = jnp.zeros((PAD - USED, D), F32)
        masked = cot[...] * row_live
        cot[...] = masked
        dy2[...] = masked.astype(BF16)
        sm[5:6, :] = jnp.sum(masked, 0, keepdims=True)
        loads["dn"].wait()
        for h in range(2):
            doc[OWN[h], :] = cot[mine[h], :]
            output_grads(h)

    def take(h):
        half = HALVES[h]

        @pl.when(first)
        def _():
            unit, _ = normed(tok[half, :])
            a1[half, :] = (unit * gains[0:1, :] + shifts[0:1, :]).astype(BF16)
            xc[OWN[h], :] = tok[mine[h], :]

        @pl.when(second)
        def _():
            arrive(forth[h])
            unit, _ = normed(pipe_f[half, :].astype(F32))
            a1[half, :] = (unit * gains[0:1, :] + shifts[0:1, :]).astype(BF16)
            xc[OWN[h], :] = pipe_f[mine[h], :].astype(F32)

    def head_rows(values, n):
        return (values.astype(F32) * jnp.where(head_of == n, 1.0, 0.0)).astype(BF16)

    def attend(h):
        half, keys = HALVES[h], slice(0, (h + 1) * HALF)
        for j in range(3):
            part = dot_nn(a1[half, :], wqkv[j])
            if j != 1:
                part = part + qvb[j // 2 : j // 2 + 1, :]
            qkv[half, j * W : (j + 1) * W] = part.astype(BF16)
        attended = jnp.zeros((HALF, W), F32)
        for n in range(HEADS):
            scores = dot_nt(head_rows(qkv[half, 0:W], n), qkv[keys, W : 2 * W]) * (1.0 / math.sqrt(HD))
            scores = jnp.where(mask[half, keys] > 0.5, scores, -1000000000.0)
            expo = jnp.exp(scores - jnp.max(scores, -1, keepdims=True))
            p = expo / jnp.sum(expo, -1, keepdims=True)
            prob[n, half, keys] = p
            attended = attended + dot_nn(p.astype(BF16), head_rows(qkv[keys, 2 * W : 3 * W], n))
        att[half, :] = attended.astype(BF16)
        if h == 0:
            loads["o"].wait()
        for j in BLOCKS:
            y1s[half, j] = dot_nn(att[half, :], wo[:, j]).astype(BF16)
        if h == 0:
            pl.semaphore_wait(barrier, len(partners))
        start(ex[Y1, h])

    def middle(h):
        arrive(ex[Y1, h])
        value = xc[OWN[h], :] + summed(y1s, y1r, h) + obias[0:1, :]
        x2c[OWN[h], :] = value
        unit, _ = normed(value)
        a2[mine[h], :] = (unit * gains[1:2, :] + shifts[1:2, :]).astype(BF16)
        start(ex[A2, h])

    def feed(h):
        half = HALVES[h]
        arrive(ex[A2, h])
        for j in BLOCKS:
            hidden = dot_nn(a2[half, :], wup[:, j]) + upb[:, j]
            square = hidden * hidden
            root = math.sqrt(2.0 / math.pi)
            bent = jnp.tanh(root * hidden * (1.0 + 0.044715 * square))
            lifted = 0.5 * (1.0 + bent)
            g[half, j] = (hidden * lifted).astype(BF16)
            inner = root * (1.0 + 3.0 * 0.044715 * square)
            slope[half, j] = lifted + 0.5 * hidden * (1.0 - bent * bent) * inner

    def down(h):
        half = HALVES[h]
        for j in BLOCKS:
            y2s[half, j] = dot_nn(g[half, :], wdn[:, j]).astype(BF16)
        start(ex[Y2, h])

    def layer_output(h):
        arrive(ex[Y2, h])
        result = (x2c[OWN[h], :] + summed(y2s, y2r, h) + obias[1:2, :]).astype(BF16)
        pipe_fs[h] = result
        actg[mine[h], :] = result

    take(0)
    loads["qkv"].wait()
    attend(0)
    take(1)
    attend(1)
    middle(0)
    middle(1)
    loads["up"].wait()

    @pl.when(first)
    def _():
        loads["dn"].wait()

    for h in range(2):
        feed(h)
        pl.when(first)(functools.partial(down, h))

    act_copy = pltpu.make_async_copy(actg.at[pl.ds(0, USED)], act_out, out_sem.at[0])

    def down_grad():
        for j in BLOCKS:
            wg0[j, :] = dot_tn(g[:, j], dy2[...]).astype(BF16)
        now(0, 0)

    def up_grad():
        for j in BLOCKS:
            wg1[j, :] = dot_tn(a2[:, j], dh[...]).astype(BF16)
        now(1, 0)

    def attention_grads():
        for k in range(6):
            i, j = k // 2, BLOCKS[k % 2]
            part = dot_tn(a1[:, j], dqkv[:, i * W : (i + 1) * W]).astype(BF16)
            wgs[3 + k // 3][k % 3 * 512 : k % 3 * 512 + 512, :] = part
            if k % 3 == 2:
                now(3 + k // 3, 0)
        wg2[...] = dot_tn(att[...], dy1[...]).astype(BF16)
        now(2, 0)

    def feed_back(h):
        half = HALVES[h]
        for j in BLOCKS:
            grad = (dg[half, j] * slope[half, j]).astype(BF16)
            dh[half, j] = grad
            sm[7:8, j] += jnp.sum(grad.astype(F32), 0, keepdims=True)
        for j in BLOCKS:
            da2s[half, j] = dot_nt(dh[half, :], wup[j, :]).astype(BF16)
        start(ex[DA2, h])

    def receive(h):
        arrive(back[h])
        doc[OWN[h], :] = dy2[mine[h], :].astype(F32)

    @pl.when(first)
    def _():
        for h in range(2):
            layer_output(h)
            start(forth[h])
            start(ex[OUT, h])
        receive(1)
        output_grads(1)

    feed_back(1)

    @pl.when(first)
    def _():
        receive(0)
        down_grad()
        output_grads(0)

    feed_back(0)

    def middle_back(h):
        arrive(ex[DA2, h])
        grad_u, gain_grad, shift_grad = norm_back(
            summed(da2s, da2r, h), x2c[OWN[h], :], gains[1:2, :]
        )
        grad_middle = doc[OWN[h], :] + grad_u
        dy1[mine[h], :] = grad_middle.astype(BF16)
        start(ex[DY1, h])
        dx2c[OWN[h], :] = grad_middle
        sm[1:2, :] += gain_grad
        sm[3:4, :] += shift_grad
        sm[4:5, :] += jnp.sum(grad_middle, 0, keepdims=True)

    pl.when(first)(up_grad)
    early(0, 1)
    middle_back(1)
    early(1, 1)
    middle_back(0)

    def attend_back(h):
        half, keys = HALVES[h], slice(0, (h + 1) * HALF)
        count = (h + 1) * HALF
        arrive(ex[DY1, h])
        dqkv[half, 2 * W : 3 * W] = dot_nt(dy1[half, :], wo[...]).astype(BF16)
        grad_q = jnp.zeros((HALF, W), F32)
        grad_k = grad_v = jnp.zeros((count, W), F32)
        for n in range(HEADS):
            p = prob[n, half, keys]
            own = head_rows(dqkv[half, 2 * W : 3 * W], n)
            grad_p = dot_nt(own, qkv[keys, 2 * W : 3 * W])
            grad_v = grad_v + dot_tn(p.astype(BF16), own)
            grad_s = p * (grad_p - jnp.sum(grad_p * p, -1, keepdims=True))
            grad_s = grad_s.astype(BF16)
            grad_q = grad_q + dot_nn(grad_s, head_rows(qkv[keys, W : 2 * W], n))
            grad_k = grad_k + dot_tn(grad_s, head_rows(qkv[half, 0:W], n))
        if h:
            kacc[...] = grad_k[0:HALF]
            vacc[...] = grad_v[0:HALF]
            grad_k, grad_v = grad_k[HALF:], grad_v[HALF:]
        else:
            grad_k, grad_v = grad_k + kacc[...], grad_v + vacc[...]
        scale = 1.0 / math.sqrt(HD)
        for j, (grad, factor) in enumerate(((grad_q, scale), (grad_k, scale), (grad_v, 1.0))):
            low = (grad * factor).astype(BF16)
            dqkv[half, j * W : (j + 1) * W] = low
            if j != 1:
                at = (j // 2) * W
                sm[6:7, at : at + W] += jnp.sum(low.astype(F32), 0, keepdims=True)
        for j in BLOCKS:
            part = dot_nt(dqkv[half, 0:W], wqkv[0, j, :])
            part = part + dot_nt(dqkv[half, W : 2 * W], wqkv[1, j, :])
            part = part + dot_nt(dqkv[half, 2 * W : 3 * W], wqkv[2, j, :])
            da1s[half, j] = part.astype(BF16)
        start(ex[DA1, h])

    def input_grads(h):
        arrive(ex[DA1, h])
        grad_u, gain_grad, shift_grad = norm_back(
            summed(da1s, da1r, h), xc[OWN[h], :], gains[0:1, :]
        )
        low = (dx2c[OWN[h], :] + grad_u).astype(BF16)
        pipe_bs[h] = low
        pl.when(second)(lambda: start(back[h]))
        dxg[mine[h], :] = low
        start(ex[DX, h])
        sm[0:1, :] += gain_grad
        sm[2:3, :] += shift_grad

    attend_back(1)
    early(0, 2)
    attend_back(0)
    early(1, 2)
    pl.when(first)(attention_grads)
    early(0, 3)
    input_grads(1)
    early(3, 1)
    early(4, 1)
    input_grads(0)

    @pl.when(first)
    def _():
        sm[5:6, :] = jnp.sum(dy2[...].astype(F32), 0, keepdims=True)

    smz[z] = sm[...]
    start(ex[SMALL, 0])

    @pl.when(second)
    def _():
        for h in range(2):
            down(h)
        down_grad()
        up_grad()
        attention_grads()
        for h in range(2):
            layer_output(h)
            start(ex[OUT, h])

    if reduce_dp:
        core_copy = sd_copy(0, smc.at[gc], smc.at[gc], core_peer)
        y_copy = sd_copy(1, smy.at[gy], smy.at[gy], y_peer)
        x_copies = [sd_copy(2 + i, smx.at[gx], smx.at[gx], x_peers[i]) for i in range(3)]

    def small0():
        arrive(ex[SMALL, 0])
        whole = smz[0] + smz[1] + smz[2] + smz[3]
        own_rows = lax.broadcasted_iota(jnp.int32, (8, D), 0) >= 5
        whole = jnp.where(own_rows, sm[...], whole)
        if reduce_dp:
            smc[gc] = whole
            core_copy.start()
        else:
            small_out[...] = whole

    def small1():
        core_copy.wait()
        smy[gy] = smc[0] + smc[1]
        y_copy.start()

    def small2():
        y_copy.wait()
        smx[gx] = smy[0] + smy[1]
        start(x_copies)

    def small3():
        for copy in x_copies:
            copy.wait()
        small_out[...] = smx[0] + smx[1] + smx[2] + smx[3]

    dx_copy = pltpu.make_async_copy(dxg.at[pl.ds(0, USED)], dx_out, out_sem.at[1])

    def layer_results():
        for h in range(2):
            arrive(ex[OUT, h])
            arrive(ex[DX, h])
        act_copy.start()
        dx_copy.start()

    if reduce_dp:
        early(1, 3)
        early(0, 4)
        early(2, 1)

        @pl.when(second)
        def _():
            for b, s in (
                (0, 1), (1, 1), (0, 2), (1, 2), (3, 1), (4, 1), (2, 1), (0, 3), (1, 3), (0, 4),
            ):
                steps[b][s]()

        def wave(*items):
            for b, s in items:
                steps[b][s]()

        wave((3, 2), (4, 2), (1, 4), (2, 2), (0, 5))
        small0()
        wave((3, 3), (4, 3), (2, 3), (1, 5), (0, 6))
        small1()
        wave((3, 4), (4, 4), (2, 4), (1, 6))
        small2()
        wave((3, 5), (4, 5), (2, 5), (0, 7))
        small3()
        wave((3, 6), (4, 6), (2, 6), (1, 7))
        layer_results()
        wave((3, 7), (4, 7), (2, 7), (0, 8), (1, 8), (2, 8), (3, 8), (4, 8))
    else:
        small0()
        layer_results()

    act_copy.wait()
    dx_copy.wait()
    sent(ex[SMALL, 0])
    for h in range(2):
        for k in (Y1, A2, Y2, OUT, DA2, DY1, DA1, DX):
            sent(ex[k, h])

    @pl.when(first)
    def _():
        for h in range(2):
            sent(forth[h])

    @pl.when(second)
    def _():
        for h in range(2):
            sent(back[h])

    if not reduce_dp:
        copies = [
            pltpu.make_async_copy(wg, out.at[pl.ds(PLACE[b], BUCKETS[b][0])], dp_l.at[b, 0])
            for b, (wg, out) in enumerate(zip(wgs, gouts))
        ]
        start(copies)
        for copy in copies:
            copy.wait()


def call(reduce_dp, *operands):
    hbm = pl.BlockSpec(memory_space=pltpu.HBM)
    anywhere = pl.BlockSpec(memory_space=pl.ANY)
    vmem = pl.BlockSpec(memory_space=pltpu.VMEM)
    smem = pl.BlockSpec(memory_space=pltpu.SMEM)

    def low(*shape):
        return pltpu.VMEM(shape, BF16)

    def wide(*shape):
        return pltpu.VMEM(shape, F32)

    scratch = [
        wide(PAD, D), wide(PAD, D), low(3, D, W), low(256, D), low(D, D), low(D, D),
        wide(PAD, PAD), wide(2 * CH, D), low(PAD, D), low(PAD, 768), wide(HEADS, PAD, PAD), low(PAD, W),
        low(PAD, D), low(2, 3, CH, D), wide(2 * CH, D), low(PAD, D), wide(PAD, D), low(PAD, D),
        low(PAD, D), low(2, 3, CH, D), low(PAD, D), wide(2 * CH, D), low(PAD, D), wide(PAD, D), low(PAD, D),
        low(PAD, D), low(2, 3, CH, D), wide(2 * CH, D), low(PAD, D), low(PAD, 768), low(PAD, D),
        low(2, 3, CH, D), low(PAD, D),
        low(PAD, D), low(2, CH, D), low(2, CH, D), wide(HALF, W), wide(HALF, W),
        wide(8, D), wide(4, 8, D), wide(2, 8, D), wide(2, 8, D), wide(4, 8, D),
    ]
    scratch += [low(size, width) for size, width, _ in BUCKETS]
    scratch += [low(size // 2, width) for size, width, _ in BUCKETS]
    scratch += [low(size * 7 // 16, width) for size, width, _ in BUCKETS]
    scratch += [
        pltpu.VMEM((SLOTS, ROWS), jnp.int32), wide(2, D), wide(2, D), wide(2, W), wide(2, D), wide(1, D),
    ]
    dma = pltpu.SemaphoreType.DMA
    scratch += [
        dma((12,)), dma((2,)), dma((18, 3)), dma((18, 3)), dma((4, 4)), dma((4, 4)),
        dma((5, 22)), dma((5, 22)), dma((5, 3)), dma((5,)), dma((5,)),
    ]
    return pl.pallas_call(
        functools.partial(kernel, reduce_dp),
        out_shape=[
            jax.ShapeDtypeStruct((USED, D), BF16),
            jax.ShapeDtypeStruct((USED, D), BF16),
            *[jax.ShapeDtypeStruct(shape, BF16) for shape in ((D, D), (D, D), (W, D), (3 * D, W))],
            jax.ShapeDtypeStruct((8, D), F32),
        ],
        in_specs=[hbm, hbm, smem] + [hbm] * 10,
        out_specs=[anywhere] * 6 + [vmem],
        scratch_shapes=scratch,
        compiler_params=pltpu.CompilerParams(
            collective_id=0, has_side_effects=True, vmem_limit_bytes=60 * 1024 * 1024
        ),
        name="layers",
    )(*operands)


def widen_kernel(*refs):
    small, lows = refs[6], refs[:6]
    outs, (gains, shifts, qv, biases, upb) = refs[7:13], refs[13:18]
    narrow, wide, (in_sem, out_sem) = refs[18:24], refs[24:30], refs[30:]
    pieces = []
    for k in (2, 3, 5, 4, 0, 1):
        size = lows[k].shape[0]
        step = ROWS if size == USED else min(size, 128 * D // lows[k].shape[1])
        for at in range(0, size, step):
            part, n = pl.ds(at, step), len(pieces)
            pieces.append((
                pltpu.make_async_copy(lows[k].at[part], narrow[k].at[part], in_sem.at[n]),
                pltpu.make_async_copy(wide[k].at[part], outs[k].at[part], out_sem.at[n]),
                narrow[k].at[part],
                wide[k].at[part],
            ))
    for read, _, _, _ in pieces:
        read.start()
    gains[...] = small[0:2, :]
    shifts[...] = small[2:4, :]
    biases[...] = small[4:6, :]
    qv[0:1, :] = small[6:7, 0:W]
    qv[1:2, :] = small[6:7, W : 2 * W]
    upb[...] = small[7:8, :]
    for read, write, source, target in pieces:
        read.wait()
        target[...] = source[...].astype(F32)
        write.start()
    for _, write, _, _ in pieces:
        write.wait()


def widen(lows, small):
    hbm = pl.BlockSpec(memory_space=pltpu.HBM)
    vmem = pl.BlockSpec(memory_space=pltpu.VMEM)
    flat = [(2, D), (2, D), (2, W), (2, D), (1, D)]
    return pl.pallas_call(
        widen_kernel,
        out_shape=[jax.ShapeDtypeStruct(a.shape, F32) for a in lows]
        + [jax.ShapeDtypeStruct(shape, F32) for shape in flat],
        in_specs=[hbm] * 6 + [vmem],
        out_specs=[hbm] * 6 + [vmem] * 5,
        scratch_shapes=[pltpu.VMEM(a.shape, BF16) for a in lows]
        + [pltpu.VMEM(a.shape, F32) for a in lows]
        + [pltpu.SemaphoreType.DMA((32,)), pltpu.SemaphoreType.DMA((32,))],
        compiler_params=pltpu.CompilerParams(vmem_limit_bytes=60 * 1024 * 1024),
        name="widen",
    )(*lows, small)


def local(
    tokens,
    cotangent,
    doc_lengths,
    live_mask,
    norm_gains,
    norm_biases,
    query_key_value,
    query_value_bias,
    output_weight,
    output_biases,
    expand_weight,
    expand_bias,
    reduce_weight,
):
    reduce_dp = lax.axis_size("dp") == 16
    act, dx, gdn, gup, go, gqkv, small = call(
        reduce_dp,
        tokens.reshape(USED, D),
        cotangent.reshape(USED, D),
        doc_lengths,
        live_mask,
        norm_gains[0],
        norm_biases[0],
        query_key_value[0].transpose(1, 0, 2),
        query_value_bias[0],
        output_weight[0],
        output_biases[0],
        expand_weight[0],
        expand_bias,
        reduce_weight[0],
    )
    act, dx, gdn, gup, go, gqkv, gains, shifts, qv, biases, upb = widen(
        (act, dx, gdn, gup, go, gqkv), small
    )
    return (
        act.reshape(1, SLOTS, ROWS, D),
        dx.reshape(1, SLOTS, ROWS, D),
        gains[None],
        shifts[None],
        gqkv.reshape(3, D, W).transpose(1, 0, 2)[None],
        qv[None],
        go[None],
        biases[None],
        gup[None],
        upb,
        gdn[None],
    )


def solution(mesh):
    in_specs = (
        P(None, "dp", None),
        P(None, "dp", None),
        P(None, "dp", None),
        P(None, "dp"),
        P("pipe", None, None),
        P("pipe", None, None),
        P("pipe", None, None, "tensor"),
        P("pipe", None, "tensor"),
        P("pipe", "tensor", None),
        P("pipe", None, None),
        P("pipe", None, "tensor"),
        P("pipe", "tensor"),
        P("pipe", "tensor", None),
    )
    out_specs = (
        P("pipe", None, "dp", None),
        P("pipe", None, "dp", None),
        P("pipe", None, None),
        P("pipe", None, None),
        P("pipe", None, None, "tensor"),
        P("pipe", None, "tensor"),
        P("pipe", "tensor", None),
        P("pipe", None, None),
        P("pipe", None, "tensor"),
        P("pipe", "tensor"),
        P("pipe", "tensor", None),
    )
    return jax.shard_map(local, mesh=mesh, in_specs=in_specs, out_specs=out_specs, check_vma=False)
```

```python
import functools
import math

import jax
import jax.numpy as jnp
from jax import lax
from jax.experimental import pallas as pl
from jax.experimental.pallas import tpu as pltpu
from jax.sharding import PartitionSpec as P

MESH = pl.DeviceIdType.MESH
F32 = jnp.float32
BF16 = jnp.bfloat16
D = 1024
ROWS = 80
SLOTS = 3
USED = ROWS * SLOTS
PAD = 256
TEN = 4
HALF = PAD // 2
CH = HALF // TEN
HALVES = (slice(0, HALF), slice(HALF, PAD))
OWN = (slice(0, CH), slice(CH, 2 * CH))
HEADS = 4
HD = 64
W = 256
BLOCKS = (slice(0, 512), slice(512, 1024))
BUCKETS = (
    (1024, 1024, (256, 128, 128)),
    (1024, 1024, (128, 256, 128)),
    (256, 1024, (0, 0, 128)),
    (1536, 256, (256, 256, 256)),
    (1536, 256, (256, 256, 256)),
)
PLACE = (0, 0, 0, 0, 1536)
Y1, A2, Y2, OUT, DA2, DY1, DA1, DX, SMALL = range(9)


def dot_nn(a, b):
    return lax.dot_general(a, b, (((1,), (0,)), ((), ())), preferred_element_type=F32)


def dot_nt(a, b):
    return lax.dot_general(a, b, (((1,), (1,)), ((), ())), preferred_element_type=F32)


def dot_tn(a, b):
    return lax.dot_general(a, b, (((0,), (0,)), ((), ())), preferred_element_type=F32)


def tile(j, size=W):
    return pl.ds(pl.multiple_of(j * size, size), size)


def normed(u):
    center = u - jnp.mean(u, -1, keepdims=True)
    inverse = lax.rsqrt(jnp.mean(center * center, -1, keepdims=True) + 1e-05)
    return center * inverse, inverse


def norm_back(grad, u, gain):
    unit, inverse = normed(u)
    scaled = grad * gain
    along = jnp.mean(scaled * unit, -1, keepdims=True)
    grad_u = inverse * (scaled - jnp.mean(scaled, -1, keepdims=True) - unit * along)
    return grad_u, jnp.sum(grad * unit, 0, keepdims=True), jnp.sum(grad, 0, keepdims=True)


def kernel(
    reduce_dp,
    tok_hbm, cot_hbm, docs, live_hbm, gains_hbm, shifts_hbm, wqkv_hbm, qvb_hbm, wo_hbm, obias_hbm,
    wup_hbm, upb_hbm, wdn_hbm,
    act_out, dx_out, gdn_out, gup_out, go_out, gqkv_out, small_out,
    tok, cot, wqkv, wo, wup, wdn, mask, xc, a1, qkv, prob, att, y1s, y1r, x2c, a2, slope, g,
    y2s, y2r, actg, doc, dy2, dg, dh, da2s, da2r, dx2c, dy1, dqkv, da1s, da1r, dxg,
    pipe_f, pipe_fs, pipe_bs, kacc, vacc, smo, sm, smz, smc, smy, smx,
    wg0, wg1, wg2, wg3, wg4, rc0, rc1, rc2, rc3, rc4, in0, in1, in2, in3, in4,
    live, gains, shifts, qvb, obias, upb,
    load_sem, out_sem, tp_s, tp_r, pp_s, pp_r, dp_s, dp_r, dp_l, sd_s, sd_r,
):
    wgs, rcs = (wg0, wg1, wg2, wg3, wg4), (rc0, rc1, rc2, rc3, rc4)
    ins = (in0, in1, in2, in3, in4)
    gouts = (gdn_out, gup_out, go_out, gqkv_out, gqkv_out)
    pipe = lax.axis_index("pipe")
    dp = lax.axis_index("dp")
    z = lax.axis_index("tensor")
    first = pipe == 0
    second = pipe == 1
    gx, gy, gc = dp // 4, (dp // 2) % 2, dp % 2
    core_peer = gx * 4 + gy * 2 + (1 - gc)
    y_peer = gx * 4 + (1 - gy) * 2 + gc
    x_peers = [((gx + t) % 4) * 4 + gy * 2 + gc for t in (1, 2, 3)]
    mine = [pl.ds(pl.multiple_of(h * HALF + z * CH, CH), CH) for h in range(2)]
    cube_bits = (((gx + 1) // 2) % 2, gx // 2, gy)
    cube_peers = (
        (gx + 1 - 2 * (gx % 2)) * 4 + gy * 2 + gc,
        (3 - gx) * 4 + gy * 2 + gc,
        y_peer,
    )

    def load(k, src, dst):
        return pltpu.make_async_copy(src, dst, load_sem.at[k])

    loads = {
        "tok": load(0, tok_hbm, tok.at[pl.ds(0, USED)]),
        "cot": load(1, cot_hbm, cot.at[pl.ds(0, USED)]),
        "qkv": load(2, wqkv_hbm, wqkv),
        "o": load(3, wo_hbm, wo),
        "up": load(4, wup_hbm, wup),
        "dn": load(5, wdn_hbm, wdn),
    }

    small_loads = [
        load(6 + k, src, dst)
        for k, (src, dst) in enumerate((
            (live_hbm, live), (gains_hbm, gains), (shifts_hbm, shifts),
            (qvb_hbm, qvb), (obias_hbm, obias), (upb_hbm, upb),
        ))
    ]
    for copy in small_loads:
        copy.start()

    @pl.when(first)
    def _():
        for name in ("tok", "qkv", "o", "up", "dn"):
            loads[name].start()

    @pl.when(second)
    def _():
        for name in ("cot", "dn", "qkv", "o", "up"):
            loads[name].start()

    barrier = pltpu.get_barrier_semaphore()
    partners = [{"tensor": (z + t) % 4} for t in (1, 2, 3)]
    partners += [{"pipe": 1 - pipe, "tensor": (z + t) % 4} for t in range(4)]
    if reduce_dp:
        partners += [{"dp": core_peer}, {"dp": y_peer}] + [{"dp": p} for p in x_peers]
    for partner in partners:
        pl.semaphore_signal(barrier, inc=1, device_id=partner, device_id_type=MESH)

    def places(shape, axis):
        at = lax.broadcasted_iota(jnp.int32, shape, axis)
        slot = (at >= ROWS).astype(jnp.int32) + (at >= 2 * ROWS).astype(jnp.int32)
        slot = slot + (at >= 3 * ROWS).astype(jnp.int32)
        spot = at - ROWS * slot
        segment = 4 * slot
        alive = jnp.zeros(shape, F32)
        for s in range(SLOTS):
            end = jnp.int32(0)
            for k in range(3):
                end = end + docs[s, 0, k]
                segment = segment + jnp.where((slot == s) & (spot >= end), 1, 0)
            alive = jnp.where((slot == s) & (spot.astype(F32) < counts[s : s + 1, :]), 1.0, alive)
        return at, segment, alive

    for copy in small_loads:
        copy.wait()
    counts = jnp.sum(live[...].astype(F32), 1, keepdims=True)
    row_at, row_segment, row_live = places((PAD, 1), 0)
    col_at, col_segment, col_live = places((1, PAD), 1)
    seen = (row_segment == col_segment) & (col_at <= row_at)
    seen = seen & ((col_live + jnp.where(row_at == col_at, 1.0, 0.0)) > 0.5)
    mask[...] = jnp.where(seen, 1.0, 0.0)
    sm[...] = jnp.zeros_like(sm)
    head_of = lax.broadcasted_iota(jnp.int32, (1, W), 1) // HD

    def tp_copy(k, h, t, src, dst):
        return pltpu.make_async_remote_copy(
            src_ref=src,
            dst_ref=dst,
            send_sem=tp_s.at[2 * k + h, t - 1],
            recv_sem=tp_r.at[2 * k + h, t - 1],
            device_id={"tensor": (z + t) % 4},
            device_id_type=MESH,
        )

    def scatter(k, h, src, dst):
        copies = []
        for t in (2, 1, 3):
            at = pl.multiple_of(h * HALF + ((z + t) % 4) * CH, CH)
            copies.append(tp_copy(k, h, t, src.at[pl.ds(at, CH)], dst.at[h, t - 1]))
        return copies

    def gather(k, h, buf):
        return [tp_copy(k, h, t, buf.at[mine[h]], buf.at[mine[h]]) for t in (2, 1, 3)]

    def start(copies):
        for copy in copies:
            copy.start()

    def arrive(copies):
        for copy in copies:
            copy.wait_recv()

    def sent(copies):
        for copy in copies:
            copy.wait_send()

    ex = {}
    for h in range(2):
        for k, buf in ((A2, a2), (OUT, actg), (DY1, dy1), (DX, dxg)):
            ex[k, h] = gather(k, h, buf)
        for k, src, dst in ((Y1, y1s, y1r), (Y2, y2s, y2r), (DA2, da2s, da2r), (DA1, da1s, da1r)):
            ex[k, h] = scatter(k, h, src, dst)
    ex[SMALL, 0] = [tp_copy(SMALL, 0, t, smz.at[z], smz.at[z]) for t in (2, 1, 3)]

    def hand_over(src, dst, k, h):
        return [
            pltpu.make_async_remote_copy(
                src_ref=src.at[h], dst_ref=dst.at[mine[h]],
                send_sem=pp_s.at[k + h, t], recv_sem=pp_r.at[k + h, t],
                device_id={"pipe": 1 - pipe, "tensor": (z + t) % 4}, device_id_type=MESH,
            )
            for t in (2, 1, 3, 0)
        ]

    forth = [hand_over(pipe_fs, pipe_f, 0, h) for h in range(2)]
    back = [hand_over(pipe_bs, dy2, 2, h) for h in range(2)]

    def summed(src, dst, h):
        total = src[mine[h], :].astype(F32)
        for t in range(3):
            total = total + dst[h, t].astype(F32)
        return total

    def dp_copy(b, k, src, dst, peer):
        return pltpu.make_async_remote_copy(
            src_ref=src, dst_ref=dst, send_sem=dp_s.at[b, k], recv_sem=dp_r.at[b, k],
            device_id={"dp": peer}, device_id_type=MESH,
        )

    def rows(at, size):
        return pl.ds(pl.multiple_of(at, 16), size)

    def add_into(dst, at, size, term):
        step = next(n for n in (64, 48, 32, 16) if size % n == 0)

        @pl.loop(0, size // step)
        def _(i):
            off = pl.multiple_of(i * step, 16)
            total = dst[rows(at + off, step), :].astype(F32) + term(off, step).astype(F32)
            dst[rows(at + off, step), :] = total.astype(BF16)

    def bucket(b):
        size, _, parts = BUCKETS[b]
        half = size // 2
        wg, rc, inc, out = wgs[b], rcs[b], ins[b], gouts[b]
        base = PLACE[b] + gc * half
        whole = rows((1 - gc) * half, half)
        core = dp_copy(b, 0, wg.at[whole], rc, core_peer)
        pieces = []
        for part, count in enumerate(parts):
            if not count:
                continue
            at = sum(parts[:part])
            begin, spare, size = at, at * 7 // 8, count
            down, up = [], []
            for step in range(3):
                link = (part + step) % 3
                bit, peer = cube_bits[link], cube_peers[link]
                size = size // 2
                own = begin + bit * size
                copy = dp_copy(
                    b, 1 + part * 6 + step, rc.at[rows(begin + (1 - bit) * size, size)],
                    inc.at[rows(spare, size)], peer,
                )
                down.append((copy, own, size, spare))
                here = out.at[rows(base + own, size)]
                source = rc.at[rows(own, size)] if step == 2 else here
                up.append(dp_copy(b, 4 + part * 6 + step, source, here, peer))
                begin, spare = own, spare + size
            keep = pltpu.make_async_copy(
                rc.at[rows(begin, size)], out.at[rows(base + begin, size)], dp_l.at[b, part]
            )
            there = out.at[rows(base + at, count)]
            last = dp_copy(b, 19 + part, there, there, core_peer)
            pieces.append((at, count, down, up, keep, last))

        def step0():
            core.start()

        def step1():
            core.wait_recv()
            for at, count, down, up, keep, last in pieces:
                add_into(rc, at, count, lambda o, n, at=at: wg[rows(gc * half + at + o, n), :])
                down[0][0].start()

        def reduce(step):
            def run():
                for at, count, down, up, keep, last in pieces:
                    copy, own, size, spare = down[step]
                    copy.wait_recv()
                    add_into(rc, own, size, lambda o, n, spare=spare: inc[rows(spare + o, n), :])
                    if step < 2:
                        down[step + 1][0].start()
                    else:
                        up[2].start()
                        keep.start()

            return run

        def spread(step):
            def run():
                for at, count, down, up, keep, last in pieces:
                    up[step].wait_recv()
                    if step == 2:
                        keep.wait()
                    if step:
                        up[step - 1].start()
                    else:
                        last.start()

            return run

        def finish():
            core.wait_send()
            for at, count, down, up, keep, last in pieces:
                last.wait_recv()
                for copy in [d[0] for d in down] + up + [last]:
                    copy.wait_send()

        return [step0, step1, reduce(0), reduce(1), reduce(2), spread(2), spread(1), spread(0), finish]

    def sd_copy(k, src, dst, peer):
        return pltpu.make_async_remote_copy(
            src_ref=src, dst_ref=dst, send_sem=sd_s.at[k], recv_sem=sd_r.at[k],
            device_id={"dp": peer}, device_id_type=MESH,
        )

    steps = [bucket(b) for b in range(5)] if reduce_dp else None

    def now(b, s):
        if reduce_dp:
            steps[b][s]()

    def early(b, s):
        if reduce_dp:
            pl.when(first)(steps[b][s])

    def output_grads(h):
        half = HALVES[h]
        for j in BLOCKS:
            dg[half, j] = dot_nt(dy2[half, :], wdn[j, :])

    @pl.when(first)
    def _():
        loads["tok"].wait()
        tok[pl.ds(USED, PAD - USED), :] = jnp.zeros((PAD - USED, D), F32)

    @pl.when(second)
    def _():
        loads["cot"].wait()
        cot[pl.ds(USED, PAD - USED), :] = jnp.zeros((PAD - USED, D), F32)
        masked = cot[...] * row_live
        cot[...] = masked
        dy2[...] = masked.astype(BF16)
        sm[5:6, :] = jnp.sum(masked, 0, keepdims=True)
        loads["dn"].wait()
        for h in range(2):
            doc[OWN[h], :] = cot[mine[h], :]
            output_grads(h)

    def take(h):
        half = HALVES[h]

        @pl.when(first)
        def _():
            unit, _ = normed(tok[half, :])
            a1[half, :] = (unit * gains[0:1, :] + shifts[0:1, :]).astype(BF16)
            xc[OWN[h], :] = tok[mine[h], :]

        @pl.when(second)
        def _():
            arrive(forth[h])
            unit, _ = normed(pipe_f[half, :].astype(F32))
            a1[half, :] = (unit * gains[0:1, :] + shifts[0:1, :]).astype(BF16)
            xc[OWN[h], :] = pipe_f[mine[h], :].astype(F32)

    def head_rows(values, n):
        return (values.astype(F32) * jnp.where(head_of == n, 1.0, 0.0)).astype(BF16)

    def attend(h):
        half, keys = HALVES[h], slice(0, (h + 1) * HALF)
        for j in range(3):
            part = dot_nn(a1[half, :], wqkv[j])
            if j != 1:
                part = part + qvb[j // 2 : j // 2 + 1, :]
            qkv[half, j * W : (j + 1) * W] = part.astype(BF16)
        attended = jnp.zeros((HALF, W), F32)
        for n in range(HEADS):
            scores = dot_nt(head_rows(qkv[half, 0:W], n), qkv[keys, W : 2 * W]) * (1.0 / math.sqrt(HD))
            scores = jnp.where(mask[half, keys] > 0.5, scores, -1000000000.0)
            expo = jnp.exp(scores - jnp.max(scores, -1, keepdims=True))
            p = expo / jnp.sum(expo, -1, keepdims=True)
            prob[n, half, keys] = p
            attended = attended + dot_nn(p.astype(BF16), head_rows(qkv[keys, 2 * W : 3 * W], n))
        att[half, :] = attended.astype(BF16)
        if h == 0:
            loads["o"].wait()
        for j in BLOCKS:
            y1s[half, j] = dot_nn(att[half, :], wo[:, j]).astype(BF16)
        if h == 0:
            pl.semaphore_wait(barrier, len(partners))
        start(ex[Y1, h])

    def middle(h):
        arrive(ex[Y1, h])
        value = xc[OWN[h], :] + summed(y1s, y1r, h) + obias[0:1, :]
        x2c[OWN[h], :] = value
        unit, _ = normed(value)
        a2[mine[h], :] = (unit * gains[1:2, :] + shifts[1:2, :]).astype(BF16)
        start(ex[A2, h])

    def feed(h):
        half = HALVES[h]
        arrive(ex[A2, h])
        for j in BLOCKS:
            hidden = dot_nn(a2[half, :], wup[:, j]) + upb[:, j]
            square = hidden * hidden
            root = math.sqrt(2.0 / math.pi)
            bent = jnp.tanh(root * hidden * (1.0 + 0.044715 * square))
            lifted = 0.5 * (1.0 + bent)
            g[half, j] = (hidden * lifted).astype(BF16)
            inner = root * (1.0 + 3.0 * 0.044715 * square)
            slope[half, j] = lifted + 0.5 * hidden * (1.0 - bent * bent) * inner

    def down(h):
        half = HALVES[h]
        for j in BLOCKS:
            y2s[half, j] = dot_nn(g[half, :], wdn[:, j]).astype(BF16)
        start(ex[Y2, h])

    def layer_output(h):
        arrive(ex[Y2, h])
        result = (x2c[OWN[h], :] + summed(y2s, y2r, h) + obias[1:2, :]).astype(BF16)
        pipe_fs[h] = result
        actg[mine[h], :] = result

    take(0)
    loads["qkv"].wait()
    attend(0)
    take(1)
    attend(1)
    middle(0)
    middle(1)
    loads["up"].wait()

    @pl.when(first)
    def _():
        loads["dn"].wait()

    for h in range(2):
        feed(h)
        pl.when(first)(functools.partial(down, h))

    act_copy = pltpu.make_async_copy(actg.at[pl.ds(0, USED)], act_out, out_sem.at[0])

    def down_grad():
        for j in BLOCKS:
            wg0[j, :] = dot_tn(g[:, j], dy2[...]).astype(BF16)
        now(0, 0)

    def up_grad():
        for j in BLOCKS:
            wg1[j, :] = dot_tn(a2[:, j], dh[...]).astype(BF16)
        now(1, 0)

    def attention_grads():
        for k in range(6):
            i, j = k // 2, BLOCKS[k % 2]
            part = dot_tn(a1[:, j], dqkv[:, i * W : (i + 1) * W]).astype(BF16)
            wgs[3 + k // 3][k % 3 * 512 : k % 3 * 512 + 512, :] = part
            if k % 3 == 2:
                now(3 + k // 3, 0)
        wg2[...] = dot_tn(att[...], dy1[...]).astype(BF16)
        now(2, 0)

    def feed_back(h):
        half = HALVES[h]
        for j in BLOCKS:
            grad = (dg[half, j] * slope[half, j]).astype(BF16)
            dh[half, j] = grad
            sm[7:8, j] += jnp.sum(grad.astype(F32), 0, keepdims=True)
        for j in BLOCKS:
            da2s[half, j] = dot_nt(dh[half, :], wup[j, :]).astype(BF16)
        start(ex[DA2, h])

    def receive(h):
        arrive(back[h])
        doc[OWN[h], :] = dy2[mine[h], :].astype(F32)

    @pl.when(first)
    def _():
        for h in range(2):
            layer_output(h)
            start(forth[h])
            start(ex[OUT, h])
        receive(1)
        output_grads(1)

    feed_back(1)

    @pl.when(first)
    def _():
        receive(0)
        down_grad()
        output_grads(0)

    feed_back(0)

    def middle_back(h):
        arrive(ex[DA2, h])
        grad_u, gain_grad, shift_grad = norm_back(
            summed(da2s, da2r, h), x2c[OWN[h], :], gains[1:2, :]
        )
        grad_middle = doc[OWN[h], :] + grad_u
        dy1[mine[h], :] = grad_middle.astype(BF16)
        start(ex[DY1, h])
        dx2c[OWN[h], :] = grad_middle
        sm[1:2, :] += gain_grad
        sm[3:4, :] += shift_grad
        sm[4:5, :] += jnp.sum(grad_middle, 0, keepdims=True)

    pl.when(first)(up_grad)
    early(0, 1)
    middle_back(1)
    middle_back(0)
    early(1, 1)

    def attend_back(h):
        half, keys = HALVES[h], slice(0, (h + 1) * HALF)
        count = (h + 1) * HALF
        arrive(ex[DY1, h])
        dqkv[half, 2 * W : 3 * W] = dot_nt(dy1[half, :], wo[...]).astype(BF16)
        grad_q = jnp.zeros((HALF, W), F32)
        grad_k = grad_v = jnp.zeros((count, W), F32)
        for n in range(HEADS):
            p = prob[n, half, keys]
            own = head_rows(dqkv[half, 2 * W : 3 * W], n)
            grad_p = dot_nt(own, qkv[keys, 2 * W : 3 * W])
            grad_v = grad_v + dot_tn(p.astype(BF16), own)
            grad_s = p * (grad_p - jnp.sum(grad_p * p, -1, keepdims=True))
            grad_s = grad_s.astype(BF16)
            grad_q = grad_q + dot_nn(grad_s, head_rows(qkv[keys, W : 2 * W], n))
            grad_k = grad_k + dot_tn(grad_s, head_rows(qkv[half, 0:W], n))
        if h:
            kacc[...] = grad_k[0:HALF]
            vacc[...] = grad_v[0:HALF]
            grad_k, grad_v = grad_k[HALF:], grad_v[HALF:]
        else:
            grad_k, grad_v = grad_k + kacc[...], grad_v + vacc[...]
        scale = 1.0 / math.sqrt(HD)
        for j, (grad, factor) in enumerate(((grad_q, scale), (grad_k, scale), (grad_v, 1.0))):
            low = (grad * factor).astype(BF16)
            dqkv[half, j * W : (j + 1) * W] = low
            if j != 1:
                at = (j // 2) * W
                sm[6:7, at : at + W] += jnp.sum(low.astype(F32), 0, keepdims=True)
        for j in BLOCKS:
            part = dot_nt(dqkv[half, 0:W], wqkv[0, j, :])
            part = part + dot_nt(dqkv[half, W : 2 * W], wqkv[1, j, :])
            part = part + dot_nt(dqkv[half, 2 * W : 3 * W], wqkv[2, j, :])
            da1s[half, j] = part.astype(BF16)
        start(ex[DA1, h])

    def input_grads(h):
        arrive(ex[DA1, h])
        grad_u, gain_grad, shift_grad = norm_back(
            summed(da1s, da1r, h), xc[OWN[h], :], gains[0:1, :]
        )
        low = (dx2c[OWN[h], :] + grad_u).astype(BF16)
        pipe_bs[h] = low
        pl.when(second)(lambda: start(back[h]))
        dxg[mine[h], :] = low
        start(ex[DX, h])
        sm[0:1, :] += gain_grad
        sm[2:3, :] += shift_grad

    attend_back(1)
    early(0, 2)
    attend_back(0)
    early(1, 2)
    pl.when(first)(attention_grads)
    early(0, 3)
    input_grads(1)
    early(3, 1)
    early(4, 1)
    input_grads(0)

    @pl.when(first)
    def _():
        sm[5:6, :] = jnp.sum(dy2[...].astype(F32), 0, keepdims=True)

    smz[z] = sm[...]
    start(ex[SMALL, 0])

    @pl.when(second)
    def _():
        for h in range(2):
            down(h)
        down_grad()
        up_grad()
        attention_grads()
        for h in range(2):
            layer_output(h)
            start(ex[OUT, h])

    if reduce_dp:
        core_copy = sd_copy(0, smc.at[gc], smc.at[gc], core_peer)
        y_copy = sd_copy(1, smy.at[gy], smy.at[gy], y_peer)
        x_copies = [sd_copy(2 + i, smx.at[gx], smx.at[gx], x_peers[i]) for i in range(3)]

    small_copy = pltpu.make_async_copy(smo, small_out, out_sem.at[2])

    def small0():
        arrive(ex[SMALL, 0])
        whole = smz[0] + smz[1] + smz[2] + smz[3]
        own_rows = lax.broadcasted_iota(jnp.int32, (8, D), 0) >= 5
        whole = jnp.where(own_rows, sm[...], whole)
        if reduce_dp:
            smc[gc] = whole
            core_copy.start()
        else:
            smo[...] = whole
            small_copy.start()

    def small1():
        core_copy.wait()
        smy[gy] = smc[0] + smc[1]
        y_copy.start()

    def small2():
        y_copy.wait()
        smx[gx] = smy[0] + smy[1]
        start(x_copies)

    def small3():
        for copy in x_copies:
            copy.wait()
        smo[...] = smx[0] + smx[1] + smx[2] + smx[3]
        small_copy.start()

    dx_copy = pltpu.make_async_copy(dxg.at[pl.ds(0, USED)], dx_out, out_sem.at[1])

    def layer_results():
        for h in range(2):
            arrive(ex[OUT, h])
            arrive(ex[DX, h])
        act_copy.start()
        dx_copy.start()

    if reduce_dp:
        early(1, 3)
        early(0, 4)
        early(2, 1)

        @pl.when(second)
        def _():
            for b, s in (
                (0, 1), (1, 1), (0, 2), (1, 2), (3, 1), (4, 1), (2, 1), (0, 3), (1, 3), (0, 4),
            ):
                steps[b][s]()

        def wave(*items):
            for b, s in items:
                steps[b][s]()

        wave((3, 2), (4, 2), (1, 4), (2, 2), (0, 5))
        small0()
        wave((3, 3), (4, 3), (2, 3), (1, 5), (0, 6))
        small1()
        wave((3, 4), (4, 4), (2, 4), (1, 6))
        small2()
        wave((3, 5), (4, 5), (2, 5), (0, 7))
        small3()
        wave((3, 6), (4, 6), (2, 6), (1, 7))
        layer_results()
        wave((3, 7), (4, 7), (2, 7), (0, 8), (1, 8), (2, 8), (3, 8), (4, 8))
    else:
        small0()
        layer_results()

    act_copy.wait()
    dx_copy.wait()
    small_copy.wait()
    sent(ex[SMALL, 0])
    for h in range(2):
        for k in (Y1, A2, Y2, OUT, DA2, DY1, DA1, DX):
            sent(ex[k, h])

    @pl.when(first)
    def _():
        for h in range(2):
            sent(forth[h])

    @pl.when(second)
    def _():
        for h in range(2):
            sent(back[h])

    if not reduce_dp:
        copies = [
            pltpu.make_async_copy(wg, out.at[pl.ds(PLACE[b], BUCKETS[b][0])], dp_l.at[b, 0])
            for b, (wg, out) in enumerate(zip(wgs, gouts))
        ]
        start(copies)
        for copy in copies:
            copy.wait()


def call(reduce_dp, *operands):
    hbm = pl.BlockSpec(memory_space=pltpu.HBM)
    anywhere = pl.BlockSpec(memory_space=pl.ANY)
    smem = pl.BlockSpec(memory_space=pltpu.SMEM)

    def low(*shape):
        return pltpu.VMEM(shape, BF16)

    def wide(*shape):
        return pltpu.VMEM(shape, F32)

    scratch = [
        wide(PAD, D), wide(PAD, D), low(3, D, W), low(256, D), low(D, D), low(D, D),
        wide(PAD, PAD), wide(2 * CH, D), low(PAD, D), low(PAD, 768), wide(HEADS, PAD, PAD), low(PAD, W),
        low(PAD, D), low(2, 3, CH, D), wide(2 * CH, D), low(PAD, D), wide(PAD, D), low(PAD, D),
        low(PAD, D), low(2, 3, CH, D), low(PAD, D), wide(2 * CH, D), low(PAD, D), wide(PAD, D), low(PAD, D),
        low(PAD, D), low(2, 3, CH, D), wide(2 * CH, D), low(PAD, D), low(PAD, 768), low(PAD, D),
        low(2, 3, CH, D), low(PAD, D),
        low(PAD, D), low(2, CH, D), low(2, CH, D), wide(HALF, W), wide(HALF, W),
        wide(8, D),
        wide(8, D), wide(4, 8, D), wide(2, 8, D), wide(2, 8, D), wide(4, 8, D),
    ]
    scratch += [low(size, width) for size, width, _ in BUCKETS]
    scratch += [low(size // 2, width) for size, width, _ in BUCKETS]
    scratch += [low(size * 7 // 16, width) for size, width, _ in BUCKETS]
    scratch += [
        pltpu.VMEM((SLOTS, ROWS), jnp.int32), wide(2, D), wide(2, D), wide(2, W), wide(2, D), wide(1, D),
    ]
    dma = pltpu.SemaphoreType.DMA
    scratch += [
        dma((12,)), dma((3,)), dma((18, 3)), dma((18, 3)), dma((4, 4)), dma((4, 4)),
        dma((5, 22)), dma((5, 22)), dma((5, 3)), dma((5,)), dma((5,)),
    ]
    return pl.pallas_call(
        functools.partial(kernel, reduce_dp),
        out_shape=[
            jax.ShapeDtypeStruct((USED, D), BF16),
            jax.ShapeDtypeStruct((USED, D), BF16),
            *[jax.ShapeDtypeStruct(shape, BF16) for shape in ((D, D), (D, D), (W, D), (3 * D, W))],
            jax.ShapeDtypeStruct((8, D), F32),
        ],
        in_specs=[hbm, hbm, smem] + [hbm] * 10,
        out_specs=[anywhere] * 7,
        scratch_shapes=scratch,
        compiler_params=pltpu.CompilerParams(
            collective_id=0, has_side_effects=True, vmem_limit_bytes=60 * 1024 * 1024
        ),
        name="layers",
    )(*operands)


def widen_kernel(*refs):
    small_in, lows = refs[6], refs[:6]
    outs, flat = refs[7:13], refs[13:18]
    narrow, wide = refs[18:24], refs[24:30]
    small, (gains, shifts, qv, biases, upb), (in_sem, out_sem) = refs[30], refs[31:36], refs[36:]
    first = pltpu.make_async_copy(small_in, small, in_sem.at[32])
    first.start()
    pieces = []
    for k in (2, 3, 5, 4, 0, 1):
        size = lows[k].shape[0]
        step = ROWS if size == USED else min(size, 128 * D // lows[k].shape[1])
        for at in range(0, size, step):
            part, n = pl.ds(at, step), len(pieces)
            pieces.append((
                pltpu.make_async_copy(lows[k].at[part], narrow[k].at[part], in_sem.at[n]),
                pltpu.make_async_copy(wide[k].at[part], outs[k].at[part], out_sem.at[n]),
                narrow[k].at[part],
                wide[k].at[part],
            ))
    for read, _, _, _ in pieces:
        read.start()
    first.wait()
    gains[...] = small[0:2, :]
    shifts[...] = small[2:4, :]
    biases[...] = small[4:6, :]
    qv[0:1, :] = small[6:7, 0:W]
    qv[1:2, :] = small[6:7, W : 2 * W]
    upb[...] = small[7:8, :]
    last = [
        pltpu.make_async_copy(source, out, out_sem.at[32 + n])
        for n, (source, out) in enumerate(zip((gains, shifts, qv, biases, upb), flat))
    ]
    for copy in last:
        copy.start()
    for read, write, source, target in pieces:
        read.wait()
        target[...] = source[...].astype(F32)
        write.start()
    for _, write, _, _ in pieces:
        write.wait()
    for copy in last:
        copy.wait()


def widen(lows, small):
    hbm = pl.BlockSpec(memory_space=pltpu.HBM)
    flat = [(2, D), (2, D), (2, W), (2, D), (1, D)]
    return pl.pallas_call(
        widen_kernel,
        out_shape=[jax.ShapeDtypeStruct(a.shape, F32) for a in lows]
        + [jax.ShapeDtypeStruct(shape, F32) for shape in flat],
        in_specs=[hbm] * 7,
        out_specs=[hbm] * 11,
        scratch_shapes=[pltpu.VMEM(a.shape, BF16) for a in lows]
        + [pltpu.VMEM(a.shape, F32) for a in lows]
        + [pltpu.VMEM((8, D), F32)]
        + [pltpu.VMEM(shape, F32) for shape in flat]
        + [pltpu.SemaphoreType.DMA((33,)), pltpu.SemaphoreType.DMA((37,))],
        compiler_params=pltpu.CompilerParams(vmem_limit_bytes=60 * 1024 * 1024),
        name="widen",
    )(*lows, small)


def local(
    tokens,
    cotangent,
    doc_lengths,
    live_mask,
    norm_gains,
    norm_biases,
    query_key_value,
    query_value_bias,
    output_weight,
    output_biases,
    expand_weight,
    expand_bias,
    reduce_weight,
):
    reduce_dp = lax.axis_size("dp") == 16
    act, dx, gdn, gup, go, gqkv, small = call(
        reduce_dp,
        tokens.reshape(USED, D),
        cotangent.reshape(USED, D),
        doc_lengths,
        live_mask,
        norm_gains[0],
        norm_biases[0],
        query_key_value[0].transpose(1, 0, 2),
        query_value_bias[0],
        output_weight[0],
        output_biases[0],
        expand_weight[0],
        expand_bias,
        reduce_weight[0],
    )
    act, dx, gdn, gup, go, gqkv, gains, shifts, qv, biases, upb = widen(
        (act, dx, gdn, gup, go, gqkv), small
    )
    return (
        act.reshape(1, SLOTS, ROWS, D),
        dx.reshape(1, SLOTS, ROWS, D),
        gains[None],
        shifts[None],
        gqkv.reshape(3, D, W).transpose(1, 0, 2)[None],
        qv[None],
        go[None],
        biases[None],
        gup[None],
        upb,
        gdn[None],
    )


def solution(mesh):
    in_specs = (
        P(None, "dp", None),
        P(None, "dp", None),
        P(None, "dp", None),
        P(None, "dp"),
        P("pipe", None, None),
        P("pipe", None, None),
        P("pipe", None, None, "tensor"),
        P("pipe", None, "tensor"),
        P("pipe", "tensor", None),
        P("pipe", None, None),
        P("pipe", None, "tensor"),
        P("pipe", "tensor"),
        P("pipe", "tensor", None),
    )
    out_specs = (
        P("pipe", None, "dp", None),
        P("pipe", None, "dp", None),
        P("pipe", None, None),
        P("pipe", None, None),
        P("pipe", None, None, "tensor"),
        P("pipe", None, "tensor"),
        P("pipe", "tensor", None),
        P("pipe", None, None),
        P("pipe", None, "tensor"),
        P("pipe", "tensor"),
        P("pipe", "tensor", None),
    )
    return jax.shard_map(local, mesh=mesh, in_specs=in_specs, out_specs=out_specs, check_vma=False)
```
